32 devices in a mesh: grp: 4 (over x, core), dev: 8 (over z, y).
Axes of the slice: x: 2, y: 2, z: 4, core: 2. Of those that a mesh axis runs over, the one named last changes fastest.
Arguments:
- density: float32 [2, 8192, 8192], P(None, 'dev', 'grp'), may hold values from -64 to 64, as said below
- costate: float32 [2, 8192, 8192], P(None, 'dev', 'grp'), may hold values from -64 to 64, as said below
- phases: float32 [24, 2, 64], replicated, may hold values from -3.140625 to 3.140625
- displacements: float32 [24, 2, 2, 64, 64], replicated, may hold values from -0.5 to 0.5
- table_slot: int32 [24], replicated, may hold values from 0 to 23, each once
- checkpoint: int32 [1], replicated, may hold values from 0 to 22
Outputs:
- costate_start: float32 [2, 8192, 8192], P(None, 'dev', 'grp')
- phase_grads: float32 [2, 2, 64], replicated
The draws below stay inside these ranges and needn't reach their ends.
Inputs may be any that keep to these rules, and one draw needn't show every extreme that they name: `density`: Hermitian: real part symmetric, imaginary part antisymmetric. `costate`: Hermitian: real part symmetric, imaginary part antisymmetric. `table_slot`: every row of phases once.
All inputs are finite; a program needn't handle non-finite values.
Results may differ from the reference program's by a relative error of at most 0.00011.
Values sent between devices are 32-bit elements; how exact they have to be, the bound alone decides.
No kernel may reach another device: no remote copies, remote signals or barrier semaphores. Data moves between devices by JAX's collectives and lax.ppermute only.
A program may use at most 384 MiB of HBM per device.

```python
import jax
import jax.numpy as jnp
from jax import lax

LEVELS = 64
TRANSMON = 2
TABLES = 24
WINDOW = 2
NN = 8192


def hermitian_pair(key):
    first_key, second_key = jax.random.split(key, 2)
    real_part = jax.random.normal(first_key, (NN, NN), jnp.float32)
    imag_part = jax.random.normal(second_key, (NN, NN), jnp.float32)
    real_part = (real_part + real_part.T) * 0.7071
    imag_part = (imag_part - imag_part.T) * 0.7071
    return jnp.stack([real_part, imag_part])


def draw_density(key, part):
    key = jax.random.fold_in(key, 11)
    pair = hermitian_pair(key)
    return pair


def draw_costate(key, part):
    key = jax.random.fold_in(key, 23)
    pair = hermitian_pair(key)
    return pair


def centred(key, extent, deviation, bound, held_as=jnp.bfloat16):
    array = jax.random.normal(key, extent, jnp.float32) * deviation
    return jnp.minimum(jnp.maximum(array, -bound), bound).astype(held_as)


def setup_inputs(seed: int = 0) -> dict:
    key_list = jax.random.split(jax.random.key(seed), 7)
    return {
        "density": draw_density(jax.random.fold_in(key_list[6], 71), 0),
        "costate": draw_costate(jax.random.fold_in(key_list[6], 71), 0),
        "phases": jnp.clip(jax.random.uniform(key_list[2], (TABLES, 2, LEVELS), jnp.float32, -3.140625, 3.140625), -3.140625, 3.140625),
        "displacements": centred(key_list[3], (TABLES, 2, 2, LEVELS, LEVELS), (2 * LEVELS) ** -0.5, 0.5, jnp.float32),
        "table_slot": jax.random.permutation(key_list[4], TABLES).astype(jnp.int32),
        "checkpoint": jax.random.randint(key_list[5], (1,), 0, TABLES - 1).astype(jnp.int32),
    }


HIGH = lax.Precision.HIGHEST


def quad(real_part, imag_part):
    return jnp.stack([jnp.stack([real_part, -imag_part]), jnp.stack([imag_part, real_part])])


def mode_apply(quads, field, dim):
    letters = "abcdef"
    source = "p" + letters[:dim - 1] + "m" + letters[dim:]
    target = "o" + letters[:dim - 1] + "n" + letters[dim:]
    return jnp.einsum("opnm," + source + "->" + target, quads, field, precision=HIGH)


def turn(field, rows_angle, cols_angle):
    angles = rows_angle[:, :, None, None, None, None] - cols_angle[None, None, None, :, :, None]
    cosine = jnp.cos(angles)
    sine = jnp.sin(angles)
    return jnp.stack([cosine * field[0] - sine * field[1], sine * field[0] + cosine * field[1]])


def both_sides(field, matrix, row_dim, forward):
    real_part = matrix[0]
    imag_part = matrix[1]
    if forward:
        left_side = quad(real_part, imag_part)
        right_side = quad(real_part, -imag_part)
    else:
        left_side = quad(real_part.T, -imag_part.T)
        right_side = quad(real_part.T, imag_part.T)
    return mode_apply(right_side, mode_apply(left_side, field, row_dim), row_dim + 3)


def grad_terms(snapped, pulled):
    return 2.0 * jnp.sum(snapped[0] * pulled[1] - snapped[1] * pulled[0], axis=(3, 4, 5))


def reference(density, costate, phases, displacements, table_slot, checkpoint):
    shaped = (2, LEVELS, LEVELS, TRANSMON, LEVELS, LEVELS, TRANSMON)
    state_zero = density.reshape(shaped)
    adjoint_two = costate.reshape(shaped)
    start = checkpoint[0]
    grids = []
    matrices = []
    for layer in range(WINDOW):
        slot = table_slot[start + layer]
        table = lax.dynamic_index_in_dim(phases, slot, 0, keepdims=False)
        grids.append(table[0][:, None] + table[1][None, :])
        matrices.append(lax.dynamic_index_in_dim(displacements, start + layer, 0, keepdims=False))
    snapped_zero = turn(state_zero, grids[0], grids[0])
    state_one = both_sides(both_sides(snapped_zero, matrices[0][1], 2, True), matrices[0][0], 1, True)
    snapped_one = turn(state_one, grids[1], grids[1])
    pulled_one = both_sides(both_sides(adjoint_two, matrices[1][1], 2, False), matrices[1][0], 1, False)
    adjoint_one = turn(pulled_one, -grids[1], -grids[1])
    pulled_zero = both_sides(both_sides(adjoint_one, matrices[0][0], 1, False), matrices[0][1], 2, False)
    adjoint_zero = turn(pulled_zero, -grids[0], -grids[0])
    stacked = []
    for terms in (grad_terms(snapped_zero, pulled_zero), grad_terms(snapped_one, pulled_one)):
        stacked.append(jnp.stack([jnp.sum(terms, axis=(1, 2)), jnp.sum(terms, axis=(0, 2))]))
    return adjoint_zero.reshape(2, NN, NN), jnp.stack(stacked)
```

```python
import functools

import jax
import jax.numpy as jnp
from jax import lax
from jax.experimental import pallas as pl
from jax.experimental.pallas import tpu as pltpu
from jax.sharding import PartitionSpec as P

LEVELS = 64
TRANSMON = 2
WIDE = LEVELS * TRANSMON
PAIR = 2 * WIDE
HIGH = lax.Precision.HIGHEST
F32 = jnp.float32
BF16 = jnp.bfloat16
PARAMS = pltpu.CompilerParams(vmem_limit_bytes=48 * 1024 * 1024)


def split_value(value):
    high = value.astype(BF16)
    low = (value - high.astype(F32)).astype(BF16)
    return high, low


def mxu(left, right, dims=(((1,), (0,)), ((), ()))):
    return lax.dot_general(left, right, dims, preferred_element_type=F32)


def split_matrix(matrix):
    high = lax.reduce_precision(matrix, exponent_bits=8, mantissa_bits=7)
    return high.astype(BF16), (matrix - high).astype(BF16)


def lane_matrix(real_part, imag_part):
    eye = jnp.eye(TRANSMON, dtype=F32)
    real_part = jnp.kron(real_part, eye)
    imag_part = jnp.kron(imag_part, eye)
    return jnp.concatenate(
        [
            jnp.concatenate([real_part, imag_part], axis=1),
            jnp.concatenate([-imag_part, real_part], axis=1),
        ],
        axis=0,
    )


def lane_weights(real_part, imag_part):
    return jnp.stack(split_matrix(lane_matrix(real_part, imag_part)))


def level_weights(real_part, imag_part):
    full = jnp.concatenate(
        [
            jnp.concatenate([real_part.T, -imag_part.T], axis=1),
            jnp.concatenate([imag_part.T, real_part.T], axis=1),
        ],
        axis=0,
    )
    high, low = split_matrix(full)
    return jnp.concatenate(
        [
            jnp.concatenate([high, high], axis=1),
            jnp.concatenate([low, jnp.zeros_like(low)], axis=1),
        ],
        axis=0,
    )


def open_kernel(parts, chunks, fold, seat_ref, weight_ref, field_ref, *out_refs):
    seat = seat_ref[0]
    rows = field_ref.shape[1]
    firsts = rows // WIDE
    share = WIDE // parts
    size = share // chunks
    if fold:
        both = jnp.concatenate([field_ref[0], field_ref[1]], axis=1)
        high, low = split_value(both)
        across = (((1,), (1,)), ((), ()))
        made = mxu(weight_ref[0], high, across) + (
            mxu(weight_ref[0], low, across) + mxu(weight_ref[1], high, across)
        )
        for step in range(parts):
            part = lax.bitwise_xor(seat, step)
            del part
        scratch = out_refs[-1]
        scratch[...] = made.reshape(2, parts, share, rows)
        for step in range(parts):
            part = lax.bitwise_xor(seat, step)
            for chunk in range(chunks):
                out = out_refs[chunk * parts + step]
                for half in range(2):
                    piece = scratch[half, part, chunk * size:(chunk + 1) * size, :]
                    for first in range(firsts):
                        out[first, half * size:(half + 1) * size, :] = piece[
                            :, first * WIDE:(first + 1) * WIDE
                        ]
    else:
        for step in range(parts):
            part = lax.bitwise_xor(seat, step)
            for chunk in range(chunks):
                out = out_refs[chunk * parts + step]
                for half in range(2):
                    for first in range(firsts):
                        start = pl.multiple_of(
                            first * WIDE + part * share + chunk * size, size
                        )
                        out[first, half * size:(half + 1) * size, :] = field_ref[
                            half, pl.ds(start, size), :
                        ]


def open_pieces(field, seat, weights, parts, chunks, fold):
    rows, cols = field.shape[1:]
    firsts = rows // WIDE
    column_levels = cols // WIDE
    size = WIDE // parts // chunks
    count = parts * chunks
    shape = jax.ShapeDtypeStruct((firsts, column_levels * 2 * size, WIDE), F32)
    scratch = [pltpu.VMEM((2, parts, WIDE // parts, rows), F32)] if fold else []
    outs = pl.pallas_call(
        functools.partial(open_kernel, parts, chunks, fold),
        grid=(column_levels,),
        in_specs=[
            pl.BlockSpec(memory_space=pltpu.SMEM),
            pl.BlockSpec((2, PAIR, PAIR), lambda i: (0, 0, 0)),
            pl.BlockSpec((2, rows, WIDE), lambda i: (0, 0, i)),
        ],
        out_specs=[pl.BlockSpec((firsts, 2 * size, WIDE), lambda i: (0, i, 0))] * count,
        out_shape=[shape] * count,
        scratch_shapes=scratch,
        compiler_params=PARAMS,
        cost_estimate=pl.CostEstimate(
            flops=(6 * rows * column_levels * PAIR * PAIR) if fold else 0,
            bytes_accessed=16 * rows * cols,
            transcendentals=0,
        ),
    )(seat, weights, field)
    return [outs[c * parts:(c + 1) * parts] for c in range(chunks)]


def level_apply(weights, real_part, imag_part):
    real_high, real_low = split_value(real_part)
    imag_high, imag_low = split_value(imag_part)
    stacked = jnp.concatenate([real_high, imag_high, real_low, imag_low], axis=0)
    made = mxu(weights, stacked)
    return made[:WIDE] + made[WIDE:]


def lane_apply(weight_ref, index, real_part, imag_part):
    high, low = split_value(jnp.concatenate([real_part, imag_part], axis=1))
    made = mxu(high, weight_ref[index, 0]) + (
        mxu(low, weight_ref[index, 0]) + mxu(high, weight_ref[index, 1])
    )
    return made[:, :WIDE], made[:, WIDE:]


def gather_levels(refs, size, half):
    columns = []
    for place in range(size):
        parts = [
            ref[pl.ds(half * size + place, ref.shape[0] // (2 * size), stride=2 * size), :]
            for ref in refs
        ]
        columns.append(jnp.concatenate(parts, axis=0) if len(parts) > 1 else parts[0])
    return jnp.concatenate(columns, axis=1)


def scatter_levels(ref, size, half, value):
    for place in range(size):
        ref[pl.ds(half * size + place, LEVELS, stride=2 * size), :] = value[
            :, place * WIDE:(place + 1) * WIDE
        ]


def turn_kernel(parts, size, weight_ref, *refs):
    pieces = refs[:parts]
    out_ref = refs[parts].reshape(LEVELS * 2 * size, WIDE)
    made = level_apply(
        weight_ref[...], gather_levels(pieces, size, 0), gather_levels(pieces, size, 1)
    )
    scatter_levels(out_ref, size, 0, made[:LEVELS])
    scatter_levels(out_ref, size, 1, made[LEVELS:])


def turn_columns(pieces, weights, size):
    firsts = pieces[0].shape[0]
    parts = len(pieces)
    block = pieces[0].shape[1:]
    return pl.pallas_call(
        functools.partial(turn_kernel, parts, size),
        grid=(firsts,),
        in_specs=[pl.BlockSpec((PAIR, PAIR), lambda i: (0, 0))]
        + [pl.BlockSpec((None,) + block, lambda i: (i, 0, 0))] * parts,
        out_specs=pl.BlockSpec((LEVELS, None, 2 * size, WIDE), lambda i: (0, i, 0, 0)),
        out_shape=jax.ShapeDtypeStruct((LEVELS, firsts, 2 * size, WIDE), F32),
        compiler_params=PARAMS,
        cost_estimate=pl.CostEstimate(
            flops=2 * PAIR * PAIR * firsts * size * WIDE,
            bytes_accessed=16 * LEVELS * firsts * size * WIDE,
            transcendentals=0,
        ),
    )(weights, *pieces)


def halves(value, size):
    value = value.reshape(LEVELS, 2, size, WIDE)
    rows = LEVELS * size
    return value[:, 0].reshape(rows, WIDE), value[:, 1].reshape(rows, WIDE)


def join(real_part, imag_part, size):
    shape = (LEVELS, 1, size, WIDE)
    both = jnp.concatenate([real_part.reshape(shape), imag_part.reshape(shape)], axis=1)
    return both.reshape(LEVELS * 2 * size, WIDE)


def close_kernel(parts, size, lane_ref, level_ref, field_ref, *refs):
    rho_refs = refs[:parts]
    out_refs = refs[parts:2 * parts]
    grad_ref, work_a, work_b = refs[2 * parts:]
    step = pl.program_id(0)

    @pl.when(step == 0)
    def _():
        grad_ref[...] = jnp.zeros_like(grad_ref)

    flat = field_ref.reshape(LEVELS * 2 * size, WIDE)
    real_part, imag_part = lane_apply(lane_ref, 0, *halves(flat[...], size))
    work_a[...] = join(real_part, imag_part, size)

    rho = jnp.concatenate([ref[...] for ref in rho_refs], axis=0)
    rho_real, rho_imag = halves(rho, size)
    real_part, imag_part = lane_apply(lane_ref, 1, rho_real, rho_imag)
    work_b[...] = join(real_part, imag_part, size)

    mid = level_apply(level_ref[0], gather_levels([work_a], size, 0), gather_levels([work_a], size, 1))
    seen = level_apply(level_ref[1], gather_levels([work_b], size, 0), gather_levels([work_b], size, 1))
    terms = seen[:LEVELS] * mid[LEVELS:] - seen[LEVELS:] * mid[:LEVELS]
    total = terms[:, :WIDE]
    for place in range(1, size):
        total = total + terms[:, place * WIDE:(place + 1) * WIDE]
    grad_ref[1] += total

    last = level_apply(level_ref[2], mid[:LEVELS], mid[LEVELS:])
    scatter_levels(work_a, size, 0, last[:LEVELS])
    scatter_levels(work_a, size, 1, last[LEVELS:])
    real_part, imag_part = lane_apply(lane_ref, 2, *halves(work_a[...], size))
    terms = rho_real * imag_part - rho_imag * real_part
    grad_ref[0] += jnp.sum(terms.reshape(LEVELS, size, WIDE), axis=1)
    made = join(real_part, imag_part, size)
    rows = made.shape[0] // parts
    for part in range(parts):
        out_refs[part][...] = made[part * rows:(part + 1) * rows]


def close_columns(field, rho_pieces, lane, level, size):
    total_first, firsts = field.shape[:2]
    devs = total_first // firsts
    parts = len(rho_pieces)
    rows = LEVELS * 2 * size
    field = field.reshape(devs, firsts, firsts * 2 * size, WIDE)
    piece = rho_pieces[0]
    piece_spec = pl.BlockSpec((None,) + piece.shape[1:], lambda i: (i, 0, 0))
    outs = pl.pallas_call(
        functools.partial(close_kernel, parts, size),
        grid=(firsts,),
        in_specs=[
            pl.BlockSpec(lane.shape, lambda i: (0, 0, 0, 0)),
            pl.BlockSpec(level.shape, lambda i: (0, 0, 0)),
            pl.BlockSpec((devs, None, firsts * 2 * size, WIDE), lambda i: (0, i, 0, 0)),
        ]
        + [piece_spec] * parts,
        out_specs=[piece_spec] * parts + [pl.BlockSpec((2, LEVELS, WIDE), lambda i: (0, 0, 0))],
        out_shape=[jax.ShapeDtypeStruct(piece.shape, F32)] * parts
        + [jax.ShapeDtypeStruct((2, LEVELS, WIDE), F32)],
        scratch_shapes=[pltpu.VMEM((rows, WIDE), F32), pltpu.VMEM((rows, WIDE), F32)],
        compiler_params=PARAMS,
        cost_estimate=pl.CostEstimate(
            flops=firsts * (3 * 3 * PAIR * PAIR * rows + 3 * 2 * PAIR * PAIR * size * WIDE),
            bytes_accessed=12 * firsts * rows * WIDE,
            transcendentals=0,
        ),
    )(lane, level, field, *rho_pieces)
    return outs[:parts], outs[parts]


def place_kernel(parts, size, aliased, seat_ref, *refs):
    pieces = refs[:parts]
    out_ref = refs[parts + aliased]
    seat = seat_ref[0]
    levels = pieces[0].shape[0] // (2 * size)
    for step in range(parts):
        part = lax.bitwise_xor(seat, step)
        for half in range(2):
            for level in range(levels):
                start = level * 2 * size + half * size
                out_ref[half, part, :, level * WIDE:(level + 1) * WIDE] = pieces[step][
                    start:start + size, :
                ]


def place_pieces(pieces, seat, held, chunk, shape, size):
    parts = len(pieces)
    firsts, chunks = shape[1], shape[3]
    aliased = 0 if held is None else 1
    piece = pieces[0]
    cols = shape[-1]
    return pl.pallas_call(
        functools.partial(place_kernel, parts, size, aliased),
        grid=(firsts,),
        in_specs=[pl.BlockSpec(memory_space=pltpu.SMEM)]
        + [pl.BlockSpec((None,) + piece.shape[1:], lambda i: (i, 0, 0))] * parts
        + [pl.BlockSpec(memory_space=pl.ANY)] * aliased,
        out_specs=pl.BlockSpec(
            (2, None, parts, None, size, cols), lambda i: (0, i, 0, chunk, 0, 0)
        ),
        out_shape=jax.ShapeDtypeStruct(shape, F32),
        input_output_aliases={parts + 1: 0} if aliased else {},
        compiler_params=PARAMS,
        cost_estimate=pl.CostEstimate(
            flops=0, bytes_accessed=8 * 2 * firsts * parts * size * cols, transcendentals=0
        ),
    )(seat, *pieces, *([held] if aliased else []))


def swap(pieces, parts):
    moved = [pieces[0]]
    for step in range(1, parts):
        pairs = [(member, member ^ step) for member in range(parts)]
        moved.append(lax.ppermute(pieces[step], "grp", pairs))
    return moved


def per_device(density, costate, phases, displacements, table_slot, checkpoint):
    parts = lax.axis_size("grp")
    share = WIDE // parts
    chunks = max(1, min(4, share // 8))
    size = share // chunks
    seat = lax.axis_index("grp").astype(jnp.int32)
    seats = seat.reshape(1)
    rows, cols = costate.shape[1:]

    start = checkpoint[0]
    slots = lax.dynamic_slice_in_dim(table_slot, start, 2)
    angles = jnp.take(phases, slots, axis=0)
    given = lax.dynamic_slice_in_dim(displacements, start, 2)
    cosine = jnp.cos(angles)[:, :, None, :]
    sine = jnp.sin(angles)[:, :, None, :]
    real_part = given[:, :, 0] * cosine - given[:, :, 1] * sine
    imag_part = given[:, :, 0] * sine + given[:, :, 1] * cosine
    later = jnp.concatenate(
        [
            jnp.concatenate([real_part[1], -imag_part[1]], axis=2),
            jnp.concatenate([imag_part[1], real_part[1]], axis=2),
        ],
        axis=1,
    )
    product = jnp.einsum(
        "mij,mjk->mik", later, jnp.concatenate([real_part[0], imag_part[0]], axis=1), precision=HIGH
    )
    both_real = product[:, :LEVELS]
    both_imag = product[:, LEVELS:]
    flip = jnp.concatenate([jnp.ones((WIDE, 1), F32), -jnp.ones((WIDE, 1), F32)], axis=0)
    open_weights = jnp.stack(split_matrix(flip * lane_matrix(both_real[1], both_imag[1]).T))

    state = open_pieces(costate, seats, open_weights, parts, chunks, True)
    rho = open_pieces(density, seats, open_weights, parts, chunks, False)

    order = lax.bitwise_xor(seat, jnp.arange(parts, dtype=jnp.int32))
    width = LEVELS // parts
    order = (order[:, None] * width + jnp.arange(width, dtype=jnp.int32)[None, :]).reshape(LEVELS)
    turn_weights = level_weights(
        jnp.take(both_real[0], order, axis=0), -jnp.take(both_imag[0], order, axis=0)
    )
    first_real, first_imag = real_part[0, 0], imag_part[0, 0]
    level = jnp.stack(
        [
            level_weights(real_part[1, 0], imag_part[1, 0]),
            level_weights(
                jnp.take(first_real.T, order, axis=0), -jnp.take(first_imag.T, order, axis=0)
            ),
            level_weights(
                jnp.take(first_real, order, axis=1), jnp.take(first_imag, order, axis=1)
            ),
        ]
    )
    lane = jnp.stack(
        [
            lane_weights(real_part[1, 1], imag_part[1, 1]),
            lane_weights(real_part[0, 1].T, -imag_part[0, 1].T),
            lane_weights(real_part[0, 1], imag_part[0, 1]),
        ]
    )

    grads = []
    whole = None
    shape = (2, rows // WIDE, parts, chunks, size, cols)
    for chunk in range(chunks):
        turned = turn_columns(swap(state[chunk], parts), turn_weights, size)
        turned = lax.all_to_all(turned, "dev", split_axis=0, concat_axis=0, tiled=True)
        made, grad = close_columns(turned, swap(rho[chunk], parts), lane, level, size)
        grads.append(grad)
        whole = place_pieces(swap(made, parts), seats, whole, chunk, shape, size)

    grad = -2.0 * sum(grads)
    lane_sum = jnp.sum(grad, axis=2)
    lane_sum = jnp.stack([jnp.take(lane_sum[0], order), lane_sum[1]])
    level_sum = jnp.sum(jnp.sum(grad, axis=1).reshape(2, LEVELS, TRANSMON), axis=2)
    gradients = lax.psum(jnp.stack([lane_sum, level_sum], axis=1), ("grp", "dev"))
    return whole.reshape(costate.shape), gradients


def solution(mesh):
    return jax.shard_map(
        per_device,
        mesh=mesh,
        in_specs=(P(None, "dev", "grp"), P(None, "dev", "grp"), P(), P(), P(), P()),
        out_specs=(P(None, "dev", "grp"), P()),
        check_vma=False,
    )
```

```python
import functools

import jax
import jax.numpy as jnp
from jax import lax
from jax.experimental import pallas as pl
from jax.experimental.pallas import tpu as pltpu
from jax.sharding import PartitionSpec as P

LEVELS = 64
TRANSMON = 2
WIDE = LEVELS * TRANSMON
PAIR = 2 * WIDE
HIGH = lax.Precision.HIGHEST
F32 = jnp.float32
BF16 = jnp.bfloat16
PARAMS = pltpu.CompilerParams(vmem_limit_bytes=48 * 1024 * 1024)


def split_value(value):
    high = value.astype(BF16)
    low = (value - high.astype(F32)).astype(BF16)
    return high, low


def mxu(left, right, dims=(((1,), (0,)), ((), ()))):
    return lax.dot_general(left, right, dims, preferred_element_type=F32)


def exact(left, right, dims=(((1,), (0,)), ((), ()))):
    return lax.dot_general(left, right, dims, precision=HIGH, preferred_element_type=F32)


def grid_of(shape, dim):
    return lax.broadcasted_iota(jnp.int32, shape, dim)


def pick_matrix(count, chosen):
    shape = (count, count)
    return (chosen(grid_of(shape, 0)) == grid_of(shape, 1)).astype(F32)


def spread(matrix):
    tall = (grid_of((WIDE, LEVELS), 0) // TRANSMON == grid_of((WIDE, LEVELS), 1)).astype(F32)
    long = (grid_of((LEVELS, WIDE), 1) // TRANSMON == grid_of((LEVELS, WIDE), 0)).astype(F32)
    same = grid_of((WIDE, WIDE), 0) % TRANSMON == grid_of((WIDE, WIDE), 1) % TRANSMON
    return jnp.where(same, exact(exact(tall, matrix), long), 0.0)


def blocks(upper_left, upper_right, lower_left, lower_right):
    return jnp.concatenate(
        [
            jnp.concatenate([upper_left, upper_right], axis=1),
            jnp.concatenate([lower_left, lower_right], axis=1),
        ],
        axis=0,
    )


def complex_product(left, right):
    return (
        exact(left[0], right[0]) - exact(left[1], right[1]),
        exact(left[0], right[1]) + exact(left[1], right[0]),
    )


def weights_kernel(parts, chunks, slot_ref, start_ref, seat_ref, *refs):
    angle_refs, matrix_refs = refs[0:2], refs[2:4]
    open_ref, turn_ref, level_ref, lane_ref = refs[-4:]
    seat = seat_ref[0]
    width = LEVELS // parts
    share = WIDE // parts
    size = share // chunks
    first, second = [], []
    for layer in range(2):
        cosine = jnp.cos(angle_refs[layer][...])
        sine = jnp.sin(angle_refs[layer][...])
        for mode, kept in enumerate((first, second)):
            turn_real, turn_imag = cosine[mode:mode + 1], sine[mode:mode + 1]
            real_part = matrix_refs[layer][mode, 0]
            imag_part = matrix_refs[layer][mode, 1]
            kept.append(
                (
                    real_part * turn_real - imag_part * turn_imag,
                    real_part * turn_imag + imag_part * turn_real,
                )
            )
    both_first = complex_product(first[1], first[0])
    both_second = complex_product(second[1], second[0])

    order = pick_matrix(
        LEVELS, lambda row: lax.bitwise_xor(row // width, seat) * width + row % width
    )

    def put_level(ref, index, real_part, imag_part):
        full = blocks(real_part, -imag_part, imag_part, real_part)
        high, low = split_value(full)
        made = blocks(high, high, low, jnp.zeros_like(low))
        if index is None:
            ref[...] = made
        else:
            ref[index] = made

    put_level(turn_ref, None, exact(both_first[0].T, order), exact(-both_first[1].T, order))
    put_level(level_ref, 0, first[1][0].T, first[1][1].T)
    put_level(level_ref, 1, exact(first[0][0], order), exact(-first[0][1], order))
    put_level(level_ref, 2, exact(order, first[0][0].T), exact(order, first[0][1].T))

    def put_lane(index, real_part, imag_part):
        real_part, imag_part = spread(real_part), spread(imag_part)
        high, low = split_value(blocks(real_part, imag_part, -imag_part, real_part))
        lane_ref[index, 0] = high
        lane_ref[index, 1] = low

    put_lane(0, *second[1])
    put_lane(1, second[0][0].T, -second[0][1].T)
    put_lane(2, *second[0])

    real_part, imag_part = spread(both_second[0].T), spread(both_second[1].T)
    full = blocks(real_part, -imag_part, -imag_part, -real_part)

    def source(row):
        chunk, rest = row // (2 * size * parts), row % (2 * size * parts)
        step, rest = rest // (2 * size), rest % (2 * size)
        half, place = rest // size, rest % size
        return half * WIDE + lax.bitwise_xor(step, seat) * share + chunk * size + place

    high, low = split_value(exact(pick_matrix(PAIR, source), full))
    open_ref[0] = high
    open_ref[1] = low


def make_weights(phases, displacements, table_slot, checkpoint, seat, parts, chunks, waited):
    def angles(layer):
        return pl.BlockSpec(
            (None, 2, LEVELS), lambda i, slot, start, own: (slot[start[0] + layer], 0, 0)
        )

    def matrices(layer):
        return pl.BlockSpec(
            (None, 2, 2, LEVELS, LEVELS),
            lambda i, slot, start, own: (start[0] + layer, 0, 0, 0, 0),
        )

    def whole(shape):
        return pl.BlockSpec(shape, lambda i, slot, start, own: (0,) * len(shape))

    shapes = [(2, PAIR, PAIR), (PAIR, PAIR), (3, PAIR, PAIR), (3, 2, PAIR, PAIR)]
    return pl.pallas_call(
        functools.partial(weights_kernel, parts, chunks),
        grid_spec=pltpu.PrefetchScalarGridSpec(
            num_scalar_prefetch=3,
            grid=(1,),
            in_specs=[angles(0), angles(1), matrices(0), matrices(1)]
            + [pl.BlockSpec(memory_space=pl.ANY)] * len(waited),
            out_specs=[whole(shape) for shape in shapes],
        ),
        out_shape=[jax.ShapeDtypeStruct(shape, BF16) for shape in shapes],
        compiler_params=PARAMS,
        cost_estimate=pl.CostEstimate(flops=10**9, bytes_accessed=10**6, transcendentals=0),
    )(table_slot, checkpoint, seat, phases, phases, displacements, displacements, *waited)


def open_kernel(count, weight_ref, field_ref, *out_refs):
    both = jnp.concatenate([field_ref[0], field_ref[1]], axis=1)
    high, low = split_value(both)
    across = (((1,), (1,)), ((), ()))
    made = mxu(weight_ref[0], high, across) + (
        mxu(weight_ref[0], low, across) + mxu(weight_ref[1], high, across)
    )
    tall = made.shape[0] // count
    for place, out in enumerate(out_refs):
        piece = made[place * tall:(place + 1) * tall]
        for first in range(out.shape[0]):
            out[first] = piece[:, first * WIDE:(first + 1) * WIDE]


def open_state(field, weights, parts, size, chunk_start, chunk_count):
    rows, cols = field.shape[1:]
    firsts = rows // WIDE
    column_levels = cols // WIDE
    count = parts * chunk_count
    tall = count * 2 * size
    shape = jax.ShapeDtypeStruct((firsts, column_levels * 2 * size, WIDE), F32)
    weights = lax.slice_in_dim(
        weights, chunk_start * parts * 2 * size, chunk_start * parts * 2 * size + tall, axis=1
    )
    outs = pl.pallas_call(
        functools.partial(open_kernel, count),
        grid=(column_levels,),
        in_specs=[
            pl.BlockSpec((2, tall, PAIR), lambda i: (0, 0, 0)),
            pl.BlockSpec((2, rows, WIDE), lambda i: (0, 0, i)),
        ],
        out_specs=[pl.BlockSpec((firsts, 2 * size, WIDE), lambda i: (0, i, 0))] * count,
        out_shape=[shape] * count,
        compiler_params=PARAMS,
        cost_estimate=pl.CostEstimate(
            flops=6 * rows * column_levels * tall * PAIR,
            bytes_accessed=8 * rows * cols,
            transcendentals=0,
        ),
    )(weights, field)
    return [outs[c * parts:(c + 1) * parts] for c in range(chunk_count)]


def cut_kernel(size, seat_ref, field_ref, *out_refs):
    seat = seat_ref[0]
    levels = field_ref.shape[-1] // WIDE
    for step, out in enumerate(out_refs):
        part = lax.bitwise_xor(seat, step)
        for half in range(2):
            for level in range(levels):
                start = (2 * level + half) * size
                out[start:start + size, :] = field_ref[
                    half, part, :, level * WIDE:(level + 1) * WIDE
                ]


def cut_pieces(field, seat, parts, chunk, size):
    rows, cols = field.shape[1:]
    firsts = rows // WIDE
    chunks = WIDE // parts // size
    tall = cols // WIDE * 2 * size
    return pl.pallas_call(
        functools.partial(cut_kernel, size),
        grid=(firsts,),
        in_specs=[
            pl.BlockSpec(memory_space=pltpu.SMEM),
            pl.BlockSpec((2, None, parts, None, size, cols), lambda i: (0, i, 0, chunk, 0, 0)),
        ],
        out_specs=[pl.BlockSpec((None, tall, WIDE), lambda i: (i, 0, 0))] * parts,
        out_shape=[jax.ShapeDtypeStruct((firsts, tall, WIDE), F32)] * parts,
        compiler_params=PARAMS,
        cost_estimate=pl.CostEstimate(
            flops=0, bytes_accessed=16 * firsts * parts * size * cols, transcendentals=0
        ),
    )(seat, field.reshape(2, firsts, parts, chunks, size, cols))


def level_apply(weights, real_part, imag_part):
    real_high, real_low = split_value(real_part)
    imag_high, imag_low = split_value(imag_part)
    stacked = jnp.concatenate([real_high, imag_high, real_low, imag_low], axis=0)
    made = mxu(weights, stacked)
    return made[:WIDE] + made[WIDE:]


def lane_apply(weight_ref, index, real_part, imag_part):
    high, low = split_value(jnp.concatenate([real_part, imag_part], axis=1))
    made = mxu(high, weight_ref[index, 0]) + (
        mxu(low, weight_ref[index, 0]) + mxu(high, weight_ref[index, 1])
    )
    return made[:, :WIDE], made[:, WIDE:]


def gather_levels(refs, size, half):
    columns = []
    for place in range(size):
        parts = [
            ref[pl.ds(half * size + place, ref.shape[0] // (2 * size), stride=2 * size), :]
            for ref in refs
        ]
        columns.append(jnp.concatenate(parts, axis=0) if len(parts) > 1 else parts[0])
    return jnp.concatenate(columns, axis=1)


def scatter_levels(ref, size, half, value):
    for place in range(size):
        ref[pl.ds(half * size + place, LEVELS, stride=2 * size), :] = value[
            :, place * WIDE:(place + 1) * WIDE
        ]


def turn_kernel(parts, size, weight_ref, *refs):
    pieces = refs[:parts]
    out_ref = refs[-1].reshape(LEVELS * 2 * size, WIDE)
    made = level_apply(
        weight_ref[...], gather_levels(pieces, size, 0), gather_levels(pieces, size, 1)
    )
    scatter_levels(out_ref, size, 0, made[:LEVELS])
    scatter_levels(out_ref, size, 1, made[LEVELS:])


def turn_columns(pieces, weights, size, waited):
    firsts = pieces[0].shape[0]
    parts = len(pieces)
    block = pieces[0].shape[1:]
    return pl.pallas_call(
        functools.partial(turn_kernel, parts, size),
        grid=(firsts,),
        in_specs=[pl.BlockSpec((PAIR, PAIR), lambda i: (0, 0))]
        + [pl.BlockSpec((None,) + block, lambda i: (i, 0, 0))] * parts
        + [pl.BlockSpec(memory_space=pl.ANY)] * len(waited),
        out_specs=pl.BlockSpec((LEVELS, None, 2 * size, WIDE), lambda i: (0, i, 0, 0)),
        out_shape=jax.ShapeDtypeStruct((LEVELS, firsts, 2 * size, WIDE), F32),
        compiler_params=PARAMS,
        cost_estimate=pl.CostEstimate(
            flops=2 * PAIR * PAIR * firsts * size * WIDE,
            bytes_accessed=16 * LEVELS * firsts * size * WIDE,
            transcendentals=0,
        ),
    )(weights, *pieces, *waited)


def halves(value, size):
    value = value.reshape(LEVELS, 2, size, WIDE)
    rows = LEVELS * size
    return value[:, 0].reshape(rows, WIDE), value[:, 1].reshape(rows, WIDE)


def join(real_part, imag_part, size):
    shape = (LEVELS, 1, size, WIDE)
    both = jnp.concatenate([real_part.reshape(shape), imag_part.reshape(shape)], axis=1)
    return both.reshape(LEVELS * 2 * size, WIDE)


def close_kernel(parts, size, lane_ref, level_ref, field_ref, *refs):
    rho_refs = refs[:parts]
    out_refs = refs[parts:2 * parts]
    grad_ref, work_a, work_b = refs[2 * parts:]
    step = pl.program_id(0)

    @pl.when(step == 0)
    def _():
        grad_ref[...] = jnp.zeros_like(grad_ref)

    flat = field_ref.reshape(LEVELS * 2 * size, WIDE)
    real_part, imag_part = lane_apply(lane_ref, 0, *halves(flat[...], size))
    work_a[...] = join(real_part, imag_part, size)

    rho = jnp.concatenate([ref[...] for ref in rho_refs], axis=0)
    rho_real, rho_imag = halves(rho, size)
    real_part, imag_part = lane_apply(lane_ref, 1, rho_real, rho_imag)
    work_b[...] = join(real_part, imag_part, size)

    mid = level_apply(level_ref[0], gather_levels([work_a], size, 0), gather_levels([work_a], size, 1))
    seen = level_apply(level_ref[1], gather_levels([work_b], size, 0), gather_levels([work_b], size, 1))
    terms = seen[:LEVELS] * mid[LEVELS:] - seen[LEVELS:] * mid[:LEVELS]
    total = terms[:, :WIDE]
    for place in range(1, size):
        total = total + terms[:, place * WIDE:(place + 1) * WIDE]
    grad_ref[1] += total

    last = level_apply(level_ref[2], mid[:LEVELS], mid[LEVELS:])
    scatter_levels(work_a, size, 0, last[:LEVELS])
    scatter_levels(work_a, size, 1, last[LEVELS:])
    real_part, imag_part = lane_apply(lane_ref, 2, *halves(work_a[...], size))
    terms = rho_real * imag_part - rho_imag * real_part
    grad_ref[0] += jnp.sum(terms.reshape(LEVELS, size, WIDE), axis=1)
    made = join(real_part, imag_part, size)
    rows = made.shape[0] // parts
    for part in range(parts):
        out_refs[part][...] = made[part * rows:(part + 1) * rows]


def close_columns(field, rho_pieces, lane, level, size):
    total_first, firsts = field.shape[:2]
    devs = total_first // firsts
    parts = len(rho_pieces)
    rows = LEVELS * 2 * size
    field = field.reshape(devs, firsts, firsts * 2 * size, WIDE)
    piece = rho_pieces[0]
    piece_spec = pl.BlockSpec((None,) + piece.shape[1:], lambda i: (i, 0, 0))
    outs = pl.pallas_call(
        functools.partial(close_kernel, parts, size),
        grid=(firsts,),
        in_specs=[
            pl.BlockSpec(lane.shape, lambda i: (0, 0, 0, 0)),
            pl.BlockSpec(level.shape, lambda i: (0, 0, 0)),
            pl.BlockSpec((devs, None, firsts * 2 * size, WIDE), lambda i: (0, i, 0, 0)),
        ]
        + [piece_spec] * parts,
        out_specs=[piece_spec] * parts + [pl.BlockSpec((2, LEVELS, WIDE), lambda i: (0, 0, 0))],
        out_shape=[jax.ShapeDtypeStruct(piece.shape, F32)] * parts
        + [jax.ShapeDtypeStruct((2, LEVELS, WIDE), F32)],
        scratch_shapes=[pltpu.VMEM((rows, WIDE), F32), pltpu.VMEM((rows, WIDE), F32)],
        compiler_params=PARAMS,
        cost_estimate=pl.CostEstimate(
            flops=firsts * (3 * 3 * PAIR * PAIR * rows + 3 * 2 * PAIR * PAIR * size * WIDE),
            bytes_accessed=12 * firsts * rows * WIDE,
            transcendentals=0,
        ),
    )(lane, level, field, *rho_pieces)
    return outs[:parts], outs[parts]


def place_kernel(parts, size, aliased, seat_ref, *refs):
    pieces = refs[:parts]
    out_ref = refs[parts + aliased]
    seat = seat_ref[0]
    levels = pieces[0].shape[0] // (2 * size)
    for step in range(parts):
        part = lax.bitwise_xor(seat, step)
        for half in range(2):
            for level in range(levels):
                start = level * 2 * size + half * size
                out_ref[half, part, :, level * WIDE:(level + 1) * WIDE] = pieces[step][
                    start:start + size, :
                ]


def place_pieces(pieces, seat, held, chunk, shape, size):
    parts = len(pieces)
    firsts, chunks = shape[1], shape[3]
    aliased = 0 if held is None else 1
    piece = pieces[0]
    cols = shape[-1]
    return pl.pallas_call(
        functools.partial(place_kernel, parts, size, aliased),
        grid=(firsts,),
        in_specs=[pl.BlockSpec(memory_space=pltpu.SMEM)]
        + [pl.BlockSpec((None,) + piece.shape[1:], lambda i: (i, 0, 0))] * parts
        + [pl.BlockSpec(memory_space=pl.ANY)] * aliased,
        out_specs=pl.BlockSpec(
            (2, None, parts, None, size, cols), lambda i: (0, i, 0, chunk, 0, 0)
        ),
        out_shape=jax.ShapeDtypeStruct(shape, F32),
        input_output_aliases={parts + 1: 0} if aliased else {},
        compiler_params=PARAMS,
        cost_estimate=pl.CostEstimate(
            flops=0, bytes_accessed=8 * 2 * firsts * parts * size * cols, transcendentals=0
        ),
    )(seat, *pieces, *([held] if aliased else []))


def swap(pieces, parts):
    moved = [pieces[0]]
    for step in range(1, parts):
        pairs = [(member, member ^ step) for member in range(parts)]
        moved.append(lax.ppermute(pieces[step], "grp", pairs))
    return moved


def per_device(density, costate, phases, displacements, table_slot, checkpoint):
    parts = lax.axis_size("grp")
    share = WIDE // parts
    chunks = max(1, min(4, share // 8))
    size = share // chunks
    seat = lax.axis_index("grp").astype(jnp.int32)
    seats = seat.reshape(1)
    rows, cols = costate.shape[1:]

    rho = [cut_pieces(density, seats, parts, 0, size)]
    opened, turned_by, level, lane = make_weights(
        phases, displacements, table_slot, checkpoint, seats, parts, chunks, rho[0]
    )
    rho_there = [swap(rho[0], parts)]
    state = open_state(costate, opened, parts, size, 0, 1)
    if chunks > 1:
        state += open_state(costate, opened, parts, size, 1, chunks - 1)
    for chunk in range(1, chunks):
        rho_there.append(swap(cut_pieces(density, seats, parts, chunk, size), parts))

    shape = (2, rows // WIDE, parts, chunks, size, cols)
    grads, made = [], []
    fields = []
    for chunk in range(chunks):
        waited = rho_there[chunk]
        if chunk == chunks - 1 and chunks > 2:
            out, grad = close_columns(fields[0], rho_there[0], lane, level, size)
            made.append(swap(out, parts))
            grads.append(grad)
            waited = made[0]
        field = turn_columns(swap(state[chunk], parts), turned_by, size, waited[1:])
        fields.append(lax.all_to_all(field, "dev", split_axis=0, concat_axis=0, tiled=True))
    for chunk in range(len(made), chunks):
        out, grad = close_columns(fields[chunk], rho_there[chunk], lane, level, size)
        made.append(swap(out, parts))
        grads.append(grad)
    whole = None
    for chunk in range(chunks - 1):
        whole = place_pieces(made[chunk], seats, whole, chunk, shape, size)

    grad = sum(grads)
    if whole is not None:
        grad, whole = lax.optimization_barrier((grad, whole))
    lane_sum = -2.0 * jnp.sum(grad, axis=2)
    width = LEVELS // parts
    order = lax.bitwise_xor(seat, jnp.arange(parts, dtype=jnp.int32))
    order = (order[:, None] * width + jnp.arange(width, dtype=jnp.int32)[None, :]).reshape(LEVELS)
    lane_sum = jnp.stack([jnp.take(lane_sum[0], order), lane_sum[1]])
    level_sum = -2.0 * jnp.sum(jnp.sum(grad, axis=1).reshape(2, LEVELS, TRANSMON), axis=2)
    gradients = lax.psum(jnp.stack([lane_sum, level_sum], axis=1), ("grp", "dev"))
    whole = place_pieces(made[-1], seats, whole, chunks - 1, shape, size)
    return whole.reshape(costate.shape), gradients


def solution(mesh):
    return jax.shard_map(
        per_device,
        mesh=mesh,
        in_specs=(P(None, "dev", "grp"), P(None, "dev", "grp"), P(), P(), P(), P()),
        out_specs=(P(None, "dev", "grp"), P()),
        check_vma=False,
    )
```

```python
import functools

import jax
import jax.numpy as jnp
from jax import lax
from jax.experimental import pallas as pl
from jax.experimental.pallas import tpu as pltpu
from jax.sharding import PartitionSpec as P

LEVELS = 64
TRANSMON = 2
WIDE = LEVELS * TRANSMON
PAIR = 2 * WIDE
HIGH = lax.Precision.HIGHEST
F32 = jnp.float32
BF16 = jnp.bfloat16
PARAMS = pltpu.CompilerParams(vmem_limit_bytes=48 * 1024 * 1024)


def split_value(value):
    high = value.astype(BF16)
    low = (value - high.astype(F32)).astype(BF16)
    return high, low


def mxu(left, right, dims=(((1,), (0,)), ((), ()))):
    return lax.dot_general(left, right, dims, preferred_element_type=F32)


def exact(left, right, dims=(((1,), (0,)), ((), ()))):
    return lax.dot_general(left, right, dims, precision=HIGH, preferred_element_type=F32)


def grid_of(shape, dim):
    return lax.broadcasted_iota(jnp.int32, shape, dim)


def pick_matrix(count, chosen):
    shape = (count, count)
    return (chosen(grid_of(shape, 0)) == grid_of(shape, 1)).astype(F32)


def spread(matrix):
    tall = (grid_of((WIDE, LEVELS), 0) // TRANSMON == grid_of((WIDE, LEVELS), 1)).astype(F32)
    long = (grid_of((LEVELS, WIDE), 1) // TRANSMON == grid_of((LEVELS, WIDE), 0)).astype(F32)
    same = grid_of((WIDE, WIDE), 0) % TRANSMON == grid_of((WIDE, WIDE), 1) % TRANSMON
    return jnp.where(same, exact(exact(tall, matrix), long), 0.0)


def blocks(upper_left, upper_right, lower_left, lower_right):
    return jnp.concatenate(
        [
            jnp.concatenate([upper_left, upper_right], axis=1),
            jnp.concatenate([lower_left, lower_right], axis=1),
        ],
        axis=0,
    )


def complex_product(left, right):
    return (
        exact(left[0], right[0]) - exact(left[1], right[1]),
        exact(left[0], right[1]) + exact(left[1], right[0]),
    )


def weights_kernel(parts, chunks, slot_ref, start_ref, seat_ref, *refs):
    angle_refs, matrix_refs = refs[0:2], refs[2:4]
    open_ref, turn_ref, level_ref, lane_ref = refs[-4:]
    seat = seat_ref[0]
    width = LEVELS // parts
    share = WIDE // parts
    size = share // chunks
    first, second = [], []
    for layer in range(2):
        cosine = jnp.cos(angle_refs[layer][...])
        sine = jnp.sin(angle_refs[layer][...])
        for mode, kept in enumerate((first, second)):
            turn_real, turn_imag = cosine[mode:mode + 1], sine[mode:mode + 1]
            real_part = matrix_refs[layer][mode, 0]
            imag_part = matrix_refs[layer][mode, 1]
            kept.append(
                (
                    real_part * turn_real - imag_part * turn_imag,
                    real_part * turn_imag + imag_part * turn_real,
                )
            )
    both_first = complex_product(first[1], first[0])
    both_second = complex_product(second[1], second[0])

    order = pick_matrix(
        LEVELS, lambda row: lax.bitwise_xor(row // width, seat) * width + row % width
    )

    def put_level(ref, index, real_part, imag_part):
        full = blocks(real_part, -imag_part, imag_part, real_part)
        high, low = split_value(full)
        made = blocks(high, high, low, jnp.zeros_like(low))
        if index is None:
            ref[...] = made
        else:
            ref[index] = made

    put_level(turn_ref, None, exact(both_first[0].T, order), exact(-both_first[1].T, order))
    put_level(level_ref, 0, first[1][0].T, first[1][1].T)
    put_level(level_ref, 1, exact(first[0][0], order), exact(-first[0][1], order))
    put_level(level_ref, 2, exact(order, first[0][0].T), exact(order, first[0][1].T))

    def put_lane(index, real_part, imag_part):
        real_part, imag_part = spread(real_part), spread(imag_part)
        high, low = split_value(blocks(real_part, imag_part, -imag_part, real_part))
        lane_ref[index, 0] = high
        lane_ref[index, 1] = low

    put_lane(0, *second[1])
    put_lane(1, second[0][0].T, -second[0][1].T)
    put_lane(2, *second[0])

    real_part, imag_part = spread(both_second[0].T), spread(both_second[1].T)
    full = blocks(real_part, -imag_part, -imag_part, -real_part)

    def source(row):
        chunk, rest = row // (2 * size * parts), row % (2 * size * parts)
        step, rest = rest // (2 * size), rest % (2 * size)
        half, place = rest // size, rest % size
        return half * WIDE + lax.bitwise_xor(step, seat) * share + chunk * size + place

    high, low = split_value(exact(pick_matrix(PAIR, source), full))
    open_ref[0] = high
    open_ref[1] = low


def make_weights(phases, displacements, table_slot, checkpoint, seat, parts, chunks, waited):
    def angles(layer):
        return pl.BlockSpec(
            (None, 2, LEVELS), lambda i, slot, start, own: (slot[start[0] + layer], 0, 0)
        )

    def matrices(layer):
        return pl.BlockSpec(
            (None, 2, 2, LEVELS, LEVELS),
            lambda i, slot, start, own: (start[0] + layer, 0, 0, 0, 0),
        )

    def whole(shape):
        return pl.BlockSpec(shape, lambda i, slot, start, own: (0,) * len(shape))

    shapes = [(2, PAIR, PAIR), (PAIR, PAIR), (3, PAIR, PAIR), (3, 2, PAIR, PAIR)]
    return pl.pallas_call(
        functools.partial(weights_kernel, parts, chunks),
        grid_spec=pltpu.PrefetchScalarGridSpec(
            num_scalar_prefetch=3,
            grid=(1,),
            in_specs=[angles(0), angles(1), matrices(0), matrices(1)]
            + [pl.BlockSpec(memory_space=pl.ANY)] * len(waited),
            out_specs=[whole(shape) for shape in shapes],
        ),
        out_shape=[jax.ShapeDtypeStruct(shape, BF16) for shape in shapes],
        compiler_params=PARAMS,
        cost_estimate=pl.CostEstimate(flops=10**9, bytes_accessed=10**6, transcendentals=0),
    )(table_slot, checkpoint, seat, phases, phases, displacements, displacements, *waited)


def open_kernel(count, weight_ref, field_ref, *out_refs):
    both = jnp.concatenate([field_ref[0], field_ref[1]], axis=1)
    high, low = split_value(both)
    across = (((1,), (1,)), ((), ()))
    made = mxu(weight_ref[0], high, across) + (
        mxu(weight_ref[0], low, across) + mxu(weight_ref[1], high, across)
    )
    tall = made.shape[0] // count
    for place, out in enumerate(out_refs):
        piece = made[place * tall:(place + 1) * tall]
        for first in range(out.shape[0]):
            out[first] = piece[:, first * WIDE:(first + 1) * WIDE]


def open_state(field, weights, parts, size, chunk_start, chunk_count):
    rows, cols = field.shape[1:]
    firsts = rows // WIDE
    column_levels = cols // WIDE
    count = parts * chunk_count
    tall = count * 2 * size
    shape = jax.ShapeDtypeStruct((firsts, column_levels * 2 * size, WIDE), F32)
    weights = lax.slice_in_dim(
        weights, chunk_start * parts * 2 * size, chunk_start * parts * 2 * size + tall, axis=1
    )
    outs = pl.pallas_call(
        functools.partial(open_kernel, count),
        grid=(column_levels,),
        in_specs=[
            pl.BlockSpec((2, tall, PAIR), lambda i: (0, 0, 0)),
            pl.BlockSpec((2, rows, WIDE), lambda i: (0, 0, i)),
        ],
        out_specs=[pl.BlockSpec((firsts, 2 * size, WIDE), lambda i: (0, i, 0))] * count,
        out_shape=[shape] * count,
        compiler_params=PARAMS,
        cost_estimate=pl.CostEstimate(
            flops=6 * rows * column_levels * tall * PAIR,
            bytes_accessed=8 * rows * cols,
            transcendentals=0,
        ),
    )(weights, field)
    return [outs[c * parts:(c + 1) * parts] for c in range(chunk_count)]


def cut_kernel(size, seat_ref, field_ref, *out_refs):
    seat = seat_ref[0]
    levels = field_ref.shape[-1] // WIDE
    for step, out in enumerate(out_refs):
        part = lax.bitwise_xor(seat, step)
        for half in range(2):
            for level in range(levels):
                start = (2 * level + half) * size
                out[start:start + size, :] = field_ref[
                    half, part, :, level * WIDE:(level + 1) * WIDE
                ]


def cut_pieces(field, seat, parts, chunk, size):
    rows, cols = field.shape[1:]
    firsts = rows // WIDE
    chunks = WIDE // parts // size
    tall = cols // WIDE * 2 * size
    return pl.pallas_call(
        functools.partial(cut_kernel, size),
        grid=(firsts,),
        in_specs=[
            pl.BlockSpec(memory_space=pltpu.SMEM),
            pl.BlockSpec((2, None, parts, None, size, cols), lambda i: (0, i, 0, chunk, 0, 0)),
        ],
        out_specs=[pl.BlockSpec((None, tall, WIDE), lambda i: (i, 0, 0))] * parts,
        out_shape=[jax.ShapeDtypeStruct((firsts, tall, WIDE), F32)] * parts,
        compiler_params=PARAMS,
        cost_estimate=pl.CostEstimate(
            flops=0, bytes_accessed=16 * firsts * parts * size * cols, transcendentals=0
        ),
    )(seat, field.reshape(2, firsts, parts, chunks, size, cols))


def level_apply(weights, real_part, imag_part):
    real_high, real_low = split_value(real_part)
    imag_high, imag_low = split_value(imag_part)
    stacked = jnp.concatenate([real_high, imag_high, real_low, imag_low], axis=0)
    made = mxu(weights, stacked)
    return made[:WIDE] + made[WIDE:]


def lane_apply(weight_ref, index, real_part, imag_part):
    high, low = split_value(jnp.concatenate([real_part, imag_part], axis=1))
    made = mxu(high, weight_ref[index, 0]) + (
        mxu(low, weight_ref[index, 0]) + mxu(high, weight_ref[index, 1])
    )
    return made[:, :WIDE], made[:, WIDE:]


def gather_levels(refs, size, half):
    columns = []
    for place in range(size):
        parts = [
            ref[pl.ds(half * size + place, ref.shape[0] // (2 * size), stride=2 * size), :]
            for ref in refs
        ]
        columns.append(jnp.concatenate(parts, axis=0) if len(parts) > 1 else parts[0])
    return jnp.concatenate(columns, axis=1)


def scatter_levels(ref, size, half, value):
    for place in range(size):
        ref[pl.ds(half * size + place, LEVELS, stride=2 * size), :] = value[
            :, place * WIDE:(place + 1) * WIDE
        ]


def turn_kernel(parts, size, weight_ref, *refs):
    pieces = refs[:parts]
    out_ref = refs[-1].reshape(LEVELS * 2 * size, WIDE)
    made = level_apply(
        weight_ref[...], gather_levels(pieces, size, 0), gather_levels(pieces, size, 1)
    )
    scatter_levels(out_ref, size, 0, made[:LEVELS])
    scatter_levels(out_ref, size, 1, made[LEVELS:])


def turn_columns(pieces, weights, size, waited):
    firsts = pieces[0].shape[0]
    parts = len(pieces)
    block = pieces[0].shape[1:]
    return pl.pallas_call(
        functools.partial(turn_kernel, parts, size),
        grid=(firsts,),
        in_specs=[pl.BlockSpec((PAIR, PAIR), lambda i: (0, 0))]
        + [pl.BlockSpec((None,) + block, lambda i: (i, 0, 0))] * parts
        + [pl.BlockSpec(memory_space=pl.ANY)] * len(waited),
        out_specs=pl.BlockSpec((LEVELS, None, 2 * size, WIDE), lambda i: (0, i, 0, 0)),
        out_shape=jax.ShapeDtypeStruct((LEVELS, firsts, 2 * size, WIDE), F32),
        compiler_params=PARAMS,
        cost_estimate=pl.CostEstimate(
            flops=2 * PAIR * PAIR * firsts * size * WIDE,
            bytes_accessed=16 * LEVELS * firsts * size * WIDE,
            transcendentals=0,
        ),
    )(weights, *pieces, *waited)


def halves(value, size):
    value = value.reshape(LEVELS, 2, size, WIDE)
    rows = LEVELS * size
    return value[:, 0].reshape(rows, WIDE), value[:, 1].reshape(rows, WIDE)


def join(real_part, imag_part, size):
    shape = (LEVELS, 1, size, WIDE)
    both = jnp.concatenate([real_part.reshape(shape), imag_part.reshape(shape)], axis=1)
    return both.reshape(LEVELS * 2 * size, WIDE)


def close_kernel(parts, size, lane_ref, level_ref, field_ref, *refs):
    rho_refs = refs[:parts]
    out_refs = refs[-parts - 3:-3]
    grad_ref, work_a, work_b = refs[-3:]
    step = pl.program_id(0)

    @pl.when(step == 0)
    def _():
        grad_ref[...] = jnp.zeros_like(grad_ref)

    flat = field_ref.reshape(LEVELS * 2 * size, WIDE)
    real_part, imag_part = lane_apply(lane_ref, 0, *halves(flat[...], size))
    work_a[...] = join(real_part, imag_part, size)

    rho = jnp.concatenate([ref[...] for ref in rho_refs], axis=0)
    rho_real, rho_imag = halves(rho, size)
    real_part, imag_part = lane_apply(lane_ref, 1, rho_real, rho_imag)
    work_b[...] = join(real_part, imag_part, size)

    mid = level_apply(level_ref[0], gather_levels([work_a], size, 0), gather_levels([work_a], size, 1))
    seen = level_apply(level_ref[1], gather_levels([work_b], size, 0), gather_levels([work_b], size, 1))
    terms = seen[:LEVELS] * mid[LEVELS:] - seen[LEVELS:] * mid[:LEVELS]
    total = terms[:, :WIDE]
    for place in range(1, size):
        total = total + terms[:, place * WIDE:(place + 1) * WIDE]
    grad_ref[1] += total

    last = level_apply(level_ref[2], mid[:LEVELS], mid[LEVELS:])
    scatter_levels(work_a, size, 0, last[:LEVELS])
    scatter_levels(work_a, size, 1, last[LEVELS:])
    real_part, imag_part = lane_apply(lane_ref, 2, *halves(work_a[...], size))
    terms = rho_real * imag_part - rho_imag * real_part
    grad_ref[0] += jnp.sum(terms.reshape(LEVELS, size, WIDE), axis=1)
    made = join(real_part, imag_part, size)
    rows = made.shape[0] // parts
    for part in range(parts):
        out_refs[part][...] = made[part * rows:(part + 1) * rows]


def close_columns(field, rho_pieces, lane, level, size, waited):
    total_first, firsts = field.shape[:2]
    devs = total_first // firsts
    parts = len(rho_pieces)
    rows = LEVELS * 2 * size
    field = field.reshape(devs, firsts, firsts * 2 * size, WIDE)
    piece = rho_pieces[0]
    piece_spec = pl.BlockSpec((None,) + piece.shape[1:], lambda i: (i, 0, 0))
    outs = pl.pallas_call(
        functools.partial(close_kernel, parts, size),
        grid=(firsts,),
        in_specs=[
            pl.BlockSpec(lane.shape, lambda i: (0, 0, 0, 0)),
            pl.BlockSpec(level.shape, lambda i: (0, 0, 0)),
            pl.BlockSpec((devs, None, firsts * 2 * size, WIDE), lambda i: (0, i, 0, 0)),
        ]
        + [piece_spec] * parts
        + [pl.BlockSpec(memory_space=pl.ANY)] * len(waited),
        out_specs=[piece_spec] * parts + [pl.BlockSpec((2, LEVELS, WIDE), lambda i: (0, 0, 0))],
        out_shape=[jax.ShapeDtypeStruct(piece.shape, F32)] * parts
        + [jax.ShapeDtypeStruct((2, LEVELS, WIDE), F32)],
        scratch_shapes=[pltpu.VMEM((rows, WIDE), F32), pltpu.VMEM((rows, WIDE), F32)],
        compiler_params=PARAMS,
        cost_estimate=pl.CostEstimate(
            flops=firsts * (3 * 3 * PAIR * PAIR * rows + 3 * 2 * PAIR * PAIR * size * WIDE),
            bytes_accessed=12 * firsts * rows * WIDE,
            transcendentals=0,
        ),
    )(lane, level, field, *rho_pieces, *waited)
    return list(outs[:parts]), outs[parts]


def place_kernel(parts, size, aliased, seat_ref, *refs):
    pieces = refs[:parts]
    out_ref = refs[parts + aliased]
    seat = seat_ref[0]
    levels = pieces[0].shape[0] // (2 * size)
    for step in range(parts):
        part = lax.bitwise_xor(seat, step)
        for half in range(2):
            for level in range(levels):
                start = level * 2 * size + half * size
                out_ref[half, part, :, level * WIDE:(level + 1) * WIDE] = pieces[step][
                    start:start + size, :
                ]


def place_pieces(pieces, seat, held, chunk, shape, size):
    parts = len(pieces)
    firsts, chunks = shape[1], shape[3]
    aliased = 0 if held is None else 1
    piece = pieces[0]
    cols = shape[-1]
    return pl.pallas_call(
        functools.partial(place_kernel, parts, size, aliased),
        grid=(firsts,),
        in_specs=[pl.BlockSpec(memory_space=pltpu.SMEM)]
        + [pl.BlockSpec((None,) + piece.shape[1:], lambda i: (i, 0, 0))] * parts
        + [pl.BlockSpec(memory_space=pl.ANY)] * aliased,
        out_specs=pl.BlockSpec(
            (2, None, parts, None, size, cols), lambda i: (0, i, 0, chunk, 0, 0)
        ),
        out_shape=jax.ShapeDtypeStruct(shape, F32),
        input_output_aliases={parts + 1: 0} if aliased else {},
        compiler_params=PARAMS,
        cost_estimate=pl.CostEstimate(
            flops=0, bytes_accessed=8 * 2 * firsts * parts * size * cols, transcendentals=0
        ),
    )(seat, *pieces, *([held] if aliased else []))


def swap(pieces, parts):
    moved = [pieces[0]]
    for step in range(1, parts):
        pairs = [(member, member ^ step) for member in range(parts)]
        moved.append(lax.ppermute(pieces[step], "grp", pairs))
    return moved


def grand_total(value):
    rounds = []
    for axis in ("grp", "dev"):
        count = lax.axis_size(axis)
        rounds.append([(axis, 1 << bit, count) for bit in range(count.bit_length() - 1)])
    for axis, step, count in rounds[0][:1] + rounds[1] + rounds[0][1:]:
        pairs = [(member, member ^ step) for member in range(count)]
        value = value + lax.ppermute(value, axis, pairs)
    return value


def per_device(density, costate, phases, displacements, table_slot, checkpoint):
    parts = lax.axis_size("grp")
    share = WIDE // parts
    chunks = max(1, min(4, share // 8))
    size = share // chunks
    seat = lax.axis_index("grp").astype(jnp.int32)
    seats = seat.reshape(1)
    rows, cols = costate.shape[1:]

    rho = [cut_pieces(density, seats, parts, 0, size)]
    opened, turned_by, level, lane = make_weights(
        phases, displacements, table_slot, checkpoint, seats, parts, chunks, rho[0]
    )
    state = open_state(costate, opened, parts, size, 0, 1)
    if chunks > 1:
        state += open_state(costate, opened, parts, size, 1, chunks - 1)
    for chunk in range(1, chunks):
        rho.append(cut_pieces(density, seats, parts, chunk, size))
    state_cut = state
    state = [swap(pieces, parts) for pieces in state_cut]
    rho_there = [swap(pieces, parts) for pieces in rho]

    shape = (2, rows // WIDE, parts, chunks, size, cols)
    fields, closed, made, grads = [], [], [], []

    def close(chunk, waited):
        out, grad = close_columns(
            fields[chunk], rho_there[chunk], lane, level, size, waited
        )
        closed.append(out)
        made.append(swap(out, parts))
        grads.append(grad)

    for chunk in range(chunks):
        waited = []
        if chunk == 0:
            waited = [p for pieces in state_cut[1:2] + rho[1:2] for p in pieces[:1]]
        else:
            waited = list(rho_there[chunk - 1][1:])
        if chunk == chunks - 1 and chunks > 2:
            waited = waited + made[0][1:]
        if chunk > 1:
            close(chunk - 2, [])
            waited = waited + closed[chunk - 2][:1]
        field = turn_columns(state[chunk], turned_by, size, waited)
        fields.append(lax.all_to_all(field, "dev", split_axis=0, concat_axis=0, tiled=True))
    for chunk in range(len(made), chunks):
        close(chunk, rho_there[-1][1:] if chunk < chunks - 1 else [])
    whole = None
    for chunk in range(chunks):
        whole = place_pieces(made[chunk], seats, whole, chunk, shape, size)

    grad = sum(grads)
    lane_sum = -2.0 * jnp.sum(grad, axis=2)
    width = LEVELS // parts
    order = lax.bitwise_xor(seat, jnp.arange(parts, dtype=jnp.int32))
    order = (order[:, None] * width + jnp.arange(width, dtype=jnp.int32)[None, :]).reshape(LEVELS)
    lane_sum = jnp.stack([jnp.take(lane_sum[0], order), lane_sum[1]])
    level_sum = -2.0 * jnp.sum(jnp.sum(grad, axis=1).reshape(2, LEVELS, TRANSMON), axis=2)
    total = grand_total(jnp.stack([lane_sum, level_sum], axis=1))
    return whole.reshape(costate.shape), total


def solution(mesh):
    return jax.shard_map(
        per_device,
        mesh=mesh,
        in_specs=(P(None, "dev", "grp"), P(None, "dev", "grp"), P(), P(), P(), P()),
        out_specs=(P(None, "dev", "grp"), P()),
        check_vma=False,
    )
```

```python
import functools

import jax
import jax.numpy as jnp
from jax import lax
from jax.experimental import pallas as pl
from jax.experimental.pallas import tpu as pltpu
from jax.sharding import PartitionSpec as P

LEVELS = 64
TRANSMON = 2
WIDE = LEVELS * TRANSMON
PAIR = 2 * WIDE
HIGH = lax.Precision.HIGHEST
F32 = jnp.float32
BF16 = jnp.bfloat16
SMALL = pl.CostEstimate(flops=1024, bytes_accessed=1024, transcendentals=0)
PARAMS = pltpu.CompilerParams(vmem_limit_bytes=48 * 1024 * 1024)


def split_value(value):
    high = value.astype(BF16)
    low = (value - high.astype(F32)).astype(BF16)
    return high, low


def mxu(left, right, dims=(((1,), (0,)), ((), ()))):
    return lax.dot_general(left, right, dims, preferred_element_type=F32)


def exact(left, right, dims=(((1,), (0,)), ((), ()))):
    return lax.dot_general(left, right, dims, precision=HIGH, preferred_element_type=F32)


def grid_of(shape, dim):
    return lax.broadcasted_iota(jnp.int32, shape, dim)


def pick_matrix(count, chosen):
    shape = (count, count)
    return (chosen(grid_of(shape, 0)) == grid_of(shape, 1)).astype(F32)


def spread(matrix):
    tall = (grid_of((WIDE, LEVELS), 0) // TRANSMON == grid_of((WIDE, LEVELS), 1)).astype(F32)
    long = (grid_of((LEVELS, WIDE), 1) // TRANSMON == grid_of((LEVELS, WIDE), 0)).astype(F32)
    same = grid_of((WIDE, WIDE), 0) % TRANSMON == grid_of((WIDE, WIDE), 1) % TRANSMON
    return jnp.where(same, exact(exact(tall, matrix), long), 0.0)


def blocks(upper_left, upper_right, lower_left, lower_right):
    return jnp.concatenate(
        [
            jnp.concatenate([upper_left, upper_right], axis=1),
            jnp.concatenate([lower_left, lower_right], axis=1),
        ],
        axis=0,
    )


def complex_product(left, right):
    return (
        exact(left[0], right[0]) - exact(left[1], right[1]),
        exact(left[0], right[1]) + exact(left[1], right[0]),
    )


def weights_kernel(parts, chunks, slot_ref, start_ref, seat_ref, *refs):
    angle_refs, matrix_refs = refs[0:2], refs[2:4]
    open_ref, turn_ref, level_ref, lane_ref = refs[-4:]
    seat = seat_ref[0]
    width = LEVELS // parts
    share = WIDE // parts
    size = share // chunks
    first, second = [], []
    for layer in range(2):
        cosine = jnp.cos(angle_refs[layer][...])
        sine = jnp.sin(angle_refs[layer][...])
        for mode, kept in enumerate((first, second)):
            turn_real, turn_imag = cosine[mode:mode + 1], sine[mode:mode + 1]
            real_part = matrix_refs[layer][mode, 0]
            imag_part = matrix_refs[layer][mode, 1]
            kept.append(
                (
                    real_part * turn_real - imag_part * turn_imag,
                    real_part * turn_imag + imag_part * turn_real,
                )
            )
    both_first = complex_product(first[1], first[0])
    both_second = complex_product(second[1], second[0])

    order = pick_matrix(
        LEVELS, lambda row: lax.bitwise_xor(row // width, seat) * width + row % width
    )

    def put_level(ref, index, real_part, imag_part):
        full = blocks(real_part, -imag_part, imag_part, real_part)
        high, low = split_value(full)
        made = blocks(high, high, low, jnp.zeros_like(low))
        if index is None:
            ref[...] = made
        else:
            ref[index] = made

    put_level(turn_ref, None, exact(both_first[0].T, order), exact(-both_first[1].T, order))
    put_level(level_ref, 0, first[1][0].T, first[1][1].T)
    put_level(level_ref, 1, exact(first[0][0], order), exact(-first[0][1], order))
    put_level(level_ref, 2, exact(order, first[0][0].T), exact(order, first[0][1].T))

    def put_lane(index, real_part, imag_part):
        real_part, imag_part = spread(real_part), spread(imag_part)
        high, low = split_value(blocks(real_part, imag_part, -imag_part, real_part))
        lane_ref[index, 0] = high
        lane_ref[index, 1] = low

    put_lane(0, *second[1])
    put_lane(1, second[0][0].T, -second[0][1].T)
    put_lane(2, *second[0])

    real_part, imag_part = spread(both_second[0].T), spread(both_second[1].T)
    full = blocks(real_part, -imag_part, -imag_part, -real_part)

    def source(row):
        chunk, rest = row // (2 * size * parts), row % (2 * size * parts)
        step, rest = rest // (2 * size), rest % (2 * size)
        half, place = rest // size, rest % size
        return half * WIDE + lax.bitwise_xor(step, seat) * share + chunk * size + place

    high, low = split_value(exact(pick_matrix(PAIR, source), full))
    open_ref[0] = high
    open_ref[1] = low


def make_weights(phases, displacements, table_slot, checkpoint, seat, parts, chunks):
    def angles(layer):
        return pl.BlockSpec(
            (None, 2, LEVELS), lambda i, slot, start, own: (slot[start[0] + layer], 0, 0)
        )

    def matrices(layer):
        return pl.BlockSpec(
            (None, 2, 2, LEVELS, LEVELS),
            lambda i, slot, start, own: (start[0] + layer, 0, 0, 0, 0),
        )

    def whole(shape):
        return pl.BlockSpec(shape, lambda i, slot, start, own: (0,) * len(shape))

    shapes = [(2, PAIR, PAIR), (PAIR, PAIR), (3, PAIR, PAIR), (3, 2, PAIR, PAIR)]
    return pl.pallas_call(
        functools.partial(weights_kernel, parts, chunks),
        grid_spec=pltpu.PrefetchScalarGridSpec(
            num_scalar_prefetch=3,
            grid=(1,),
            in_specs=[angles(0), angles(1), matrices(0), matrices(1)],
            out_specs=[whole(shape) for shape in shapes],
        ),
        out_shape=[jax.ShapeDtypeStruct(shape, BF16) for shape in shapes],
        compiler_params=PARAMS,
        cost_estimate=SMALL,
    )(table_slot, checkpoint, seat, phases, phases, displacements, displacements)


def open_kernel(count, waited, weight_ref, field_ref, *refs):
    both = jnp.concatenate([field_ref[0], field_ref[1]], axis=1)
    high, low = split_value(both)
    across = (((1,), (1,)), ((), ()))
    made = mxu(weight_ref[0], high, across) + (
        mxu(weight_ref[0], low, across) + mxu(weight_ref[1], high, across)
    )
    tall = made.shape[0] // count
    for place, out in enumerate(refs[waited:]):
        piece = made[place * tall:(place + 1) * tall]
        for first in range(out.shape[0]):
            out[first] = piece[:, first * WIDE:(first + 1) * WIDE]


def open_state(field, weights, parts, size, chunk_start, chunk_count, waited):
    rows, cols = field.shape[1:]
    firsts = rows // WIDE
    column_levels = cols // WIDE
    count = parts * chunk_count
    tall = count * 2 * size
    shape = jax.ShapeDtypeStruct((firsts, column_levels * 2 * size, WIDE), F32)
    weights = lax.slice_in_dim(
        weights, chunk_start * parts * 2 * size, chunk_start * parts * 2 * size + tall, axis=1
    )
    outs = pl.pallas_call(
        functools.partial(open_kernel, count, len(waited)),
        grid=(column_levels,),
        in_specs=[
            pl.BlockSpec((2, tall, PAIR), lambda i: (0, 0, 0)),
            pl.BlockSpec((2, rows, WIDE), lambda i: (0, 0, i)),
        ]
        + [pl.BlockSpec(memory_space=pl.ANY)] * len(waited),
        out_specs=[pl.BlockSpec((firsts, 2 * size, WIDE), lambda i: (0, i, 0))] * count,
        out_shape=[shape] * count,
        compiler_params=PARAMS,
        cost_estimate=SMALL,
    )(weights, field, *waited)
    return [outs[c * parts:(c + 1) * parts] for c in range(chunk_count)]


def cut_kernel(size, waited, seat_ref, field_ref, *refs):
    seat = seat_ref[0]
    levels = field_ref.shape[-1] // WIDE
    for step, out in enumerate(refs[waited:]):
        part = lax.bitwise_xor(seat, step)
        for half in range(2):
            for level in range(levels):
                start = (2 * level + half) * size
                out[start:start + size, :] = field_ref[
                    half, part, :, level * WIDE:(level + 1) * WIDE
                ]


def cut_pieces(field, seat, parts, chunk, size, waited):
    rows, cols = field.shape[1:]
    firsts = rows // WIDE
    chunks = WIDE // parts // size
    tall = cols // WIDE * 2 * size
    return pl.pallas_call(
        functools.partial(cut_kernel, size, len(waited)),
        grid=(firsts,),
        in_specs=[
            pl.BlockSpec(memory_space=pltpu.SMEM),
            pl.BlockSpec((2, None, parts, None, size, cols), lambda i: (0, i, 0, chunk, 0, 0)),
        ]
        + [pl.BlockSpec(memory_space=pl.ANY)] * len(waited),
        out_specs=[pl.BlockSpec((None, tall, WIDE), lambda i: (i, 0, 0))] * parts,
        out_shape=[jax.ShapeDtypeStruct((firsts, tall, WIDE), F32)] * parts,
        compiler_params=PARAMS,
        cost_estimate=SMALL,
    )(seat, field.reshape(2, firsts, parts, chunks, size, cols), *waited)


def level_apply(weights, real_part, imag_part):
    real_high, real_low = split_value(real_part)
    imag_high, imag_low = split_value(imag_part)
    stacked = jnp.concatenate([real_high, imag_high, real_low, imag_low], axis=0)
    made = mxu(weights, stacked)
    return made[:WIDE] + made[WIDE:]


def lane_apply(weight_ref, index, real_part, imag_part):
    high, low = split_value(jnp.concatenate([real_part, imag_part], axis=1))
    made = mxu(high, weight_ref[index, 0]) + (
        mxu(low, weight_ref[index, 0]) + mxu(high, weight_ref[index, 1])
    )
    return made[:, :WIDE], made[:, WIDE:]


def gather_levels(refs, size, half):
    columns = []
    for place in range(size):
        parts = [
            ref[pl.ds(half * size + place, ref.shape[0] // (2 * size), stride=2 * size), :]
            for ref in refs
        ]
        columns.append(jnp.concatenate(parts, axis=0) if len(parts) > 1 else parts[0])
    return jnp.concatenate(columns, axis=1)


def scatter_levels(ref, size, half, value):
    for place in range(size):
        ref[pl.ds(half * size + place, LEVELS, stride=2 * size), :] = value[
            :, place * WIDE:(place + 1) * WIDE
        ]


def turn_kernel(parts, size, weight_ref, *refs):
    pieces = refs[:parts]
    out_ref = refs[-1].reshape(LEVELS * 2 * size, WIDE)
    made = level_apply(
        weight_ref[...], gather_levels(pieces, size, 0), gather_levels(pieces, size, 1)
    )
    scatter_levels(out_ref, size, 0, made[:LEVELS])
    scatter_levels(out_ref, size, 1, made[LEVELS:])


def turn_columns(pieces, weights, size, waited):
    firsts = pieces[0].shape[0]
    parts = len(pieces)
    block = pieces[0].shape[1:]
    return pl.pallas_call(
        functools.partial(turn_kernel, parts, size),
        grid=(firsts,),
        in_specs=[pl.BlockSpec((PAIR, PAIR), lambda i: (0, 0))]
        + [pl.BlockSpec((None,) + block, lambda i: (i, 0, 0))] * parts
        + [pl.BlockSpec(memory_space=pl.ANY)] * len(waited),
        out_specs=pl.BlockSpec((LEVELS, None, 2 * size, WIDE), lambda i: (0, i, 0, 0)),
        out_shape=jax.ShapeDtypeStruct((LEVELS, firsts, 2 * size, WIDE), F32),
        compiler_params=PARAMS,
        cost_estimate=SMALL,
    )(weights, *pieces, *waited)


def halves(value, size):
    value = value.reshape(LEVELS, 2, size, WIDE)
    rows = LEVELS * size
    return value[:, 0].reshape(rows, WIDE), value[:, 1].reshape(rows, WIDE)


def join(real_part, imag_part, size):
    shape = (LEVELS, 1, size, WIDE)
    both = jnp.concatenate([real_part.reshape(shape), imag_part.reshape(shape)], axis=1)
    return both.reshape(LEVELS * 2 * size, WIDE)


def close_kernel(parts, size, lane_ref, level_ref, field_ref, *refs):
    rho_refs = refs[:parts]
    out_refs = refs[-parts - 3:-3]
    grad_ref, work_a, work_b = refs[-3:]
    step = pl.program_id(0)

    @pl.when(step == 0)
    def _():
        grad_ref[...] = jnp.zeros_like(grad_ref)

    flat = field_ref.reshape(LEVELS * 2 * size, WIDE)
    real_part, imag_part = lane_apply(lane_ref, 0, *halves(flat[...], size))
    work_a[...] = join(real_part, imag_part, size)

    rho = jnp.concatenate([ref[...] for ref in rho_refs], axis=0)
    rho_real, rho_imag = halves(rho, size)
    real_part, imag_part = lane_apply(lane_ref, 1, rho_real, rho_imag)
    work_b[...] = join(real_part, imag_part, size)

    mid = level_apply(level_ref[0], gather_levels([work_a], size, 0), gather_levels([work_a], size, 1))
    seen = level_apply(level_ref[1], gather_levels([work_b], size, 0), gather_levels([work_b], size, 1))
    terms = seen[:LEVELS] * mid[LEVELS:] - seen[LEVELS:] * mid[:LEVELS]
    total = terms[:, :WIDE]
    for place in range(1, size):
        total = total + terms[:, place * WIDE:(place + 1) * WIDE]
    grad_ref[1] += total

    last = level_apply(level_ref[2], mid[:LEVELS], mid[LEVELS:])
    scatter_levels(work_a, size, 0, last[:LEVELS])
    scatter_levels(work_a, size, 1, last[LEVELS:])
    real_part, imag_part = lane_apply(lane_ref, 2, *halves(work_a[...], size))
    terms = rho_real * imag_part - rho_imag * real_part
    grad_ref[0] += jnp.sum(terms.reshape(LEVELS, size, WIDE), axis=1)
    made = join(real_part, imag_part, size)
    rows = made.shape[0] // parts
    for part in range(parts):
        out_refs[part][...] = made[part * rows:(part + 1) * rows]


def close_columns(field, rho_pieces, lane, level, size, waited):
    total_first, firsts = field.shape[:2]
    devs = total_first // firsts
    parts = len(rho_pieces)
    rows = LEVELS * 2 * size
    field = field.reshape(devs, firsts, firsts * 2 * size, WIDE)
    piece = rho_pieces[0]
    piece_spec = pl.BlockSpec((None,) + piece.shape[1:], lambda i: (i, 0, 0))
    outs = pl.pallas_call(
        functools.partial(close_kernel, parts, size),
        grid=(firsts,),
        in_specs=[
            pl.BlockSpec(lane.shape, lambda i: (0, 0, 0, 0)),
            pl.BlockSpec(level.shape, lambda i: (0, 0, 0)),
            pl.BlockSpec((devs, None, firsts * 2 * size, WIDE), lambda i: (0, i, 0, 0)),
        ]
        + [piece_spec] * parts
        + [pl.BlockSpec(memory_space=pl.ANY)] * len(waited),
        out_specs=[piece_spec] * parts + [pl.BlockSpec((2, LEVELS, WIDE), lambda i: (0, 0, 0))],
        out_shape=[jax.ShapeDtypeStruct(piece.shape, F32)] * parts
        + [jax.ShapeDtypeStruct((2, LEVELS, WIDE), F32)],
        scratch_shapes=[pltpu.VMEM((rows, WIDE), F32), pltpu.VMEM((rows, WIDE), F32)],
        compiler_params=PARAMS,
        cost_estimate=SMALL,
    )(lane, level, field, *rho_pieces, *waited)
    return list(outs[:parts]), outs[parts]


def place_kernel(parts, size, aliased, seat_ref, *refs):
    pieces = refs[:parts]
    out_ref = refs[parts + aliased]
    seat = seat_ref[0]
    levels = pieces[0].shape[0] // (2 * size)
    for step in range(parts):
        part = lax.bitwise_xor(seat, step)
        for half in range(2):
            for level in range(levels):
                start = level * 2 * size + half * size
                out_ref[half, part, :, level * WIDE:(level + 1) * WIDE] = pieces[step][
                    start:start + size, :
                ]


def place_pieces(pieces, seat, held, chunk, shape, size):
    parts = len(pieces)
    firsts, chunks = shape[1], shape[3]
    aliased = 0 if held is None else 1
    piece = pieces[0]
    cols = shape[-1]
    return pl.pallas_call(
        functools.partial(place_kernel, parts, size, aliased),
        grid=(firsts,),
        in_specs=[pl.BlockSpec(memory_space=pltpu.SMEM)]
        + [pl.BlockSpec((None,) + piece.shape[1:], lambda i: (i, 0, 0))] * parts
        + [pl.BlockSpec(memory_space=pl.ANY)] * aliased,
        out_specs=pl.BlockSpec(
            (2, None, parts, None, size, cols), lambda i: (0, i, 0, chunk, 0, 0)
        ),
        out_shape=jax.ShapeDtypeStruct(shape, F32),
        input_output_aliases={parts + 1: 0} if aliased else {},
        compiler_params=PARAMS,
        cost_estimate=SMALL,
    )(seat, *pieces, *([held] if aliased else []))


def swap(pieces, parts):
    moved = [pieces[0]]
    for step in range(1, parts):
        pairs = [(member, member ^ step) for member in range(parts)]
        moved.append(lax.ppermute(pieces[step], "grp", pairs))
    return moved


def grand_total(value):
    return jnp.sum(lax.all_gather(value, ("grp", "dev")), axis=0)


def per_device(density, costate, phases, displacements, table_slot, checkpoint):
    parts = lax.axis_size("grp")
    share = WIDE // parts
    chunks = max(1, min(4, share // 8))
    size = share // chunks
    seat = lax.axis_index("grp").astype(jnp.int32)
    seats = seat.reshape(1)
    rows, cols = costate.shape[1:]

    opened, turned_by, level, lane = make_weights(
        phases, displacements, table_slot, checkpoint, seats, parts, chunks
    )
    state_cut = open_state(costate, opened, parts, size, 0, 1, [])
    if chunks > 1:
        state_cut += open_state(
            costate, opened, parts, size, 1, chunks - 1, list(state_cut[0][:1])
        )
    rho = [cut_pieces(density, seats, parts, 0, size, list(state_cut[-1][:1]))]
    state = [swap(pieces, parts) for pieces in state_cut]
    rho_there = [swap(rho[0], parts)]

    shape = (2, rows // WIDE, parts, chunks, size, cols)
    fields, closed, made, grads = [], [], [], []

    def close(chunk, waited):
        out, grad = close_columns(
            fields[chunk], rho_there[chunk], lane, level, size, waited
        )
        closed.append(out)
        made.append(swap(out, parts))
        grads.append(grad)

    for chunk in range(chunks):
        waited = list(rho[0][:1]) if chunk == 0 else []
        if chunk > 1:
            close(chunk - 2, [])
            waited = closed[chunk - 2][:1]
        field = turn_columns(state[chunk], turned_by, size, waited)
        if chunk > 0:
            rho_there.append(swap(cut_pieces(density, seats, parts, chunk, size, [field]), parts))
        fields.append(lax.all_to_all(field, "dev", split_axis=0, concat_axis=0, tiled=True))
    for chunk in range(len(made), chunks):
        close(chunk, closed[chunk - 1][:1] if chunk > 0 else [])
    whole = None
    for chunk in range(chunks):
        whole = place_pieces(made[chunk], seats, whole, chunk, shape, size)

    grad = sum(grads)
    lane_sum = -2.0 * jnp.sum(grad, axis=2)
    width = LEVELS // parts
    order = lax.bitwise_xor(seat, jnp.arange(parts, dtype=jnp.int32))
    order = (order[:, None] * width + jnp.arange(width, dtype=jnp.int32)[None, :]).reshape(LEVELS)
    lane_sum = jnp.stack([jnp.take(lane_sum[0], order), lane_sum[1]])
    level_sum = -2.0 * jnp.sum(jnp.sum(grad, axis=1).reshape(2, LEVELS, TRANSMON), axis=2)
    total = grand_total(jnp.stack([lane_sum, level_sum], axis=1))
    return whole.reshape(costate.shape), total


def solution(mesh):
    return jax.shard_map(
        per_device,
        mesh=mesh,
        in_specs=(P(None, "dev", "grp"), P(None, "dev", "grp"), P(), P(), P(), P()),
        out_specs=(P(None, "dev", "grp"), P()),
        check_vma=False,
    )
```

```python
import functools

import jax
import jax.numpy as jnp
from jax import lax
from jax.experimental import pallas as pl
from jax.experimental.pallas import tpu as pltpu
from jax.sharding import PartitionSpec as P

LEVELS = 64
TRANSMON = 2
WIDE = LEVELS * TRANSMON
PAIR = 2 * WIDE
HIGH = lax.Precision.HIGHEST
F32 = jnp.float32
BF16 = jnp.bfloat16
SMALL = pl.CostEstimate(flops=1024, bytes_accessed=1024, transcendentals=0)
LARGE = pl.CostEstimate(flops=2 * 10**11, bytes_accessed=1024, transcendentals=0)
PARAMS = pltpu.CompilerParams(vmem_limit_bytes=48 * 1024 * 1024)


def split_value(value):
    high = value.astype(BF16)
    low = (value - high.astype(F32)).astype(BF16)
    return high, low


def mxu(left, right, dims=(((1,), (0,)), ((), ()))):
    return lax.dot_general(left, right, dims, preferred_element_type=F32)


def exact(left, right, dims=(((1,), (0,)), ((), ()))):
    return lax.dot_general(left, right, dims, precision=HIGH, preferred_element_type=F32)


def grid_of(shape, dim):
    return lax.broadcasted_iota(jnp.int32, shape, dim)


def pick_matrix(count, chosen):
    shape = (count, count)
    return (chosen(grid_of(shape, 0)) == grid_of(shape, 1)).astype(F32)


def spread(matrix):
    tall = (grid_of((WIDE, LEVELS), 0) // TRANSMON == grid_of((WIDE, LEVELS), 1)).astype(F32)
    long = (grid_of((LEVELS, WIDE), 1) // TRANSMON == grid_of((LEVELS, WIDE), 0)).astype(F32)
    same = grid_of((WIDE, WIDE), 0) % TRANSMON == grid_of((WIDE, WIDE), 1) % TRANSMON
    return jnp.where(same, exact(exact(tall, matrix), long), 0.0)


def blocks(upper_left, upper_right, lower_left, lower_right):
    return jnp.concatenate(
        [
            jnp.concatenate([upper_left, upper_right], axis=1),
            jnp.concatenate([lower_left, lower_right], axis=1),
        ],
        axis=0,
    )


def complex_product(left, right):
    return (
        exact(left[0], right[0]) - exact(left[1], right[1]),
        exact(left[0], right[1]) + exact(left[1], right[0]),
    )


def weights_kernel(parts, chunks, slot_ref, start_ref, seat_ref, *refs):
    angle_refs, matrix_refs = refs[0:2], refs[2:4]
    open_ref, turn_ref, level_ref, lane_ref = refs[-4:]
    seat = seat_ref[0]
    width = LEVELS // parts
    share = WIDE // parts
    size = share // chunks
    first, second = [], []
    for layer in range(2):
        cosine = jnp.cos(angle_refs[layer][...])
        sine = jnp.sin(angle_refs[layer][...])
        for mode, kept in enumerate((first, second)):
            turn_real, turn_imag = cosine[mode:mode + 1], sine[mode:mode + 1]
            real_part = matrix_refs[layer][mode, 0]
            imag_part = matrix_refs[layer][mode, 1]
            kept.append(
                (
                    real_part * turn_real - imag_part * turn_imag,
                    real_part * turn_imag + imag_part * turn_real,
                )
            )
    both_first = complex_product(first[1], first[0])
    both_second = complex_product(second[1], second[0])

    order = pick_matrix(
        LEVELS, lambda row: lax.bitwise_xor(row // width, seat) * width + row % width
    )

    def put_level(ref, index, real_part, imag_part):
        full = blocks(real_part, -imag_part, imag_part, real_part)
        high, low = split_value(full)
        made = blocks(high, high, low, jnp.zeros_like(low))
        if index is None:
            ref[...] = made
        else:
            ref[index] = made

    put_level(turn_ref, None, exact(both_first[0].T, order), exact(-both_first[1].T, order))
    put_level(level_ref, 0, first[1][0].T, first[1][1].T)
    put_level(level_ref, 1, exact(first[0][0], order), exact(-first[0][1], order))
    put_level(level_ref, 2, exact(order, first[0][0].T), exact(order, first[0][1].T))

    def put_lane(index, real_part, imag_part):
        real_part, imag_part = spread(real_part), spread(imag_part)
        high, low = split_value(blocks(real_part, imag_part, -imag_part, real_part))
        lane_ref[index, 0] = high
        lane_ref[index, 1] = low

    put_lane(0, *second[1])
    put_lane(1, second[0][0].T, -second[0][1].T)
    put_lane(2, *second[0])

    real_part, imag_part = spread(both_second[0].T), spread(both_second[1].T)
    full = blocks(real_part, -imag_part, -imag_part, -real_part)

    def source(row):
        chunk, rest = row // (2 * size * parts), row % (2 * size * parts)
        step, rest = rest // (2 * size), rest % (2 * size)
        half, place = rest // size, rest % size
        return half * WIDE + lax.bitwise_xor(step, seat) * share + chunk * size + place

    high, low = split_value(exact(pick_matrix(PAIR, source), full))
    open_ref[0] = high
    open_ref[1] = low


def make_weights(phases, displacements, table_slot, checkpoint, seat, parts, chunks):
    def angles(layer):
        return pl.BlockSpec(
            (None, 2, LEVELS), lambda i, slot, start, own: (slot[start[0] + layer], 0, 0)
        )

    def matrices(layer):
        return pl.BlockSpec(
            (None, 2, 2, LEVELS, LEVELS),
            lambda i, slot, start, own: (start[0] + layer, 0, 0, 0, 0),
        )

    def whole(shape):
        return pl.BlockSpec(shape, lambda i, slot, start, own: (0,) * len(shape))

    shapes = [(2, PAIR, PAIR), (PAIR, PAIR), (3, PAIR, PAIR), (3, 2, PAIR, PAIR)]
    return pl.pallas_call(
        functools.partial(weights_kernel, parts, chunks),
        grid_spec=pltpu.PrefetchScalarGridSpec(
            num_scalar_prefetch=3,
            grid=(1,),
            in_specs=[angles(0), angles(1), matrices(0), matrices(1)],
            out_specs=[whole(shape) for shape in shapes],
        ),
        out_shape=[jax.ShapeDtypeStruct(shape, BF16) for shape in shapes],
        compiler_params=PARAMS,
        cost_estimate=SMALL,
    )(table_slot, checkpoint, seat, phases, phases, displacements, displacements)


def open_kernel(count, waited, weight_ref, field_ref, *refs):
    both = jnp.concatenate([field_ref[0], field_ref[1]], axis=1)
    high, low = split_value(both)
    across = (((1,), (1,)), ((), ()))
    made = mxu(weight_ref[0], high, across) + (
        mxu(weight_ref[0], low, across) + mxu(weight_ref[1], high, across)
    )
    tall = made.shape[0] // count
    for place, out in enumerate(refs[waited:]):
        piece = made[place * tall:(place + 1) * tall]
        for first in range(out.shape[0]):
            out[first] = piece[:, first * WIDE:(first + 1) * WIDE]


def open_state(field, weights, parts, size, chunk_start, chunk_count, waited):
    rows, cols = field.shape[1:]
    firsts = rows // WIDE
    column_levels = cols // WIDE
    count = parts * chunk_count
    tall = count * 2 * size
    shape = jax.ShapeDtypeStruct((firsts, column_levels * 2 * size, WIDE), F32)
    weights = lax.slice_in_dim(
        weights, chunk_start * parts * 2 * size, chunk_start * parts * 2 * size + tall, axis=1
    )
    outs = pl.pallas_call(
        functools.partial(open_kernel, count, len(waited)),
        grid=(column_levels,),
        in_specs=[
            pl.BlockSpec((2, tall, PAIR), lambda i: (0, 0, 0)),
            pl.BlockSpec((2, rows, WIDE), lambda i: (0, 0, i)),
        ]
        + [pl.BlockSpec(memory_space=pl.ANY)] * len(waited),
        out_specs=[pl.BlockSpec((firsts, 2 * size, WIDE), lambda i: (0, i, 0))] * count,
        out_shape=[shape] * count,
        compiler_params=PARAMS,
        cost_estimate=SMALL,
    )(weights, field, *waited)
    return [outs[c * parts:(c + 1) * parts] for c in range(chunk_count)]


def cut_kernel(size, waited, seat_ref, field_ref, *refs):
    seat = seat_ref[0]
    levels = field_ref.shape[-1] // WIDE
    for step, out in enumerate(refs[waited:]):
        part = lax.bitwise_xor(seat, step)
        for half in range(2):
            for level in range(levels):
                start = (2 * level + half) * size
                out[start:start + size, :] = field_ref[
                    half, part, :, level * WIDE:(level + 1) * WIDE
                ]


def cut_pieces(field, seat, parts, chunk, size, waited):
    rows, cols = field.shape[1:]
    firsts = rows // WIDE
    chunks = WIDE // parts // size
    tall = cols // WIDE * 2 * size
    return pl.pallas_call(
        functools.partial(cut_kernel, size, len(waited)),
        grid=(firsts,),
        in_specs=[
            pl.BlockSpec(memory_space=pltpu.SMEM),
            pl.BlockSpec((2, None, parts, None, size, cols), lambda i: (0, i, 0, chunk, 0, 0)),
        ]
        + [pl.BlockSpec(memory_space=pl.ANY)] * len(waited),
        out_specs=[pl.BlockSpec((None, tall, WIDE), lambda i: (i, 0, 0))] * parts,
        out_shape=[jax.ShapeDtypeStruct((firsts, tall, WIDE), F32)] * parts,
        compiler_params=PARAMS,
        cost_estimate=SMALL,
    )(seat, field.reshape(2, firsts, parts, chunks, size, cols), *waited)


def level_apply(weights, real_part, imag_part):
    real_high, real_low = split_value(real_part)
    imag_high, imag_low = split_value(imag_part)
    stacked = jnp.concatenate([real_high, imag_high, real_low, imag_low], axis=0)
    made = mxu(weights, stacked)
    return made[:WIDE] + made[WIDE:]


def lane_apply(weight_ref, index, real_part, imag_part):
    high, low = split_value(jnp.concatenate([real_part, imag_part], axis=1))
    made = mxu(high, weight_ref[index, 0]) + (
        mxu(low, weight_ref[index, 0]) + mxu(high, weight_ref[index, 1])
    )
    return made[:, :WIDE], made[:, WIDE:]


def gather_levels(refs, size, half):
    columns = []
    for place in range(size):
        parts = [
            ref[pl.ds(half * size + place, ref.shape[0] // (2 * size), stride=2 * size), :]
            for ref in refs
        ]
        columns.append(jnp.concatenate(parts, axis=0) if len(parts) > 1 else parts[0])
    return jnp.concatenate(columns, axis=1)


def scatter_levels(ref, size, half, value):
    for place in range(size):
        ref[pl.ds(half * size + place, LEVELS, stride=2 * size), :] = value[
            :, place * WIDE:(place + 1) * WIDE
        ]


def turn_kernel(parts, size, weight_ref, *refs):
    pieces = refs[:parts]
    out_ref = refs[-1].reshape(LEVELS * 2 * size, WIDE)
    made = level_apply(
        weight_ref[...], gather_levels(pieces, size, 0), gather_levels(pieces, size, 1)
    )
    scatter_levels(out_ref, size, 0, made[:LEVELS])
    scatter_levels(out_ref, size, 1, made[LEVELS:])


def turn_columns(pieces, weights, size, waited):
    firsts = pieces[0].shape[0]
    parts = len(pieces)
    block = pieces[0].shape[1:]
    return pl.pallas_call(
        functools.partial(turn_kernel, parts, size),
        grid=(firsts,),
        in_specs=[pl.BlockSpec((PAIR, PAIR), lambda i: (0, 0))]
        + [pl.BlockSpec((None,) + block, lambda i: (i, 0, 0))] * parts
        + [pl.BlockSpec(memory_space=pl.ANY)] * len(waited),
        out_specs=pl.BlockSpec((LEVELS, None, 2 * size, WIDE), lambda i: (0, i, 0, 0)),
        out_shape=jax.ShapeDtypeStruct((LEVELS, firsts, 2 * size, WIDE), F32),
        compiler_params=PARAMS,
        cost_estimate=SMALL,
    )(weights, *pieces, *waited)


def halves(value, size):
    value = value.reshape(LEVELS, 2, size, WIDE)
    rows = LEVELS * size
    return value[:, 0].reshape(rows, WIDE), value[:, 1].reshape(rows, WIDE)


def join(real_part, imag_part, size):
    shape = (LEVELS, 1, size, WIDE)
    both = jnp.concatenate([real_part.reshape(shape), imag_part.reshape(shape)], axis=1)
    return both.reshape(LEVELS * 2 * size, WIDE)


def close_kernel(parts, size, lane_ref, level_ref, field_ref, *refs):
    rho_refs = refs[:parts]
    out_refs = refs[-parts - 3:-3]
    grad_ref, work_a, work_b = refs[-3:]
    step = pl.program_id(0)

    @pl.when(step == 0)
    def _():
        grad_ref[...] = jnp.zeros_like(grad_ref)

    flat = field_ref.reshape(LEVELS * 2 * size, WIDE)
    real_part, imag_part = lane_apply(lane_ref, 0, *halves(flat[...], size))
    work_a[...] = join(real_part, imag_part, size)

    rho = jnp.concatenate([ref[...] for ref in rho_refs], axis=0)
    rho_real, rho_imag = halves(rho, size)
    real_part, imag_part = lane_apply(lane_ref, 1, rho_real, rho_imag)
    work_b[...] = join(real_part, imag_part, size)

    mid = level_apply(level_ref[0], gather_levels([work_a], size, 0), gather_levels([work_a], size, 1))
    seen = level_apply(level_ref[1], gather_levels([work_b], size, 0), gather_levels([work_b], size, 1))
    terms = seen[:LEVELS] * mid[LEVELS:] - seen[LEVELS:] * mid[:LEVELS]
    total = terms[:, :WIDE]
    for place in range(1, size):
        total = total + terms[:, place * WIDE:(place + 1) * WIDE]
    grad_ref[1] += total

    last = level_apply(level_ref[2], mid[:LEVELS], mid[LEVELS:])
    scatter_levels(work_a, size, 0, last[:LEVELS])
    scatter_levels(work_a, size, 1, last[LEVELS:])
    real_part, imag_part = lane_apply(lane_ref, 2, *halves(work_a[...], size))
    terms = rho_real * imag_part - rho_imag * real_part
    grad_ref[0] += jnp.sum(terms.reshape(LEVELS, size, WIDE), axis=1)
    made = join(real_part, imag_part, size)
    rows = made.shape[0] // parts
    for part in range(parts):
        out_refs[part][...] = made[part * rows:(part + 1) * rows]


def close_columns(field, rho_pieces, lane, level, size, waited):
    total_first, firsts = field.shape[:2]
    devs = total_first // firsts
    parts = len(rho_pieces)
    rows = LEVELS * 2 * size
    field = field.reshape(devs, firsts, firsts * 2 * size, WIDE)
    piece = rho_pieces[0]
    piece_spec = pl.BlockSpec((None,) + piece.shape[1:], lambda i: (i, 0, 0))
    outs = pl.pallas_call(
        functools.partial(close_kernel, parts, size),
        grid=(firsts,),
        in_specs=[
            pl.BlockSpec(lane.shape, lambda i: (0, 0, 0, 0)),
            pl.BlockSpec(level.shape, lambda i: (0, 0, 0)),
            pl.BlockSpec((devs, None, firsts * 2 * size, WIDE), lambda i: (0, i, 0, 0)),
        ]
        + [piece_spec] * parts
        + [pl.BlockSpec(memory_space=pl.ANY)] * len(waited),
        out_specs=[piece_spec] * parts + [pl.BlockSpec((2, LEVELS, WIDE), lambda i: (0, 0, 0))],
        out_shape=[jax.ShapeDtypeStruct(piece.shape, F32)] * parts
        + [jax.ShapeDtypeStruct((2, LEVELS, WIDE), F32)],
        scratch_shapes=[pltpu.VMEM((rows, WIDE), F32), pltpu.VMEM((rows, WIDE), F32)],
        compiler_params=PARAMS,
        cost_estimate=LARGE,
    )(lane, level, field, *rho_pieces, *waited)
    return list(outs[:parts]), outs[parts]


def place_kernel(parts, size, aliased, seat_ref, *refs):
    pieces = refs[:parts]
    out_ref = refs[parts + aliased]
    seat = seat_ref[0]
    levels = pieces[0].shape[0] // (2 * size)
    for step in range(parts):
        part = lax.bitwise_xor(seat, step)
        for half in range(2):
            for level in range(levels):
                start = level * 2 * size + half * size
                out_ref[half, part, :, level * WIDE:(level + 1) * WIDE] = pieces[step][
                    start:start + size, :
                ]


def place_pieces(pieces, seat, held, chunk, shape, size):
    parts = len(pieces)
    firsts, chunks = shape[1], shape[3]
    aliased = 0 if held is None else 1
    piece = pieces[0]
    cols = shape[-1]
    return pl.pallas_call(
        functools.partial(place_kernel, parts, size, aliased),
        grid=(firsts,),
        in_specs=[pl.BlockSpec(memory_space=pltpu.SMEM)]
        + [pl.BlockSpec((None,) + piece.shape[1:], lambda i: (i, 0, 0))] * parts
        + [pl.BlockSpec(memory_space=pl.ANY)] * aliased,
        out_specs=pl.BlockSpec(
            (2, None, parts, None, size, cols), lambda i: (0, i, 0, chunk, 0, 0)
        ),
        out_shape=jax.ShapeDtypeStruct(shape, F32),
        input_output_aliases={parts + 1: 0} if aliased else {},
        compiler_params=PARAMS,
        cost_estimate=SMALL,
    )(seat, *pieces, *([held] if aliased else []))


def swap(pieces, parts):
    moved = [pieces[0]]
    for step in range(1, parts):
        pairs = [(member, member ^ step) for member in range(parts)]
        moved.append(lax.ppermute(pieces[step], "grp", pairs))
    return moved


def grad_kernel(parts, count, seat_ref, *refs):
    out_ref = refs[-1]
    grad = refs[0][...]
    for ref in refs[1:count]:
        grad = grad + ref[...]
    grad = -2.0 * grad
    width = LEVELS // parts
    order = pick_matrix(
        LEVELS, lambda row: lax.bitwise_xor(row // width, seat_ref[0]) * width + row % width
    )
    fold = (grid_of((WIDE, LEVELS), 0) // TRANSMON == grid_of((WIDE, LEVELS), 1)).astype(F32)
    for layer in range(2):
        firsts = exact(jnp.ones((8, WIDE), F32), grad[layer], (((1,), (1,)), ((), ())))
        if layer == 0:
            firsts = exact(firsts, order)
        seconds = exact(exact(jnp.ones((8, LEVELS), F32), grad[layer]), fold)
        out_ref[2 * layer:2 * layer + 1, :] = firsts[:1]
        out_ref[2 * layer + 1:2 * layer + 2, :] = seconds[:1]


def device_grad(grads, seat, parts, waited):
    return pl.pallas_call(
        functools.partial(grad_kernel, parts, len(grads)),
        in_specs=[pl.BlockSpec(memory_space=pltpu.SMEM)]
        + [pl.BlockSpec(memory_space=pltpu.VMEM)] * len(grads)
        + [pl.BlockSpec(memory_space=pl.ANY)] * len(waited),
        out_specs=pl.BlockSpec(memory_space=pltpu.VMEM),
        out_shape=jax.ShapeDtypeStruct((4, LEVELS), F32),
        compiler_params=PARAMS,
        cost_estimate=SMALL,
    )(seat, *grads, *waited)


def grand_total(value):
    rounds = []
    for axis in ("grp", "dev"):
        count = lax.axis_size(axis)
        rounds.append([(axis, 1 << bit, count) for bit in range(count.bit_length() - 1)])
    for axis, step, count in rounds[0][:1] + rounds[1] + rounds[0][1:]:
        pairs = [(member, member ^ step) for member in range(count)]
        value = value + lax.ppermute(value, axis, pairs)
    return value


def per_device(density, costate, phases, displacements, table_slot, checkpoint):
    parts = lax.axis_size("grp")
    share = WIDE // parts
    chunks = max(1, min(4, share // 8))
    size = share // chunks
    seat = lax.axis_index("grp").astype(jnp.int32)
    seats = seat.reshape(1)
    rows, cols = costate.shape[1:]

    opened, turned_by, level, lane = make_weights(
        phases, displacements, table_slot, checkpoint, seats, parts, chunks
    )
    state_cut = open_state(costate, opened, parts, size, 0, 1, [])
    if chunks > 1:
        state_cut += open_state(
            costate, opened, parts, size, 1, chunks - 1, list(state_cut[0][:1])
        )
    rho = [
        cut_pieces(density, seats, parts, chunk, size, list(state_cut[-1][:1]))
        for chunk in range(chunks)
    ]
    state = [swap(pieces, parts) for pieces in state_cut]
    rho_there = [swap(pieces, parts) for pieces in rho]

    shape = (2, rows // WIDE, parts, chunks, size, cols)
    fields, closed, made, grads = [], [], [], []

    def close(chunk, waited):
        out, grad = close_columns(
            fields[chunk], rho_there[chunk], lane, level, size, waited
        )
        closed.append(out)
        made.append(swap(out, parts))
        grads.append(grad)

    for chunk in range(chunks):
        waited = [pieces[0] for pieces in rho] if chunk == 0 else []
        if chunk > 1:
            close(chunk - 2, made[chunk - 4][1:] if chunk > 3 else [])
            waited = closed[chunk - 2][:1]
        field = turn_columns(state[chunk], turned_by, size, waited)
        fields.append(lax.all_to_all(field, "dev", split_axis=0, concat_axis=0, tiled=True))
    for chunk in range(len(made), chunks):
        close(chunk, made[chunk - 2][1:] if chunk > 1 else [])
    whole = None
    for chunk in range(chunks):
        whole = place_pieces(made[chunk], seats, whole, chunk, shape, size)
    grad = grand_total(device_grad(grads, seats, parts, made[-1][2:3]))
    return whole.reshape(costate.shape), grad.reshape(2, 2, LEVELS)


def solution(mesh):
    return jax.shard_map(
        per_device,
        mesh=mesh,
        in_specs=(P(None, "dev", "grp"), P(None, "dev", "grp"), P(), P(), P(), P()),
        out_specs=(P(None, "dev", "grp"), P()),
        check_vma=False,
    )
```

```python
import functools

import jax
import jax.numpy as jnp
from jax import lax
from jax.experimental import pallas as pl
from jax.experimental.pallas import tpu as pltpu
from jax.sharding import PartitionSpec as P

LEVELS = 64
TRANSMON = 2
WIDE = LEVELS * TRANSMON
PAIR = 2 * WIDE
HIGH = lax.Precision.HIGHEST
F32 = jnp.float32
BF16 = jnp.bfloat16
SMALL = pl.CostEstimate(flops=1024, bytes_accessed=1024, transcendentals=0)
LARGE = pl.CostEstimate(flops=2 * 10**11, bytes_accessed=1024, transcendentals=0)
PARAMS = pltpu.CompilerParams(vmem_limit_bytes=48 * 1024 * 1024)


def split_value(value):
    high = value.astype(BF16)
    low = (value - high.astype(F32)).astype(BF16)
    return high, low


def mxu(left, right, dims=(((1,), (0,)), ((), ()))):
    return lax.dot_general(left, right, dims, preferred_element_type=F32)


def exact(left, right, dims=(((1,), (0,)), ((), ()))):
    return lax.dot_general(left, right, dims, precision=HIGH, preferred_element_type=F32)


def grid_of(shape, dim):
    return lax.broadcasted_iota(jnp.int32, shape, dim)


def pick_matrix(count, chosen):
    shape = (count, count)
    return (chosen(grid_of(shape, 0)) == grid_of(shape, 1)).astype(F32)


def spread(matrix):
    tall = (grid_of((WIDE, LEVELS), 0) // TRANSMON == grid_of((WIDE, LEVELS), 1)).astype(F32)
    long = (grid_of((LEVELS, WIDE), 1) // TRANSMON == grid_of((LEVELS, WIDE), 0)).astype(F32)
    same = grid_of((WIDE, WIDE), 0) % TRANSMON == grid_of((WIDE, WIDE), 1) % TRANSMON
    return jnp.where(same, exact(exact(tall, matrix), long), 0.0)


def blocks(upper_left, upper_right, lower_left, lower_right):
    return jnp.concatenate(
        [
            jnp.concatenate([upper_left, upper_right], axis=1),
            jnp.concatenate([lower_left, lower_right], axis=1),
        ],
        axis=0,
    )


def complex_product(left, right):
    return (
        exact(left[0], right[0]) - exact(left[1], right[1]),
        exact(left[0], right[1]) + exact(left[1], right[0]),
    )


def weights_kernel(parts, chunks, slot_ref, start_ref, seat_ref, *refs):
    angle_refs, matrix_refs = refs[0:2], refs[2:4]
    open_ref, turn_ref, level_ref, lane_ref = refs[-4:]
    seat = seat_ref[0]
    width = LEVELS // parts
    share = WIDE // parts
    size = share // chunks
    first, second = [], []
    for layer in range(2):
        cosine = jnp.cos(angle_refs[layer][...])
        sine = jnp.sin(angle_refs[layer][...])
        for mode, kept in enumerate((first, second)):
            turn_real, turn_imag = cosine[mode:mode + 1], sine[mode:mode + 1]
            real_part = matrix_refs[layer][mode, 0]
            imag_part = matrix_refs[layer][mode, 1]
            kept.append(
                (
                    real_part * turn_real - imag_part * turn_imag,
                    real_part * turn_imag + imag_part * turn_real,
                )
            )
    both_first = complex_product(first[1], first[0])
    both_second = complex_product(second[1], second[0])

    order = pick_matrix(
        LEVELS, lambda row: lax.bitwise_xor(row // width, seat) * width + row % width
    )

    def put_level(ref, index, real_part, imag_part):
        full = blocks(real_part, -imag_part, imag_part, real_part)
        high, low = split_value(full)
        made = blocks(high, high, low, jnp.zeros_like(low))
        if index is None:
            ref[...] = made
        else:
            ref[index] = made

    put_level(turn_ref, None, exact(both_first[0].T, order), exact(-both_first[1].T, order))
    put_level(level_ref, 0, first[1][0].T, first[1][1].T)
    put_level(level_ref, 1, exact(first[0][0], order), exact(-first[0][1], order))
    put_level(level_ref, 2, exact(order, first[0][0].T), exact(order, first[0][1].T))

    def put_lane(index, real_part, imag_part):
        real_part, imag_part = spread(real_part), spread(imag_part)
        high, low = split_value(blocks(real_part, imag_part, -imag_part, real_part))
        lane_ref[index, 0] = high
        lane_ref[index, 1] = low

    put_lane(0, *second[1])
    put_lane(1, second[0][0].T, -second[0][1].T)
    put_lane(2, *second[0])

    real_part, imag_part = spread(both_second[0].T), spread(both_second[1].T)
    full = blocks(real_part, -imag_part, -imag_part, -real_part)

    def source(row):
        chunk, rest = row // (2 * size * parts), row % (2 * size * parts)
        step, rest = rest // (2 * size), rest % (2 * size)
        half, place = rest // size, rest % size
        return half * WIDE + lax.bitwise_xor(step, seat) * share + chunk * size + place

    high, low = split_value(exact(pick_matrix(PAIR, source), full))
    open_ref[0] = high
    open_ref[1] = low


def make_weights(phases, displacements, table_slot, checkpoint, seat, parts, chunks):
    def angles(layer):
        return pl.BlockSpec(
            (None, 2, LEVELS), lambda i, slot, start, own: (slot[start[0] + layer], 0, 0)
        )

    def matrices(layer):
        return pl.BlockSpec(
            (None, 2, 2, LEVELS, LEVELS),
            lambda i, slot, start, own: (start[0] + layer, 0, 0, 0, 0),
        )

    def whole(shape):
        return pl.BlockSpec(shape, lambda i, slot, start, own: (0,) * len(shape))

    shapes = [(2, PAIR, PAIR), (PAIR, PAIR), (3, PAIR, PAIR), (3, 2, PAIR, PAIR)]
    return pl.pallas_call(
        functools.partial(weights_kernel, parts, chunks),
        grid_spec=pltpu.PrefetchScalarGridSpec(
            num_scalar_prefetch=3,
            grid=(1,),
            in_specs=[angles(0), angles(1), matrices(0), matrices(1)],
            out_specs=[whole(shape) for shape in shapes],
        ),
        out_shape=[jax.ShapeDtypeStruct(shape, BF16) for shape in shapes],
        compiler_params=PARAMS,
        cost_estimate=SMALL,
    )(table_slot, checkpoint, seat, phases, phases, displacements, displacements)


def open_kernel(count, waited, weight_ref, field_ref, *refs):
    both = jnp.concatenate([field_ref[0], field_ref[1]], axis=1)
    high, low = split_value(both)
    across = (((1,), (1,)), ((), ()))
    made = mxu(weight_ref[0], high, across) + (
        mxu(weight_ref[0], low, across) + mxu(weight_ref[1], high, across)
    )
    tall = made.shape[0] // count
    for place, out in enumerate(refs[waited:]):
        piece = made[place * tall:(place + 1) * tall]
        for first in range(out.shape[0]):
            out[first] = piece[:, first * WIDE:(first + 1) * WIDE]


def open_state(field, weights, parts, size, chunk_start, chunk_count, waited):
    rows, cols = field.shape[1:]
    firsts = rows // WIDE
    column_levels = cols // WIDE
    count = parts * chunk_count
    tall = count * 2 * size
    shape = jax.ShapeDtypeStruct((firsts, column_levels * 2 * size, WIDE), F32)
    weights = lax.slice_in_dim(
        weights, chunk_start * parts * 2 * size, chunk_start * parts * 2 * size + tall, axis=1
    )
    outs = pl.pallas_call(
        functools.partial(open_kernel, count, len(waited)),
        grid=(column_levels,),
        in_specs=[
            pl.BlockSpec((2, tall, PAIR), lambda i: (0, 0, 0)),
            pl.BlockSpec((2, rows, WIDE), lambda i: (0, 0, i)),
        ]
        + [pl.BlockSpec(memory_space=pl.ANY)] * len(waited),
        out_specs=[pl.BlockSpec((firsts, 2 * size, WIDE), lambda i: (0, i, 0))] * count,
        out_shape=[shape] * count,
        compiler_params=PARAMS,
        cost_estimate=SMALL,
    )(weights, field, *waited)
    return [outs[c * parts:(c + 1) * parts] for c in range(chunk_count)]


def cut_kernel(size, waited, seat_ref, field_ref, *refs):
    seat = seat_ref[0]
    levels = field_ref.shape[-1] // WIDE
    for step, out in enumerate(refs[waited:]):
        part = lax.bitwise_xor(seat, step)
        for half in range(2):
            for level in range(levels):
                start = (2 * level + half) * size
                out[start:start + size, :] = field_ref[
                    half, part, :, level * WIDE:(level + 1) * WIDE
                ]


def cut_pieces(field, seat, parts, chunk, size, waited):
    rows, cols = field.shape[1:]
    firsts = rows // WIDE
    chunks = WIDE // parts // size
    tall = cols // WIDE * 2 * size
    return pl.pallas_call(
        functools.partial(cut_kernel, size, len(waited)),
        grid=(firsts,),
        in_specs=[
            pl.BlockSpec(memory_space=pltpu.SMEM),
            pl.BlockSpec((2, None, parts, None, size, cols), lambda i: (0, i, 0, chunk, 0, 0)),
        ]
        + [pl.BlockSpec(memory_space=pl.ANY)] * len(waited),
        out_specs=[pl.BlockSpec((None, tall, WIDE), lambda i: (i, 0, 0))] * parts,
        out_shape=[jax.ShapeDtypeStruct((firsts, tall, WIDE), F32)] * parts,
        compiler_params=PARAMS,
        cost_estimate=SMALL,
    )(seat, field.reshape(2, firsts, parts, chunks, size, cols), *waited)


def level_apply(weights, real_part, imag_part):
    real_high, real_low = split_value(real_part)
    imag_high, imag_low = split_value(imag_part)
    stacked = jnp.concatenate([real_high, imag_high, real_low, imag_low], axis=0)
    made = mxu(weights, stacked)
    return made[:WIDE] + made[WIDE:]


def lane_apply(weight_ref, index, real_part, imag_part):
    high, low = split_value(jnp.concatenate([real_part, imag_part], axis=1))
    made = mxu(high, weight_ref[index, 0]) + (
        mxu(low, weight_ref[index, 0]) + mxu(high, weight_ref[index, 1])
    )
    return made[:, :WIDE], made[:, WIDE:]


def gather_levels(refs, size, half):
    columns = []
    for place in range(size):
        parts = [
            ref[pl.ds(half * size + place, ref.shape[0] // (2 * size), stride=2 * size), :]
            for ref in refs
        ]
        columns.append(jnp.concatenate(parts, axis=0) if len(parts) > 1 else parts[0])
    return jnp.concatenate(columns, axis=1)


def scatter_levels(ref, size, half, value):
    for place in range(size):
        ref[pl.ds(half * size + place, LEVELS, stride=2 * size), :] = value[
            :, place * WIDE:(place + 1) * WIDE
        ]


def turn_kernel(parts, size, weight_ref, *refs):
    pieces = refs[:parts]
    out_ref = refs[-1].reshape(LEVELS * 2 * size, WIDE)
    made = level_apply(
        weight_ref[...], gather_levels(pieces, size, 0), gather_levels(pieces, size, 1)
    )
    scatter_levels(out_ref, size, 0, made[:LEVELS])
    scatter_levels(out_ref, size, 1, made[LEVELS:])


def turn_columns(pieces, weights, size, waited):
    firsts = pieces[0].shape[0]
    parts = len(pieces)
    block = pieces[0].shape[1:]
    return pl.pallas_call(
        functools.partial(turn_kernel, parts, size),
        grid=(firsts,),
        in_specs=[pl.BlockSpec((PAIR, PAIR), lambda i: (0, 0))]
        + [pl.BlockSpec((None,) + block, lambda i: (i, 0, 0))] * parts
        + [pl.BlockSpec(memory_space=pl.ANY)] * len(waited),
        out_specs=pl.BlockSpec((LEVELS, None, 2 * size, WIDE), lambda i: (0, i, 0, 0)),
        out_shape=jax.ShapeDtypeStruct((LEVELS, firsts, 2 * size, WIDE), F32),
        compiler_params=PARAMS,
        cost_estimate=SMALL,
    )(weights, *pieces, *waited)


def halves(value, size):
    value = value.reshape(LEVELS, 2, size, WIDE)
    rows = LEVELS * size
    return value[:, 0].reshape(rows, WIDE), value[:, 1].reshape(rows, WIDE)


def join(real_part, imag_part, size):
    shape = (LEVELS, 1, size, WIDE)
    both = jnp.concatenate([real_part.reshape(shape), imag_part.reshape(shape)], axis=1)
    return both.reshape(LEVELS * 2 * size, WIDE)


def close_kernel(parts, size, lane_ref, level_ref, field_ref, *refs):
    rho_refs = refs[:parts]
    out_refs = refs[-parts - 3:-3]
    grad_ref, work_a, work_b = refs[-3:]
    step = pl.program_id(0)

    @pl.when(step == 0)
    def _():
        grad_ref[...] = jnp.zeros_like(grad_ref)

    flat = field_ref.reshape(LEVELS * 2 * size, WIDE)
    real_part, imag_part = lane_apply(lane_ref, 0, *halves(flat[...], size))
    work_a[...] = join(real_part, imag_part, size)

    rho = jnp.concatenate([ref[...] for ref in rho_refs], axis=0)
    rho_real, rho_imag = halves(rho, size)
    real_part, imag_part = lane_apply(lane_ref, 1, rho_real, rho_imag)
    work_b[...] = join(real_part, imag_part, size)

    mid = level_apply(level_ref[0], gather_levels([work_a], size, 0), gather_levels([work_a], size, 1))
    seen = level_apply(level_ref[1], gather_levels([work_b], size, 0), gather_levels([work_b], size, 1))
    terms = seen[:LEVELS] * mid[LEVELS:] - seen[LEVELS:] * mid[:LEVELS]
    total = terms[:, :WIDE]
    for place in range(1, size):
        total = total + terms[:, place * WIDE:(place + 1) * WIDE]
    grad_ref[1] += total

    last = level_apply(level_ref[2], mid[:LEVELS], mid[LEVELS:])
    scatter_levels(work_a, size, 0, last[:LEVELS])
    scatter_levels(work_a, size, 1, last[LEVELS:])
    real_part, imag_part = lane_apply(lane_ref, 2, *halves(work_a[...], size))
    terms = rho_real * imag_part - rho_imag * real_part
    grad_ref[0] += jnp.sum(terms.reshape(LEVELS, size, WIDE), axis=1)
    made = join(real_part, imag_part, size)
    rows = made.shape[0] // parts
    for part in range(parts):
        out_refs[part][...] = made[part * rows:(part + 1) * rows]


def close_columns(field, rho_pieces, lane, level, size, waited):
    total_first, firsts = field.shape[:2]
    devs = total_first // firsts
    parts = len(rho_pieces)
    rows = LEVELS * 2 * size
    field = field.reshape(devs, firsts, firsts * 2 * size, WIDE)
    piece = rho_pieces[0]
    piece_spec = pl.BlockSpec((None,) + piece.shape[1:], lambda i: (i, 0, 0))
    outs = pl.pallas_call(
        functools.partial(close_kernel, parts, size),
        grid=(firsts,),
        in_specs=[
            pl.BlockSpec(lane.shape, lambda i: (0, 0, 0, 0)),
            pl.BlockSpec(level.shape, lambda i: (0, 0, 0)),
            pl.BlockSpec((devs, None, firsts * 2 * size, WIDE), lambda i: (0, i, 0, 0)),
        ]
        + [piece_spec] * parts
        + [pl.BlockSpec(memory_space=pl.ANY)] * len(waited),
        out_specs=[piece_spec] * parts + [pl.BlockSpec((2, LEVELS, WIDE), lambda i: (0, 0, 0))],
        out_shape=[jax.ShapeDtypeStruct(piece.shape, F32)] * parts
        + [jax.ShapeDtypeStruct((2, LEVELS, WIDE), F32)],
        scratch_shapes=[pltpu.VMEM((rows, WIDE), F32), pltpu.VMEM((rows, WIDE), F32)],
        compiler_params=PARAMS,
        cost_estimate=LARGE,
    )(lane, level, field, *rho_pieces, *waited)
    return list(outs[:parts]), outs[parts]


def place_kernel(parts, size, aliased, seat_ref, *refs):
    pieces = refs[:parts]
    out_ref = refs[parts + aliased]
    seat = seat_ref[0]
    levels = pieces[0].shape[0] // (2 * size)
    for step in range(parts):
        part = lax.bitwise_xor(seat, step)
        for half in range(2):
            for level in range(levels):
                start = level * 2 * size + half * size
                out_ref[half, part, :, level * WIDE:(level + 1) * WIDE] = pieces[step][
                    start:start + size, :
                ]


def place_pieces(pieces, seat, held, chunk, shape, size):
    parts = len(pieces)
    firsts, chunks = shape[1], shape[3]
    aliased = 0 if held is None else 1
    piece = pieces[0]
    cols = shape[-1]
    return pl.pallas_call(
        functools.partial(place_kernel, parts, size, aliased),
        grid=(firsts,),
        in_specs=[pl.BlockSpec(memory_space=pltpu.SMEM)]
        + [pl.BlockSpec((None,) + piece.shape[1:], lambda i: (i, 0, 0))] * parts
        + [pl.BlockSpec(memory_space=pl.ANY)] * aliased,
        out_specs=pl.BlockSpec(
            (2, None, parts, None, size, cols), lambda i: (0, i, 0, chunk, 0, 0)
        ),
        out_shape=jax.ShapeDtypeStruct(shape, F32),
        input_output_aliases={parts + 1: 0} if aliased else {},
        compiler_params=PARAMS,
        cost_estimate=SMALL,
    )(seat, *pieces, *([held] if aliased else []))


def swap(pieces, parts):
    moved = [pieces[0]]
    for step in range(1, parts):
        pairs = [(member, member ^ step) for member in range(parts)]
        moved.append(lax.ppermute(pieces[step], "grp", pairs))
    return moved


def grad_kernel(parts, count, seat_ref, *refs):
    out_ref = refs[-1]
    grad = refs[0][...]
    for ref in refs[1:count]:
        grad = grad + ref[...]
    grad = -2.0 * grad
    width = LEVELS // parts
    order = pick_matrix(
        LEVELS, lambda row: lax.bitwise_xor(row // width, seat_ref[0]) * width + row % width
    )
    fold = (grid_of((WIDE, LEVELS), 0) // TRANSMON == grid_of((WIDE, LEVELS), 1)).astype(F32)
    for layer in range(2):
        firsts = exact(jnp.ones((8, WIDE), F32), grad[layer], (((1,), (1,)), ((), ())))
        if layer == 0:
            firsts = exact(firsts, order)
        seconds = exact(exact(jnp.ones((8, LEVELS), F32), grad[layer]), fold)
        out_ref[2 * layer:2 * layer + 1, :] = firsts[:1]
        out_ref[2 * layer + 1:2 * layer + 2, :] = seconds[:1]


def device_grad(grads, seat, parts, waited):
    return pl.pallas_call(
        functools.partial(grad_kernel, parts, len(grads)),
        in_specs=[pl.BlockSpec(memory_space=pltpu.SMEM)]
        + [pl.BlockSpec(memory_space=pltpu.VMEM)] * len(grads)
        + [pl.BlockSpec(memory_space=pl.ANY)] * len(waited),
        out_specs=pl.BlockSpec(memory_space=pltpu.VMEM),
        out_shape=jax.ShapeDtypeStruct((4, LEVELS), F32),
        compiler_params=PARAMS,
        cost_estimate=SMALL,
    )(seat, *grads, *waited)


def grand_total(value):
    rounds = []
    for axis in ("grp", "dev"):
        count = lax.axis_size(axis)
        rounds.append([(axis, 1 << bit, count) for bit in range(count.bit_length() - 1)])
    for axis, step, count in rounds[0][:1] + rounds[1] + rounds[0][1:]:
        pairs = [(member, member ^ step) for member in range(count)]
        value = value + lax.ppermute(value, axis, pairs)
    return value


def per_device(density, costate, phases, displacements, table_slot, checkpoint):
    parts = lax.axis_size("grp")
    share = WIDE // parts
    chunks = max(1, min(4, share // 8))
    size = share // chunks
    seat = lax.axis_index("grp").astype(jnp.int32)
    seats = seat.reshape(1)
    rows, cols = costate.shape[1:]

    opened, turned_by, level, lane = make_weights(
        phases, displacements, table_slot, checkpoint, seats, parts, chunks
    )
    state_cut = open_state(costate, opened, parts, size, 0, 1, [])
    if chunks > 1:
        state_cut += open_state(
            costate, opened, parts, size, 1, chunks - 1, list(state_cut[0][:1])
        )
    rho = [
        cut_pieces(density, seats, parts, chunk, size, list(state_cut[-1][:1]))
        for chunk in range(chunks)
    ]
    state = [swap(pieces, parts) for pieces in state_cut]
    rho_there = [swap(pieces, parts) for pieces in rho]

    shape = (2, rows // WIDE, parts, chunks, size, cols)
    fields, closed, made, grads = [], [], [], []

    def close(chunk):
        waited = closed[chunk - 1][:1] if chunk > 0 else []
        waited = waited + (list(made[chunk - 2][1:]) if chunk > 1 else [])
        out, grad = close_columns(
            fields[chunk], rho_there[chunk], lane, level, size, waited
        )
        closed.append(out)
        made.append(swap(out, parts))
        grads.append(grad)

    for chunk in range(chunks):
        waited = [pieces[0] for pieces in rho] if chunk == 0 else [field]
        if chunk > 1:
            close(chunk - 2)
            waited = waited + closed[chunk - 2][:1]
        field = turn_columns(state[chunk], turned_by, size, waited)
        fields.append(lax.all_to_all(field, "dev", split_axis=0, concat_axis=0, tiled=True))
    for chunk in range(len(made), chunks):
        close(chunk)
    whole = None
    for chunk in range(chunks):
        whole = place_pieces(made[chunk], seats, whole, chunk, shape, size)
    grad = grand_total(device_grad(grads, seats, parts, made[-1][2:3]))
    return whole.reshape(costate.shape), grad.reshape(2, 2, LEVELS)


def solution(mesh):
    return jax.shard_map(
        per_device,
        mesh=mesh,
        in_specs=(P(None, "dev", "grp"), P(None, "dev", "grp"), P(), P(), P(), P()),
        out_specs=(P(None, "dev", "grp"), P()),
        check_vma=False,
    )
```

```python
import functools

import jax
import jax.numpy as jnp
from jax import lax
from jax.experimental import pallas as pl
from jax.experimental.pallas import tpu as pltpu
from jax.sharding import PartitionSpec as P

LEVELS = 64
TRANSMON = 2
WIDE = LEVELS * TRANSMON
PAIR = 2 * WIDE
HIGH = lax.Precision.HIGHEST
F32 = jnp.float32
BF16 = jnp.bfloat16
SMALL = pl.CostEstimate(flops=1024, bytes_accessed=1024, transcendentals=0)
LARGE = pl.CostEstimate(flops=2 * 10**11, bytes_accessed=1024, transcendentals=0)
PARAMS = pltpu.CompilerParams(vmem_limit_bytes=48 * 1024 * 1024)


def split_value(value):
    high = value.astype(BF16)
    low = (value - high.astype(F32)).astype(BF16)
    return high, low


def mxu(left, right, dims=(((1,), (0,)), ((), ()))):
    return lax.dot_general(left, right, dims, preferred_element_type=F32)


def exact(left, right, dims=(((1,), (0,)), ((), ()))):
    return lax.dot_general(left, right, dims, precision=HIGH, preferred_element_type=F32)


def grid_of(shape, dim):
    return lax.broadcasted_iota(jnp.int32, shape, dim)


def pick_matrix(count, chosen):
    shape = (count, count)
    return (chosen(grid_of(shape, 0)) == grid_of(shape, 1)).astype(F32)


def spread(matrix):
    tall = (grid_of((WIDE, LEVELS), 0) // TRANSMON == grid_of((WIDE, LEVELS), 1)).astype(F32)
    long = (grid_of((LEVELS, WIDE), 1) // TRANSMON == grid_of((LEVELS, WIDE), 0)).astype(F32)
    same = grid_of((WIDE, WIDE), 0) % TRANSMON == grid_of((WIDE, WIDE), 1) % TRANSMON
    return jnp.where(same, exact(exact(tall, matrix), long), 0.0)


def blocks(upper_left, upper_right, lower_left, lower_right):
    return jnp.concatenate(
        [
            jnp.concatenate([upper_left, upper_right], axis=1),
            jnp.concatenate([lower_left, lower_right], axis=1),
        ],
        axis=0,
    )


def complex_product(left, right):
    return (
        exact(left[0], right[0]) - exact(left[1], right[1]),
        exact(left[0], right[1]) + exact(left[1], right[0]),
    )


def weights_kernel(parts, chunks, slot_ref, start_ref, seat_ref, *refs):
    angle_refs, matrix_refs = refs[0:2], refs[2:4]
    open_ref, turn_ref, level_ref, lane_ref = refs[-4:]
    seat = seat_ref[0]
    width = LEVELS // parts
    share = WIDE // parts
    size = share // chunks
    first, second = [], []
    for layer in range(2):
        cosine = jnp.cos(angle_refs[layer][...])
        sine = jnp.sin(angle_refs[layer][...])
        for mode, kept in enumerate((first, second)):
            turn_real, turn_imag = cosine[mode:mode + 1], sine[mode:mode + 1]
            real_part = matrix_refs[layer][mode, 0]
            imag_part = matrix_refs[layer][mode, 1]
            kept.append(
                (
                    real_part * turn_real - imag_part * turn_imag,
                    real_part * turn_imag + imag_part * turn_real,
                )
            )
    both_first = complex_product(first[1], first[0])
    both_second = complex_product(second[1], second[0])

    order = pick_matrix(
        LEVELS, lambda row: lax.bitwise_xor(row // width, seat) * width + row % width
    )

    def put_level(ref, index, real_part, imag_part):
        full = blocks(real_part, -imag_part, imag_part, real_part)
        high, low = split_value(full)
        made = blocks(high, high, low, jnp.zeros_like(low))
        if index is None:
            ref[...] = made
        else:
            ref[index] = made

    put_level(turn_ref, None, exact(both_first[0].T, order), exact(-both_first[1].T, order))
    put_level(level_ref, 0, first[1][0].T, first[1][1].T)
    put_level(level_ref, 1, exact(first[0][0], order), exact(-first[0][1], order))
    put_level(level_ref, 2, exact(order, first[0][0].T), exact(order, first[0][1].T))

    def put_lane(index, real_part, imag_part):
        real_part, imag_part = spread(real_part), spread(imag_part)
        high, low = split_value(blocks(real_part, imag_part, -imag_part, real_part))
        lane_ref[index, 0] = high
        lane_ref[index, 1] = low

    put_lane(0, *second[1])
    put_lane(1, second[0][0].T, -second[0][1].T)
    put_lane(2, *second[0])

    real_part, imag_part = spread(both_second[0].T), spread(both_second[1].T)
    full = blocks(real_part, -imag_part, -imag_part, -real_part)

    def source(row):
        chunk, rest = row // (2 * size * parts), row % (2 * size * parts)
        step, rest = rest // (2 * size), rest % (2 * size)
        half, place = rest // size, rest % size
        return half * WIDE + lax.bitwise_xor(step, seat) * share + chunk * size + place

    high, low = split_value(exact(pick_matrix(PAIR, source), full))
    open_ref[0] = high
    open_ref[1] = low


def make_weights(phases, displacements, table_slot, checkpoint, seat, parts, chunks):
    def angles(layer):
        return pl.BlockSpec(
            (None, 2, LEVELS), lambda i, slot, start, own: (slot[start[0] + layer], 0, 0)
        )

    def matrices(layer):
        return pl.BlockSpec(
            (None, 2, 2, LEVELS, LEVELS),
            lambda i, slot, start, own: (start[0] + layer, 0, 0, 0, 0),
        )

    def whole(shape):
        return pl.BlockSpec(shape, lambda i, slot, start, own: (0,) * len(shape))

    shapes = [(2, PAIR, PAIR), (PAIR, PAIR), (3, PAIR, PAIR), (3, 2, PAIR, PAIR)]
    return pl.pallas_call(
        functools.partial(weights_kernel, parts, chunks),
        grid_spec=pltpu.PrefetchScalarGridSpec(
            num_scalar_prefetch=3,
            grid=(1,),
            in_specs=[angles(0), angles(1), matrices(0), matrices(1)],
            out_specs=[whole(shape) for shape in shapes],
        ),
        out_shape=[jax.ShapeDtypeStruct(shape, BF16) for shape in shapes],
        compiler_params=PARAMS,
        cost_estimate=SMALL,
    )(table_slot, checkpoint, seat, phases, phases, displacements, displacements)


def open_kernel(count, waited, weight_ref, field_ref, *refs):
    both = jnp.concatenate([field_ref[0], field_ref[1]], axis=1)
    high, low = split_value(both)
    across = (((1,), (1,)), ((), ()))
    made = mxu(weight_ref[0], high, across) + (
        mxu(weight_ref[0], low, across) + mxu(weight_ref[1], high, across)
    )
    tall = made.shape[0] // count
    for place, out in enumerate(refs[waited:]):
        piece = made[place * tall:(place + 1) * tall]
        for first in range(out.shape[0]):
            out[first] = piece[:, first * WIDE:(first + 1) * WIDE]


def open_state(field, weights, parts, size, chunk_start, chunk_count, waited):
    rows, cols = field.shape[1:]
    firsts = rows // WIDE
    column_levels = cols // WIDE
    count = parts * chunk_count
    tall = count * 2 * size
    shape = jax.ShapeDtypeStruct((firsts, column_levels * 2 * size, WIDE), F32)
    weights = lax.slice_in_dim(
        weights, chunk_start * parts * 2 * size, chunk_start * parts * 2 * size + tall, axis=1
    )
    outs = pl.pallas_call(
        functools.partial(open_kernel, count, len(waited)),
        grid=(column_levels,),
        in_specs=[
            pl.BlockSpec((2, tall, PAIR), lambda i: (0, 0, 0)),
            pl.BlockSpec((2, rows, WIDE), lambda i: (0, 0, i)),
        ]
        + [pl.BlockSpec(memory_space=pl.ANY)] * len(waited),
        out_specs=[pl.BlockSpec((firsts, 2 * size, WIDE), lambda i: (0, i, 0))] * count,
        out_shape=[shape] * count,
        compiler_params=PARAMS,
        cost_estimate=SMALL,
    )(weights, field, *waited)
    return [outs[c * parts:(c + 1) * parts] for c in range(chunk_count)]


def cut_kernel(size, waited, seat_ref, field_ref, *refs):
    seat = seat_ref[0]
    levels = field_ref.shape[-1] // WIDE
    for step, out in enumerate(refs[waited:]):
        part = lax.bitwise_xor(seat, step)
        for half in range(2):
            for level in range(levels):
                start = (2 * level + half) * size
                out[start:start + size, :] = field_ref[
                    half, part, :, level * WIDE:(level + 1) * WIDE
                ]


def cut_pieces(field, seat, parts, chunk, size, waited):
    rows, cols = field.shape[1:]
    firsts = rows // WIDE
    chunks = WIDE // parts // size
    tall = cols // WIDE * 2 * size
    return pl.pallas_call(
        functools.partial(cut_kernel, size, len(waited)),
        grid=(firsts,),
        in_specs=[
            pl.BlockSpec(memory_space=pltpu.SMEM),
            pl.BlockSpec((2, None, parts, None, size, cols), lambda i: (0, i, 0, chunk, 0, 0)),
        ]
        + [pl.BlockSpec(memory_space=pl.ANY)] * len(waited),
        out_specs=[pl.BlockSpec((None, tall, WIDE), lambda i: (i, 0, 0))] * parts,
        out_shape=[jax.ShapeDtypeStruct((firsts, tall, WIDE), F32)] * parts,
        compiler_params=PARAMS,
        cost_estimate=SMALL,
    )(seat, field.reshape(2, firsts, parts, chunks, size, cols), *waited)


def level_apply(weights, real_part, imag_part):
    real_high, real_low = split_value(real_part)
    imag_high, imag_low = split_value(imag_part)
    stacked = jnp.concatenate([real_high, imag_high, real_low, imag_low], axis=0)
    made = mxu(weights, stacked)
    return made[:WIDE] + made[WIDE:]


def lane_apply(weight_ref, index, real_part, imag_part):
    high, low = split_value(jnp.concatenate([real_part, imag_part], axis=1))
    made = mxu(high, weight_ref[index, 0]) + (
        mxu(low, weight_ref[index, 0]) + mxu(high, weight_ref[index, 1])
    )
    return made[:, :WIDE], made[:, WIDE:]


def gather_levels(refs, size, half):
    columns = []
    for place in range(size):
        parts = [
            ref[pl.ds(half * size + place, ref.shape[0] // (2 * size), stride=2 * size), :]
            for ref in refs
        ]
        columns.append(jnp.concatenate(parts, axis=0) if len(parts) > 1 else parts[0])
    return jnp.concatenate(columns, axis=1)


def scatter_levels(ref, size, half, value):
    for place in range(size):
        ref[pl.ds(half * size + place, LEVELS, stride=2 * size), :] = value[
            :, place * WIDE:(place + 1) * WIDE
        ]


def turn_kernel(parts, size, weight_ref, *refs):
    pieces = refs[:parts]
    out_ref = refs[-1].reshape(LEVELS * 2 * size, WIDE)
    made = level_apply(
        weight_ref[...], gather_levels(pieces, size, 0), gather_levels(pieces, size, 1)
    )
    scatter_levels(out_ref, size, 0, made[:LEVELS])
    scatter_levels(out_ref, size, 1, made[LEVELS:])


def turn_columns(pieces, weights, size, waited):
    firsts = pieces[0].shape[0]
    parts = len(pieces)
    block = pieces[0].shape[1:]
    return pl.pallas_call(
        functools.partial(turn_kernel, parts, size),
        grid=(firsts,),
        in_specs=[pl.BlockSpec((PAIR, PAIR), lambda i: (0, 0))]
        + [pl.BlockSpec((None,) + block, lambda i: (i, 0, 0))] * parts
        + [pl.BlockSpec(memory_space=pl.ANY)] * len(waited),
        out_specs=pl.BlockSpec((LEVELS, None, 2 * size, WIDE), lambda i: (0, i, 0, 0)),
        out_shape=jax.ShapeDtypeStruct((LEVELS, firsts, 2 * size, WIDE), F32),
        compiler_params=PARAMS,
        cost_estimate=SMALL,
    )(weights, *pieces, *waited)


def halves(value, size):
    value = value.reshape(LEVELS, 2, size, WIDE)
    rows = LEVELS * size
    return value[:, 0].reshape(rows, WIDE), value[:, 1].reshape(rows, WIDE)


def join(real_part, imag_part, size):
    shape = (LEVELS, 1, size, WIDE)
    both = jnp.concatenate([real_part.reshape(shape), imag_part.reshape(shape)], axis=1)
    return both.reshape(LEVELS * 2 * size, WIDE)


def close_kernel(parts, size, lane_ref, level_ref, field_ref, *refs):
    rho_refs = refs[:parts]
    out_refs = refs[-parts - 3:-3]
    grad_ref, work_a, work_b = refs[-3:]
    step = pl.program_id(0)

    @pl.when(step == 0)
    def _():
        grad_ref[...] = jnp.zeros_like(grad_ref)

    flat = field_ref.reshape(LEVELS * 2 * size, WIDE)
    real_part, imag_part = lane_apply(lane_ref, 0, *halves(flat[...], size))
    work_a[...] = join(real_part, imag_part, size)

    rho = jnp.concatenate([ref[...] for ref in rho_refs], axis=0)
    rho_real, rho_imag = halves(rho, size)
    real_part, imag_part = lane_apply(lane_ref, 1, rho_real, rho_imag)
    work_b[...] = join(real_part, imag_part, size)

    mid = level_apply(level_ref[0], gather_levels([work_a], size, 0), gather_levels([work_a], size, 1))
    seen = level_apply(level_ref[1], gather_levels([work_b], size, 0), gather_levels([work_b], size, 1))
    terms = seen[:LEVELS] * mid[LEVELS:] - seen[LEVELS:] * mid[:LEVELS]
    total = terms[:, :WIDE]
    for place in range(1, size):
        total = total + terms[:, place * WIDE:(place + 1) * WIDE]
    grad_ref[1] += total

    last = level_apply(level_ref[2], mid[:LEVELS], mid[LEVELS:])
    scatter_levels(work_a, size, 0, last[:LEVELS])
    scatter_levels(work_a, size, 1, last[LEVELS:])
    real_part, imag_part = lane_apply(lane_ref, 2, *halves(work_a[...], size))
    terms = rho_real * imag_part - rho_imag * real_part
    grad_ref[0] += jnp.sum(terms.reshape(LEVELS, size, WIDE), axis=1)
    made = join(real_part, imag_part, size)
    rows = made.shape[0] // parts
    for part in range(parts):
        out_refs[part][...] = made[part * rows:(part + 1) * rows]


def close_columns(field, rho_pieces, lane, level, size, waited):
    total_first, firsts = field.shape[:2]
    devs = total_first // firsts
    parts = len(rho_pieces)
    rows = LEVELS * 2 * size
    field = field.reshape(devs, firsts, firsts * 2 * size, WIDE)
    piece = rho_pieces[0]
    piece_spec = pl.BlockSpec((None,) + piece.shape[1:], lambda i: (i, 0, 0))
    outs = pl.pallas_call(
        functools.partial(close_kernel, parts, size),
        grid=(firsts,),
        in_specs=[
            pl.BlockSpec(lane.shape, lambda i: (0, 0, 0, 0)),
            pl.BlockSpec(level.shape, lambda i: (0, 0, 0)),
            pl.BlockSpec((devs, None, firsts * 2 * size, WIDE), lambda i: (0, i, 0, 0)),
        ]
        + [piece_spec] * parts
        + [pl.BlockSpec(memory_space=pl.ANY)] * len(waited),
        out_specs=[piece_spec] * parts + [pl.BlockSpec((2, LEVELS, WIDE), lambda i: (0, 0, 0))],
        out_shape=[jax.ShapeDtypeStruct(piece.shape, F32)] * parts
        + [jax.ShapeDtypeStruct((2, LEVELS, WIDE), F32)],
        scratch_shapes=[pltpu.VMEM((rows, WIDE), F32), pltpu.VMEM((rows, WIDE), F32)],
        compiler_params=PARAMS,
        cost_estimate=LARGE,
    )(lane, level, field, *rho_pieces, *waited)
    return list(outs[:parts]), outs[parts]


def place_kernel(parts, size, aliased, seat_ref, *refs):
    pieces = refs[:parts]
    out_ref = refs[parts + aliased]
    seat = seat_ref[0]
    levels = pieces[0].shape[0] // (2 * size)
    for step in range(parts):
        part = lax.bitwise_xor(seat, step)
        for half in range(2):
            for level in range(levels):
                start = level * 2 * size + half * size
                out_ref[half, part, :, level * WIDE:(level + 1) * WIDE] = pieces[step][
                    start:start + size, :
                ]


def place_pieces(pieces, seat, held, chunk, shape, size):
    parts = len(pieces)
    firsts, chunks = shape[1], shape[3]
    aliased = 0 if held is None else 1
    piece = pieces[0]
    cols = shape[-1]
    return pl.pallas_call(
        functools.partial(place_kernel, parts, size, aliased),
        grid=(firsts,),
        in_specs=[pl.BlockSpec(memory_space=pltpu.SMEM)]
        + [pl.BlockSpec((None,) + piece.shape[1:], lambda i: (i, 0, 0))] * parts
        + [pl.BlockSpec(memory_space=pl.ANY)] * aliased,
        out_specs=pl.BlockSpec(
            (2, None, parts, None, size, cols), lambda i: (0, i, 0, chunk, 0, 0)
        ),
        out_shape=jax.ShapeDtypeStruct(shape, F32),
        input_output_aliases={parts + 1: 0} if aliased else {},
        compiler_params=PARAMS,
        cost_estimate=SMALL,
    )(seat, *pieces, *([held] if aliased else []))


def swap(pieces, parts):
    moved = [pieces[0]]
    for step in range(1, parts):
        pairs = [(member, member ^ step) for member in range(parts)]
        moved.append(lax.ppermute(pieces[step], "grp", pairs))
    return moved


def grad_kernel(parts, count, seat_ref, *refs):
    out_ref = refs[-1]
    grad = refs[0][...]
    for ref in refs[1:count]:
        grad = grad + ref[...]
    grad = -2.0 * grad
    width = LEVELS // parts
    order = pick_matrix(
        LEVELS, lambda row: lax.bitwise_xor(row // width, seat_ref[0]) * width + row % width
    )
    fold = (grid_of((WIDE, LEVELS), 0) // TRANSMON == grid_of((WIDE, LEVELS), 1)).astype(F32)
    for layer in range(2):
        firsts = exact(jnp.ones((8, WIDE), F32), grad[layer], (((1,), (1,)), ((), ())))
        if layer == 0:
            firsts = exact(firsts, order)
        seconds = exact(exact(jnp.ones((8, LEVELS), F32), grad[layer]), fold)
        out_ref[2 * layer:2 * layer + 1, :] = firsts[:1]
        out_ref[2 * layer + 1:2 * layer + 2, :] = seconds[:1]


def device_grad(grads, seat, parts, waited):
    return pl.pallas_call(
        functools.partial(grad_kernel, parts, len(grads)),
        in_specs=[pl.BlockSpec(memory_space=pltpu.SMEM)]
        + [pl.BlockSpec(memory_space=pltpu.VMEM)] * len(grads)
        + [pl.BlockSpec(memory_space=pl.ANY)] * len(waited),
        out_specs=pl.BlockSpec(memory_space=pltpu.VMEM),
        out_shape=jax.ShapeDtypeStruct((4, LEVELS), F32),
        compiler_params=PARAMS,
        cost_estimate=SMALL,
    )(seat, *grads, *waited)


def grand_total(value):
    rounds = []
    for axis in ("grp", "dev"):
        count = lax.axis_size(axis)
        rounds.append([(axis, 1 << bit, count) for bit in range(count.bit_length() - 1)])
    for axis, step, count in rounds[0][:1] + rounds[1] + rounds[0][1:]:
        pairs = [(member, member ^ step) for member in range(count)]
        value = value + lax.ppermute(value, axis, pairs)
    return value


def per_device(density, costate, phases, displacements, table_slot, checkpoint):
    parts = lax.axis_size("grp")
    share = WIDE // parts
    chunks = max(1, min(4, share // 8))
    size = share // chunks
    seat = lax.axis_index("grp").astype(jnp.int32)
    seats = seat.reshape(1)
    rows, cols = costate.shape[1:]

    opened, turned_by, level, lane = make_weights(
        phases, displacements, table_slot, checkpoint, seats, parts, chunks
    )
    state_cut = open_state(costate, opened, parts, size, 0, 1, [])
    if chunks > 1:
        state_cut += open_state(
            costate, opened, parts, size, 1, chunks - 1, list(state_cut[0][:1])
        )
    rho = [
        cut_pieces(density, seats, parts, chunk, size, list(state_cut[-1][:1]))
        for chunk in range(chunks)
    ]
    state = [swap(pieces, parts) for pieces in state_cut[:2]]
    rho_there = [swap(pieces, parts) for pieces in rho]

    shape = (2, rows // WIDE, parts, chunks, size, cols)
    fields, closed, made, grads = [], [], [], []

    def close(chunk):
        waited = closed[chunk - 1][:1] if chunk > 0 else []
        if chunk == chunks - 1 and chunk > 0:
            waited = waited + list(made[chunk - 1][1:])
        elif chunk > 1:
            waited = waited + list(made[chunk - 2][1:])
        out, grad = close_columns(
            fields[chunk], rho_there[chunk], lane, level, size, waited
        )
        closed.append(out)
        made.append(swap(out, parts))
        grads.append(grad)

    for chunk in range(chunks):
        waited = [pieces[0] for pieces in rho] if chunk == 0 else [field]
        if chunk > 1:
            close(chunk - 2)
            waited = waited + closed[chunk - 2][:1]
        field = turn_columns(state[chunk], turned_by, size, waited)
        fields.append(lax.all_to_all(field, "dev", split_axis=0, concat_axis=0, tiled=True))
        if chunk + 2 < chunks:
            pieces, fields[chunk] = lax.optimization_barrier((state_cut[chunk + 2], fields[chunk]))
            state.append(swap(pieces, parts))
    for chunk in range(len(made), chunks):
        close(chunk)
    whole = None
    for chunk in range(chunks):
        whole = place_pieces(made[chunk], seats, whole, chunk, shape, size)
    grad = grand_total(device_grad(grads, seats, parts, made[-1][1:]))
    return whole.reshape(costate.shape), grad.reshape(2, 2, LEVELS)


def solution(mesh):
    return jax.shard_map(
        per_device,
        mesh=mesh,
        in_specs=(P(None, "dev", "grp"), P(None, "dev", "grp"), P(), P(), P(), P()),
        out_specs=(P(None, "dev", "grp"), P()),
        check_vma=False,
    )
```

```python
import functools

import jax
import jax.numpy as jnp
from jax import lax
from jax.experimental import pallas as pl
from jax.experimental.pallas import tpu as pltpu
from jax.sharding import PartitionSpec as P

LEVELS = 64
TRANSMON = 2
WIDE = LEVELS * TRANSMON
PAIR = 2 * WIDE
HIGH = lax.Precision.HIGHEST
F32 = jnp.float32
BF16 = jnp.bfloat16
SMALL = pl.CostEstimate(flops=1024, bytes_accessed=1024, transcendentals=0)
LARGE = pl.CostEstimate(flops=2 * 10**11, bytes_accessed=1024, transcendentals=0)
PARAMS = pltpu.CompilerParams(vmem_limit_bytes=48 * 1024 * 1024)


def split_value(value):
    high = value.astype(BF16)
    low = (value - high.astype(F32)).astype(BF16)
    return high, low


def mxu(left, right, dims=(((1,), (0,)), ((), ()))):
    return lax.dot_general(left, right, dims, preferred_element_type=F32)


def exact(left, right, dims=(((1,), (0,)), ((), ()))):
    return lax.dot_general(left, right, dims, precision=HIGH, preferred_element_type=F32)


def grid_of(shape, dim):
    return lax.broadcasted_iota(jnp.int32, shape, dim)


def pick_matrix(count, chosen):
    shape = (count, count)
    return (chosen(grid_of(shape, 0)) == grid_of(shape, 1)).astype(F32)


def spread(matrix):
    tall = (grid_of((WIDE, LEVELS), 0) // TRANSMON == grid_of((WIDE, LEVELS), 1)).astype(F32)
    long = (grid_of((LEVELS, WIDE), 1) // TRANSMON == grid_of((LEVELS, WIDE), 0)).astype(F32)
    same = grid_of((WIDE, WIDE), 0) % TRANSMON == grid_of((WIDE, WIDE), 1) % TRANSMON
    return jnp.where(same, exact(exact(tall, matrix), long), 0.0)


def blocks(upper_left, upper_right, lower_left, lower_right):
    return jnp.concatenate(
        [
            jnp.concatenate([upper_left, upper_right], axis=1),
            jnp.concatenate([lower_left, lower_right], axis=1),
        ],
        axis=0,
    )


def complex_product(left, right):
    return (
        exact(left[0], right[0]) - exact(left[1], right[1]),
        exact(left[0], right[1]) + exact(left[1], right[0]),
    )


def weights_kernel(parts, chunks, slot_ref, start_ref, seat_ref, *refs):
    angle_refs, matrix_refs = refs[0:2], refs[2:4]
    open_ref, turn_ref, level_ref, lane_ref = refs[-4:]
    seat = seat_ref[0]
    width = LEVELS // parts
    share = WIDE // parts
    size = share // chunks
    first, second = [], []
    for layer in range(2):
        cosine = jnp.cos(angle_refs[layer][...])
        sine = jnp.sin(angle_refs[layer][...])
        for mode, kept in enumerate((first, second)):
            turn_real, turn_imag = cosine[mode:mode + 1], sine[mode:mode + 1]
            real_part = matrix_refs[layer][mode, 0]
            imag_part = matrix_refs[layer][mode, 1]
            kept.append(
                (
                    real_part * turn_real - imag_part * turn_imag,
                    real_part * turn_imag + imag_part * turn_real,
                )
            )
    both_first = complex_product(first[1], first[0])
    both_second = complex_product(second[1], second[0])

    order = pick_matrix(
        LEVELS, lambda row: lax.bitwise_xor(row // width, seat) * width + row % width
    )

    def put_level(ref, index, real_part, imag_part):
        full = blocks(real_part, -imag_part, imag_part, real_part)
        high, low = split_value(full)
        made = blocks(high, high, low, jnp.zeros_like(low))
        if index is None:
            ref[...] = made
        else:
            ref[index] = made

    put_level(turn_ref, None, exact(both_first[0].T, order), exact(-both_first[1].T, order))
    put_level(level_ref, 0, first[1][0].T, first[1][1].T)
    put_level(level_ref, 1, exact(first[0][0], order), exact(-first[0][1], order))
    put_level(level_ref, 2, exact(order, first[0][0].T), exact(order, first[0][1].T))

    def put_lane(index, real_part, imag_part):
        real_part, imag_part = spread(real_part), spread(imag_part)
        high, low = split_value(blocks(real_part, imag_part, -imag_part, real_part))
        lane_ref[index, 0] = high
        lane_ref[index, 1] = low

    put_lane(0, *second[1])
    put_lane(1, second[0][0].T, -second[0][1].T)
    put_lane(2, *second[0])

    real_part, imag_part = spread(both_second[0].T), spread(both_second[1].T)
    full = blocks(real_part, -imag_part, -imag_part, -real_part)

    def source(row):
        chunk, rest = row // (2 * size * parts), row % (2 * size * parts)
        step, rest = rest // (2 * size), rest % (2 * size)
        half, place = rest // size, rest % size
        return half * WIDE + lax.bitwise_xor(step, seat) * share + chunk * size + place

    high, low = split_value(exact(pick_matrix(PAIR, source), full))
    open_ref[0] = high
    open_ref[1] = low


def make_weights(phases, displacements, table_slot, checkpoint, seat, parts, chunks):
    def angles(layer):
        return pl.BlockSpec(
            (None, 2, LEVELS), lambda i, slot, start, own: (slot[start[0] + layer], 0, 0)
        )

    def matrices(layer):
        return pl.BlockSpec(
            (None, 2, 2, LEVELS, LEVELS),
            lambda i, slot, start, own: (start[0] + layer, 0, 0, 0, 0),
        )

    def whole(shape):
        return pl.BlockSpec(shape, lambda i, slot, start, own: (0,) * len(shape))

    shapes = [(2, PAIR, PAIR), (PAIR, PAIR), (3, PAIR, PAIR), (3, 2, PAIR, PAIR)]
    return pl.pallas_call(
        functools.partial(weights_kernel, parts, chunks),
        grid_spec=pltpu.PrefetchScalarGridSpec(
            num_scalar_prefetch=3,
            grid=(1,),
            in_specs=[angles(0), angles(1), matrices(0), matrices(1)],
            out_specs=[whole(shape) for shape in shapes],
        ),
        out_shape=[jax.ShapeDtypeStruct(shape, BF16) for shape in shapes],
        compiler_params=PARAMS,
        cost_estimate=SMALL,
    )(table_slot, checkpoint, seat, phases, phases, displacements, displacements)


def open_kernel(count, waited, weight_ref, field_ref, *refs):
    both = jnp.concatenate([field_ref[0], field_ref[1]], axis=1)
    high, low = split_value(both)
    across = (((1,), (1,)), ((), ()))
    made = mxu(weight_ref[0], high, across) + (
        mxu(weight_ref[0], low, across) + mxu(weight_ref[1], high, across)
    )
    tall = made.shape[0] // count
    for place, out in enumerate(refs[waited:]):
        piece = made[place * tall:(place + 1) * tall]
        for first in range(out.shape[0]):
            out[first] = piece[:, first * WIDE:(first + 1) * WIDE]


def open_state(field, weights, parts, size, chunk_start, chunk_count, waited):
    rows, cols = field.shape[1:]
    firsts = rows // WIDE
    column_levels = cols // WIDE
    count = parts * chunk_count
    tall = count * 2 * size
    shape = jax.ShapeDtypeStruct((firsts, column_levels * 2 * size, WIDE), F32)
    weights = lax.slice_in_dim(
        weights, chunk_start * parts * 2 * size, chunk_start * parts * 2 * size + tall, axis=1
    )
    outs = pl.pallas_call(
        functools.partial(open_kernel, count, len(waited)),
        grid=(column_levels,),
        in_specs=[
            pl.BlockSpec((2, tall, PAIR), lambda i: (0, 0, 0)),
            pl.BlockSpec((2, rows, WIDE), lambda i: (0, 0, i)),
        ]
        + [pl.BlockSpec(memory_space=pl.ANY)] * len(waited),
        out_specs=[pl.BlockSpec((firsts, 2 * size, WIDE), lambda i: (0, i, 0))] * count,
        out_shape=[shape] * count,
        compiler_params=PARAMS,
        cost_estimate=SMALL,
    )(weights, field, *waited)
    return [outs[c * parts:(c + 1) * parts] for c in range(chunk_count)]


def cut_kernel(size, waited, seat_ref, field_ref, *refs):
    seat = seat_ref[0]
    levels = field_ref.shape[-1] // WIDE
    for step, out in enumerate(refs[waited:]):
        part = lax.bitwise_xor(seat, step)
        for half in range(2):
            for level in range(levels):
                start = (2 * level + half) * size
                out[start:start + size, :] = field_ref[
                    half, part, :, level * WIDE:(level + 1) * WIDE
                ]


def cut_pieces(field, seat, parts, chunk, size, waited):
    rows, cols = field.shape[1:]
    firsts = rows // WIDE
    chunks = WIDE // parts // size
    tall = cols // WIDE * 2 * size
    return pl.pallas_call(
        functools.partial(cut_kernel, size, len(waited)),
        grid=(firsts,),
        in_specs=[
            pl.BlockSpec(memory_space=pltpu.SMEM),
            pl.BlockSpec((2, None, parts, None, size, cols), lambda i: (0, i, 0, chunk, 0, 0)),
        ]
        + [pl.BlockSpec(memory_space=pl.ANY)] * len(waited),
        out_specs=[pl.BlockSpec((None, tall, WIDE), lambda i: (i, 0, 0))] * parts,
        out_shape=[jax.ShapeDtypeStruct((firsts, tall, WIDE), F32)] * parts,
        compiler_params=PARAMS,
        cost_estimate=SMALL,
    )(seat, field.reshape(2, firsts, parts, chunks, size, cols), *waited)


def level_apply(weights, real_part, imag_part):
    real_high, real_low = split_value(real_part)
    imag_high, imag_low = split_value(imag_part)
    stacked = jnp.concatenate([real_high, imag_high, real_low, imag_low], axis=0)
    made = mxu(weights, stacked)
    return made[:WIDE] + made[WIDE:]


def lane_apply(weight_ref, index, real_part, imag_part):
    high, low = split_value(jnp.concatenate([real_part, imag_part], axis=1))
    made = mxu(high, weight_ref[index, 0]) + (
        mxu(low, weight_ref[index, 0]) + mxu(high, weight_ref[index, 1])
    )
    return made[:, :WIDE], made[:, WIDE:]


def gather_levels(refs, size, half):
    columns = []
    for place in range(size):
        parts = [
            ref[pl.ds(half * size + place, ref.shape[0] // (2 * size), stride=2 * size), :]
            for ref in refs
        ]
        columns.append(jnp.concatenate(parts, axis=0) if len(parts) > 1 else parts[0])
    return jnp.concatenate(columns, axis=1)


def scatter_levels(ref, size, half, value):
    for place in range(size):
        ref[pl.ds(half * size + place, LEVELS, stride=2 * size), :] = value[
            :, place * WIDE:(place + 1) * WIDE
        ]


def turn_kernel(parts, size, weight_ref, *refs):
    pieces = refs[:parts]
    out_ref = refs[-1].reshape(LEVELS * 2 * size, WIDE)
    made = level_apply(
        weight_ref[...], gather_levels(pieces, size, 0), gather_levels(pieces, size, 1)
    )
    scatter_levels(out_ref, size, 0, made[:LEVELS])
    scatter_levels(out_ref, size, 1, made[LEVELS:])


def turn_columns(pieces, weights, size, waited):
    firsts = pieces[0].shape[0]
    parts = len(pieces)
    block = pieces[0].shape[1:]
    return pl.pallas_call(
        functools.partial(turn_kernel, parts, size),
        grid=(firsts,),
        in_specs=[pl.BlockSpec((PAIR, PAIR), lambda i: (0, 0))]
        + [pl.BlockSpec((None,) + block, lambda i: (i, 0, 0))] * parts
        + [pl.BlockSpec(memory_space=pl.ANY)] * len(waited),
        out_specs=pl.BlockSpec((LEVELS, None, 2 * size, WIDE), lambda i: (0, i, 0, 0)),
        out_shape=jax.ShapeDtypeStruct((LEVELS, firsts, 2 * size, WIDE), F32),
        compiler_params=PARAMS,
        cost_estimate=SMALL,
    )(weights, *pieces, *waited)


def halves(value, size):
    value = value.reshape(LEVELS, 2, size, WIDE)
    rows = LEVELS * size
    return value[:, 0].reshape(rows, WIDE), value[:, 1].reshape(rows, WIDE)


def join(real_part, imag_part, size):
    shape = (LEVELS, 1, size, WIDE)
    both = jnp.concatenate([real_part.reshape(shape), imag_part.reshape(shape)], axis=1)
    return both.reshape(LEVELS * 2 * size, WIDE)


def close_kernel(parts, size, lane_ref, level_ref, field_ref, *refs):
    rho_refs = refs[:parts]
    out_refs = refs[-parts - 3:-3]
    grad_ref, work_a, work_b = refs[-3:]
    step = pl.program_id(0)

    @pl.when(step == 0)
    def _():
        grad_ref[...] = jnp.zeros_like(grad_ref)

    flat = field_ref.reshape(LEVELS * 2 * size, WIDE)
    real_part, imag_part = lane_apply(lane_ref, 0, *halves(flat[...], size))
    work_a[...] = join(real_part, imag_part, size)

    rho = jnp.concatenate([ref[...] for ref in rho_refs], axis=0)
    rho_real, rho_imag = halves(rho, size)
    real_part, imag_part = lane_apply(lane_ref, 1, rho_real, rho_imag)
    work_b[...] = join(real_part, imag_part, size)

    mid = level_apply(level_ref[0], gather_levels([work_a], size, 0), gather_levels([work_a], size, 1))
    seen = level_apply(level_ref[1], gather_levels([work_b], size, 0), gather_levels([work_b], size, 1))
    terms = seen[:LEVELS] * mid[LEVELS:] - seen[LEVELS:] * mid[:LEVELS]
    total = terms[:, :WIDE]
    for place in range(1, size):
        total = total + terms[:, place * WIDE:(place + 1) * WIDE]
    grad_ref[1] += total

    last = level_apply(level_ref[2], mid[:LEVELS], mid[LEVELS:])
    scatter_levels(work_a, size, 0, last[:LEVELS])
    scatter_levels(work_a, size, 1, last[LEVELS:])
    real_part, imag_part = lane_apply(lane_ref, 2, *halves(work_a[...], size))
    terms = rho_real * imag_part - rho_imag * real_part
    grad_ref[0] += jnp.sum(terms.reshape(LEVELS, size, WIDE), axis=1)
    made = join(real_part, imag_part, size)
    rows = made.shape[0] // parts
    for part in range(parts):
        out_refs[part][...] = made[part * rows:(part + 1) * rows]


def close_columns(field, rho_pieces, lane, level, size, waited):
    total_first, firsts = field.shape[:2]
    devs = total_first // firsts
    parts = len(rho_pieces)
    rows = LEVELS * 2 * size
    field = field.reshape(devs, firsts, firsts * 2 * size, WIDE)
    piece = rho_pieces[0]
    piece_spec = pl.BlockSpec((None,) + piece.shape[1:], lambda i: (i, 0, 0))
    outs = pl.pallas_call(
        functools.partial(close_kernel, parts, size),
        grid=(firsts,),
        in_specs=[
            pl.BlockSpec(lane.shape, lambda i: (0, 0, 0, 0)),
            pl.BlockSpec(level.shape, lambda i: (0, 0, 0)),
            pl.BlockSpec((devs, None, firsts * 2 * size, WIDE), lambda i: (0, i, 0, 0)),
        ]
        + [piece_spec] * parts
        + [pl.BlockSpec(memory_space=pl.ANY)] * len(waited),
        out_specs=[piece_spec] * parts + [pl.BlockSpec((2, LEVELS, WIDE), lambda i: (0, 0, 0))],
        out_shape=[jax.ShapeDtypeStruct(piece.shape, F32)] * parts
        + [jax.ShapeDtypeStruct((2, LEVELS, WIDE), F32)],
        scratch_shapes=[pltpu.VMEM((rows, WIDE), F32), pltpu.VMEM((rows, WIDE), F32)],
        compiler_params=PARAMS,
        cost_estimate=LARGE,
    )(lane, level, field, *rho_pieces, *waited)
    return list(outs[:parts]), outs[parts]


def place_kernel(parts, size, aliased, seat_ref, *refs):
    pieces = refs[:parts]
    out_ref = refs[parts + aliased]
    seat = seat_ref[0]
    levels = pieces[0].shape[0] // (2 * size)
    for step in range(parts):
        part = lax.bitwise_xor(seat, step)
        for half in range(2):
            for level in range(levels):
                start = level * 2 * size + half * size
                out_ref[half, part, :, level * WIDE:(level + 1) * WIDE] = pieces[step][
                    start:start + size, :
                ]


def place_pieces(pieces, seat, held, chunk, shape, size):
    parts = len(pieces)
    firsts, chunks = shape[1], shape[3]
    aliased = 0 if held is None else 1
    piece = pieces[0]
    cols = shape[-1]
    return pl.pallas_call(
        functools.partial(place_kernel, parts, size, aliased),
        grid=(firsts,),
        in_specs=[pl.BlockSpec(memory_space=pltpu.SMEM)]
        + [pl.BlockSpec((None,) + piece.shape[1:], lambda i: (i, 0, 0))] * parts
        + [pl.BlockSpec(memory_space=pl.ANY)] * aliased,
        out_specs=pl.BlockSpec(
            (2, None, parts, None, size, cols), lambda i: (0, i, 0, chunk, 0, 0)
        ),
        out_shape=jax.ShapeDtypeStruct(shape, F32),
        input_output_aliases={parts + 1: 0} if aliased else {},
        compiler_params=PARAMS,
        cost_estimate=SMALL,
    )(seat, *pieces, *([held] if aliased else []))


def swap(pieces, parts):
    moved = [pieces[0]]
    for step in range(1, parts):
        pairs = [(member, member ^ step) for member in range(parts)]
        moved.append(lax.ppermute(pieces[step], "grp", pairs))
    return moved


def grad_kernel(parts, count, seat_ref, *refs):
    out_ref = refs[-1]
    grad = refs[0][...]
    for ref in refs[1:count]:
        grad = grad + ref[...]
    grad = -2.0 * grad
    width = LEVELS // parts
    order = pick_matrix(
        LEVELS, lambda row: lax.bitwise_xor(row // width, seat_ref[0]) * width + row % width
    )
    fold = (grid_of((WIDE, LEVELS), 0) // TRANSMON == grid_of((WIDE, LEVELS), 1)).astype(F32)
    for layer in range(2):
        firsts = exact(jnp.ones((8, WIDE), F32), grad[layer], (((1,), (1,)), ((), ())))
        if layer == 0:
            firsts = exact(firsts, order)
        seconds = exact(exact(jnp.ones((8, LEVELS), F32), grad[layer]), fold)
        out_ref[2 * layer:2 * layer + 1, :] = firsts[:1]
        out_ref[2 * layer + 1:2 * layer + 2, :] = seconds[:1]


def device_grad(grads, seat, parts, waited):
    return pl.pallas_call(
        functools.partial(grad_kernel, parts, len(grads)),
        in_specs=[pl.BlockSpec(memory_space=pltpu.SMEM)]
        + [pl.BlockSpec(memory_space=pltpu.VMEM)] * len(grads)
        + [pl.BlockSpec(memory_space=pl.ANY)] * len(waited),
        out_specs=pl.BlockSpec(memory_space=pltpu.VMEM),
        out_shape=jax.ShapeDtypeStruct((4, LEVELS), F32),
        compiler_params=PARAMS,
        cost_estimate=SMALL,
    )(seat, *grads, *waited)


def grand_total(value):
    rounds = []
    for axis in ("grp", "dev"):
        count = lax.axis_size(axis)
        rounds.append([(axis, 1 << bit, count) for bit in range(count.bit_length() - 1)])
    for axis, step, count in rounds[0][:1] + rounds[1] + rounds[0][1:]:
        pairs = [(member, member ^ step) for member in range(count)]
        value = value + lax.ppermute(value, axis, pairs)
    return value


def per_device(density, costate, phases, displacements, table_slot, checkpoint):
    parts = lax.axis_size("grp")
    share = WIDE // parts
    chunks = max(1, min(4, share // 8))
    size = share // chunks
    seat = lax.axis_index("grp").astype(jnp.int32)
    seats = seat.reshape(1)
    rows, cols = costate.shape[1:]

    opened, turned_by, level, lane = make_weights(
        phases, displacements, table_slot, checkpoint, seats, parts, chunks
    )
    state_cut = open_state(costate, opened, parts, size, 0, 1, [])
    if chunks > 1:
        state_cut += open_state(
            costate, opened, parts, size, 1, chunks - 1, list(state_cut[0][:1])
        )
    rho = [
        cut_pieces(density, seats, parts, chunk, size, list(state_cut[-1][:1]))
        for chunk in range(chunks)
    ]
    state = [swap(pieces, parts) for pieces in state_cut[:2]]
    rho_there = [swap(pieces, parts) for pieces in rho]

    shape = (2, rows // WIDE, parts, chunks, size, cols)
    fields, closed, made, grads = [], [], [], []

    def close(chunk, waited):
        if chunk > 0:
            waited = waited + closed[chunk - 1][:1]
        out, grad = close_columns(
            fields[chunk], rho_there[chunk], lane, level, size, waited
        )
        closed.append(out)
        made.append(swap(out, parts))
        grads.append(grad)

    for chunk in range(chunks):
        waited = [rho[chunk][0]]
        if chunk > 0:
            waited.append(field)
        if chunk == 1:
            waited += rho_there[0][1:]
        if chunk > 1:
            close(chunk - 2, [])
            waited += closed[chunk - 2][:1]
        field = turn_columns(state[chunk], turned_by, size, waited)
        fields.append(lax.all_to_all(field, "dev", split_axis=0, concat_axis=0, tiled=True))
        if chunk + 2 < chunks:
            pieces, fields[chunk] = lax.optimization_barrier((state_cut[chunk + 2], fields[chunk]))
            state.append(swap(pieces, parts))
    whole = None
    for chunk in range(chunks):
        if chunk == len(made):
            waited = list(made[chunk - 2][1:]) if chunk > 1 else []
            close(chunk, [whole] if 0 < chunk == chunks - 1 else waited)
        whole = place_pieces(made[chunk], seats, whole, chunk, shape, size)
    grad = grand_total(device_grad(grads, seats, parts, made[-1][1:]))
    return whole.reshape(costate.shape), grad.reshape(2, 2, LEVELS)


def solution(mesh):
    return jax.shard_map(
        per_device,
        mesh=mesh,
        in_specs=(P(None, "dev", "grp"), P(None, "dev", "grp"), P(), P(), P(), P()),
        out_specs=(P(None, "dev", "grp"), P()),
        check_vma=False,
    )
```

```python
import functools

import jax
import jax.numpy as jnp
from jax import lax
from jax.experimental import pallas as pl
from jax.experimental.pallas import tpu as pltpu
from jax.sharding import PartitionSpec as P

LEVELS = 64
TRANSMON = 2
WIDE = LEVELS * TRANSMON
PAIR = 2 * WIDE
HIGH = lax.Precision.HIGHEST
F32 = jnp.float32
BF16 = jnp.bfloat16
SMALL = pl.CostEstimate(flops=1024, bytes_accessed=1024, transcendentals=0)
LARGE = pl.CostEstimate(flops=2 * 10**11, bytes_accessed=1024, transcendentals=0)
PARAMS = pltpu.CompilerParams(vmem_limit_bytes=60 * 1024 * 1024)


def split_value(value):
    high = value.astype(BF16)
    low = (value - high.astype(F32)).astype(BF16)
    return high, low


def mxu(left, right, dims=(((1,), (0,)), ((), ()))):
    return lax.dot_general(left, right, dims, preferred_element_type=F32)


def exact(left, right, dims=(((1,), (0,)), ((), ()))):
    return lax.dot_general(left, right, dims, precision=HIGH, preferred_element_type=F32)


def grid_of(shape, dim):
    return lax.broadcasted_iota(jnp.int32, shape, dim)


def pick_matrix(count, chosen):
    shape = (count, count)
    return (chosen(grid_of(shape, 0)) == grid_of(shape, 1)).astype(F32)


def spread(matrix):
    tall = (grid_of((WIDE, LEVELS), 0) // TRANSMON == grid_of((WIDE, LEVELS), 1)).astype(F32)
    long = (grid_of((LEVELS, WIDE), 1) // TRANSMON == grid_of((LEVELS, WIDE), 0)).astype(F32)
    same = grid_of((WIDE, WIDE), 0) % TRANSMON == grid_of((WIDE, WIDE), 1) % TRANSMON
    return jnp.where(same, exact(exact(tall, matrix), long), 0.0)


def blocks(upper_left, upper_right, lower_left, lower_right):
    return jnp.concatenate(
        [
            jnp.concatenate([upper_left, upper_right], axis=1),
            jnp.concatenate([lower_left, lower_right], axis=1),
        ],
        axis=0,
    )


def complex_product(left, right):
    return (
        exact(left[0], right[0]) - exact(left[1], right[1]),
        exact(left[0], right[1]) + exact(left[1], right[0]),
    )


def weights_kernel(parts, chunks, slot_ref, start_ref, seat_ref, *refs):
    angle_refs, matrix_refs = refs[0:2], refs[2:4]
    first_ref, open_ref, turn_ref, level_ref, lane_ref = refs[-5:]
    seat = seat_ref[0]
    width = LEVELS // parts
    share = WIDE // parts
    size = share // chunks
    first, second = [], []
    for layer in range(2):
        cosine = jnp.cos(angle_refs[layer][...])
        sine = jnp.sin(angle_refs[layer][...])
        for mode, kept in enumerate((first, second)):
            turn_real, turn_imag = cosine[mode:mode + 1], sine[mode:mode + 1]
            real_part = matrix_refs[layer][mode, 0]
            imag_part = matrix_refs[layer][mode, 1]
            kept.append(
                (
                    real_part * turn_real - imag_part * turn_imag,
                    real_part * turn_imag + imag_part * turn_real,
                )
            )
    both_first = complex_product(first[1], first[0])
    both_second = complex_product(second[1], second[0])

    order = pick_matrix(
        LEVELS, lambda row: lax.bitwise_xor(row // width, seat) * width + row % width
    )

    def put_level(ref, index, real_part, imag_part):
        full = blocks(real_part, -imag_part, imag_part, real_part)
        high, low = split_value(full)
        made = blocks(high, high, low, jnp.zeros_like(low))
        if index is None:
            ref[...] = made
        else:
            ref[index] = made

    put_level(turn_ref, None, exact(both_first[0].T, order), exact(-both_first[1].T, order))
    put_level(level_ref, 0, first[1][0].T, first[1][1].T)
    put_level(level_ref, 1, exact(first[0][0], order), exact(-first[0][1], order))
    put_level(level_ref, 2, exact(order, first[0][0].T), exact(order, first[0][1].T))

    def put_lane(index, real_part, imag_part):
        real_part, imag_part = spread(real_part), spread(imag_part)
        high, low = split_value(blocks(real_part, imag_part, -imag_part, real_part))
        lane_ref[index, 0] = high
        lane_ref[index, 1] = low

    put_lane(0, *second[1])
    put_lane(1, second[0][0].T, -second[0][1].T)
    put_lane(2, *second[0])

    real_part, imag_part = spread(both_second[0].T), spread(both_second[1].T)
    full = blocks(real_part, -imag_part, -imag_part, -real_part)

    def source(row):
        chunk, rest = row // (2 * size * parts), row % (2 * size * parts)
        step, rest = rest // (2 * size), rest % (2 * size)
        half, place = rest // size, rest % size
        return half * WIDE + lax.bitwise_xor(step, seat) * share + chunk * size + place

    chosen = exact(pick_matrix(PAIR, source), full)
    high, low = split_value(chosen)
    open_ref[0] = high
    open_ref[1] = low
    high, low = split_value(chosen[:PAIR // chunks].T)
    first_ref[...] = blocks(high, low, high, jnp.zeros_like(low))


def make_weights(phases, displacements, table_slot, checkpoint, seat, parts, chunks):
    def angles(layer):
        return pl.BlockSpec(
            (None, 2, LEVELS), lambda i, slot, start, own: (slot[start[0] + layer], 0, 0)
        )

    def matrices(layer):
        return pl.BlockSpec(
            (None, 2, 2, LEVELS, LEVELS),
            lambda i, slot, start, own: (start[0] + layer, 0, 0, 0, 0),
        )

    def whole(shape):
        return pl.BlockSpec(shape, lambda i, slot, start, own: (0,) * len(shape))

    shapes = [(2 * PAIR, 2 * PAIR // chunks), (2, PAIR, PAIR), (PAIR, PAIR), (3, PAIR, PAIR), (3, 2, PAIR, PAIR)]
    return pl.pallas_call(
        functools.partial(weights_kernel, parts, chunks),
        grid_spec=pltpu.PrefetchScalarGridSpec(
            num_scalar_prefetch=3,
            grid=(1,),
            in_specs=[angles(0), angles(1), matrices(0), matrices(1)],
            out_specs=[whole(shape) for shape in shapes],
        ),
        out_shape=[jax.ShapeDtypeStruct(shape, BF16) for shape in shapes],
        compiler_params=PARAMS,
        cost_estimate=SMALL,
    )(table_slot, checkpoint, seat, phases, phases, displacements, displacements)


def open_kernel(count, waited, weight_ref, field_ref, *refs):
    both = jnp.concatenate([field_ref[0], field_ref[1]], axis=1)
    high, low = split_value(both)
    across = (((1,), (1,)), ((), ()))
    made = mxu(weight_ref[0], high, across) + (
        mxu(weight_ref[0], low, across) + mxu(weight_ref[1], high, across)
    )
    tall = made.shape[0] // count
    for place, out in enumerate(refs[waited:]):
        piece = made[place * tall:(place + 1) * tall]
        for first in range(out.shape[0]):
            out[first] = piece[:, first * WIDE:(first + 1) * WIDE]


def open_first_kernel(weight_ref, field_ref, *out_refs):
    real_high, real_low = split_value(field_ref[0])
    imag_high, imag_low = split_value(field_ref[1])
    both = jnp.concatenate([real_high, imag_high, real_low, imag_low], axis=1)
    made = mxu(both, weight_ref[...]).T
    middle = made.shape[0] // 2
    made = made[:middle] + made[middle:]
    tall = middle // len(out_refs)
    for place, out in enumerate(out_refs):
        piece = made[place * tall:(place + 1) * tall]
        for first in range(out.shape[0]):
            out[first] = piece[:, first * WIDE:(first + 1) * WIDE]


def open_first(field, weights, parts, size):
    rows, cols = field.shape[1:]
    firsts = rows // WIDE
    column_levels = cols // WIDE
    shape = jax.ShapeDtypeStruct((firsts, column_levels * 2 * size, WIDE), F32)
    outs = pl.pallas_call(
        open_first_kernel,
        grid=(column_levels,),
        in_specs=[
            pl.BlockSpec(weights.shape, lambda i: (0, 0)),
            pl.BlockSpec((2, rows, WIDE), lambda i: (0, 0, i)),
        ],
        out_specs=[pl.BlockSpec((firsts, 2 * size, WIDE), lambda i: (0, i, 0))] * parts,
        out_shape=[shape] * parts,
        compiler_params=PARAMS,
        cost_estimate=SMALL,
    )(weights, field)
    return [outs]


def open_state(field, weights, parts, size, chunk_start, chunk_count, waited):
    rows, cols = field.shape[1:]
    firsts = rows // WIDE
    column_levels = cols // WIDE
    count = parts * chunk_count
    tall = count * 2 * size
    shape = jax.ShapeDtypeStruct((firsts, column_levels * 2 * size, WIDE), F32)
    weights = lax.slice_in_dim(
        weights, chunk_start * parts * 2 * size, chunk_start * parts * 2 * size + tall, axis=1
    )
    outs = pl.pallas_call(
        functools.partial(open_kernel, count, len(waited)),
        grid=(column_levels,),
        in_specs=[
            pl.BlockSpec((2, tall, PAIR), lambda i: (0, 0, 0)),
            pl.BlockSpec((2, rows, WIDE), lambda i: (0, 0, i)),
        ]
        + [pl.BlockSpec(memory_space=pl.ANY)] * len(waited),
        out_specs=[pl.BlockSpec((firsts, 2 * size, WIDE), lambda i: (0, i, 0))] * count,
        out_shape=[shape] * count,
        compiler_params=PARAMS,
        cost_estimate=SMALL,
    )(weights, field, *waited)
    return [outs[c * parts:(c + 1) * parts] for c in range(chunk_count)]


def cut_kernel(size, waited, seat_ref, field_ref, *refs):
    seat = seat_ref[0]
    levels = field_ref.shape[-1] // WIDE
    for step, out in enumerate(refs[waited:]):
        part = lax.bitwise_xor(seat, step)
        for half in range(2):
            for level in range(levels):
                start = (2 * level + half) * size
                out[start:start + size, :] = field_ref[
                    half, part, :, level * WIDE:(level + 1) * WIDE
                ]


def cut_pieces(field, seat, parts, chunk, size, waited):
    rows, cols = field.shape[1:]
    firsts = rows // WIDE
    chunks = WIDE // parts // size
    tall = cols // WIDE * 2 * size
    return pl.pallas_call(
        functools.partial(cut_kernel, size, len(waited)),
        grid=(firsts,),
        in_specs=[
            pl.BlockSpec(memory_space=pltpu.SMEM),
            pl.BlockSpec((2, None, parts, None, size, cols), lambda i: (0, i, 0, chunk, 0, 0)),
        ]
        + [pl.BlockSpec(memory_space=pl.ANY)] * len(waited),
        out_specs=[pl.BlockSpec((None, tall, WIDE), lambda i: (i, 0, 0))] * parts,
        out_shape=[jax.ShapeDtypeStruct((firsts, tall, WIDE), F32)] * parts,
        compiler_params=PARAMS,
        cost_estimate=SMALL,
    )(seat, field.reshape(2, firsts, parts, chunks, size, cols), *waited)


def level_apply(weights, real_part, imag_part):
    real_high, real_low = split_value(real_part)
    imag_high, imag_low = split_value(imag_part)
    stacked = jnp.concatenate([real_high, imag_high, real_low, imag_low], axis=0)
    made = mxu(weights, stacked)
    return made[:WIDE] + made[WIDE:]


def lane_apply(weight_ref, index, real_part, imag_part):
    high, low = split_value(jnp.concatenate([real_part, imag_part], axis=1))
    made = mxu(high, weight_ref[index, 0]) + (
        mxu(low, weight_ref[index, 0]) + mxu(high, weight_ref[index, 1])
    )
    return made[:, :WIDE], made[:, WIDE:]


def gather_levels(refs, size, half):
    columns = []
    for place in range(size):
        parts = [
            ref[pl.ds(half * size + place, ref.shape[0] // (2 * size), stride=2 * size), :]
            for ref in refs
        ]
        columns.append(jnp.concatenate(parts, axis=0) if len(parts) > 1 else parts[0])
    return jnp.concatenate(columns, axis=1)


def scatter_levels(ref, size, half, value):
    for place in range(size):
        ref[pl.ds(half * size + place, LEVELS, stride=2 * size), :] = value[
            :, place * WIDE:(place + 1) * WIDE
        ]


def turn_kernel(parts, size, weight_ref, *refs):
    pieces = refs[:parts]
    out_ref = refs[-1].reshape(LEVELS * 2 * size, WIDE)
    made = level_apply(
        weight_ref[...], gather_levels(pieces, size, 0), gather_levels(pieces, size, 1)
    )
    scatter_levels(out_ref, size, 0, made[:LEVELS])
    scatter_levels(out_ref, size, 1, made[LEVELS:])


def turn_columns(pieces, weights, size, waited):
    firsts = pieces[0].shape[0]
    parts = len(pieces)
    block = pieces[0].shape[1:]
    return pl.pallas_call(
        functools.partial(turn_kernel, parts, size),
        grid=(firsts,),
        in_specs=[pl.BlockSpec((PAIR, PAIR), lambda i: (0, 0))]
        + [pl.BlockSpec((None,) + block, lambda i: (i, 0, 0))] * parts
        + [pl.BlockSpec(memory_space=pl.ANY)] * len(waited),
        out_specs=pl.BlockSpec((LEVELS, None, 2 * size, WIDE), lambda i: (0, i, 0, 0)),
        out_shape=jax.ShapeDtypeStruct((LEVELS, firsts, 2 * size, WIDE), F32),
        compiler_params=PARAMS,
        cost_estimate=SMALL,
    )(weights, *pieces, *waited)


def halves(value, size):
    value = value.reshape(LEVELS, 2, size, WIDE)
    rows = LEVELS * size
    return value[:, 0].reshape(rows, WIDE), value[:, 1].reshape(rows, WIDE)


def join(real_part, imag_part, size):
    shape = (LEVELS, 1, size, WIDE)
    both = jnp.concatenate([real_part.reshape(shape), imag_part.reshape(shape)], axis=1)
    return both.reshape(LEVELS * 2 * size, WIDE)


def close_kernel(parts, size, lane_ref, level_ref, field_ref, *refs):
    rho_refs = refs[:parts]
    out_refs = refs[-parts - 3:-3]
    grad_ref, work_a, work_b = refs[-3:]
    step = pl.program_id(0)

    @pl.when(step == 0)
    def _():
        grad_ref[...] = jnp.zeros_like(grad_ref)

    flat = field_ref.reshape(LEVELS * 2 * size, WIDE)
    real_part, imag_part = lane_apply(lane_ref, 0, *halves(flat[...], size))
    work_a[...] = join(real_part, imag_part, size)

    rho = jnp.concatenate([ref[...] for ref in rho_refs], axis=0)
    rho_real, rho_imag = halves(rho, size)
    real_part, imag_part = lane_apply(lane_ref, 1, rho_real, rho_imag)
    work_b[...] = join(real_part, imag_part, size)

    mid = level_apply(level_ref[0], gather_levels([work_a], size, 0), gather_levels([work_a], size, 1))
    seen = level_apply(level_ref[1], gather_levels([work_b], size, 0), gather_levels([work_b], size, 1))
    terms = seen[:LEVELS] * mid[LEVELS:] - seen[LEVELS:] * mid[:LEVELS]
    total = terms[:, :WIDE]
    for place in range(1, size):
        total = total + terms[:, place * WIDE:(place + 1) * WIDE]
    grad_ref[1] += total

    last = level_apply(level_ref[2], mid[:LEVELS], mid[LEVELS:])
    scatter_levels(work_a, size, 0, last[:LEVELS])
    scatter_levels(work_a, size, 1, last[LEVELS:])
    real_part, imag_part = lane_apply(lane_ref, 2, *halves(work_a[...], size))
    terms = rho_real * imag_part - rho_imag * real_part
    grad_ref[0] += jnp.sum(terms.reshape(LEVELS, size, WIDE), axis=1)
    made = join(real_part, imag_part, size)
    rows = made.shape[0] // parts
    for part in range(parts):
        out_refs[part][...] = made[part * rows:(part + 1) * rows]


def close_columns(field, rho_pieces, lane, level, size, waited):
    total_first, firsts = field.shape[:2]
    devs = total_first // firsts
    parts = len(rho_pieces)
    rows = LEVELS * 2 * size
    field = field.reshape(devs, firsts, firsts * 2 * size, WIDE)
    piece = rho_pieces[0]
    piece_spec = pl.BlockSpec((None,) + piece.shape[1:], lambda i: (i, 0, 0))
    outs = pl.pallas_call(
        functools.partial(close_kernel, parts, size),
        grid=(firsts,),
        in_specs=[
            pl.BlockSpec(lane.shape, lambda i: (0, 0, 0, 0)),
            pl.BlockSpec(level.shape, lambda i: (0, 0, 0)),
            pl.BlockSpec((devs, None, firsts * 2 * size, WIDE), lambda i: (0, i, 0, 0)),
        ]
        + [piece_spec] * parts
        + [pl.BlockSpec(memory_space=pl.ANY)] * len(waited),
        out_specs=[piece_spec] * parts + [pl.BlockSpec((2, LEVELS, WIDE), lambda i: (0, 0, 0))],
        out_shape=[jax.ShapeDtypeStruct(piece.shape, F32)] * parts
        + [jax.ShapeDtypeStruct((2, LEVELS, WIDE), F32)],
        scratch_shapes=[pltpu.VMEM((rows, WIDE), F32), pltpu.VMEM((rows, WIDE), F32)],
        compiler_params=PARAMS,
        cost_estimate=LARGE,
    )(lane, level, field, *rho_pieces, *waited)
    return list(outs[:parts]), outs[parts]


def place_kernel(parts, size, aliased, seat_ref, *refs):
    pieces = refs[:parts]
    out_ref = refs[parts + aliased]
    seat = seat_ref[0]
    levels = pieces[0].shape[0] // (2 * size)
    for step in range(parts):
        part = lax.bitwise_xor(seat, step)
        for half in range(2):
            for level in range(levels):
                start = level * 2 * size + half * size
                out_ref[half, part, :, level * WIDE:(level + 1) * WIDE] = pieces[step][
                    start:start + size, :
                ]


def place_pieces(pieces, seat, held, chunk, shape, size):
    parts = len(pieces)
    firsts, chunks = shape[1], shape[3]
    aliased = 0 if held is None else 1
    piece = pieces[0]
    cols = shape[-1]
    return pl.pallas_call(
        functools.partial(place_kernel, parts, size, aliased),
        grid=(firsts,),
        in_specs=[pl.BlockSpec(memory_space=pltpu.SMEM)]
        + [pl.BlockSpec((None,) + piece.shape[1:], lambda i: (i, 0, 0))] * parts
        + [pl.BlockSpec(memory_space=pl.ANY)] * aliased,
        out_specs=pl.BlockSpec(
            (2, None, parts, None, size, cols), lambda i: (0, i, 0, chunk, 0, 0)
        ),
        out_shape=jax.ShapeDtypeStruct(shape, F32),
        input_output_aliases={parts + 1: 0} if aliased else {},
        compiler_params=PARAMS,
        cost_estimate=SMALL,
    )(seat, *pieces, *([held] if aliased else []))


def swap(pieces, parts):
    moved = [pieces[0]]
    for step in range(1, parts):
        pairs = [(member, member ^ step) for member in range(parts)]
        moved.append(lax.ppermute(pieces[step], "grp", pairs))
    return moved


def grad_kernel(parts, count, seat_ref, *refs):
    out_ref = refs[-1]
    grad = refs[0][...]
    for ref in refs[1:count]:
        grad = grad + ref[...]
    grad = -2.0 * grad
    width = LEVELS // parts
    order = pick_matrix(
        LEVELS, lambda row: lax.bitwise_xor(row // width, seat_ref[0]) * width + row % width
    )
    fold = (grid_of((WIDE, LEVELS), 0) // TRANSMON == grid_of((WIDE, LEVELS), 1)).astype(F32)
    for layer in range(2):
        firsts = exact(jnp.ones((8, WIDE), F32), grad[layer], (((1,), (1,)), ((), ())))
        if layer == 0:
            firsts = exact(firsts, order)
        seconds = exact(exact(jnp.ones((8, LEVELS), F32), grad[layer]), fold)
        out_ref[2 * layer:2 * layer + 1, :] = firsts[:1]
        out_ref[2 * layer + 1:2 * layer + 2, :] = seconds[:1]


def device_grad(grads, seat, parts, waited):
    return pl.pallas_call(
        functools.partial(grad_kernel, parts, len(grads)),
        in_specs=[pl.BlockSpec(memory_space=pltpu.SMEM)]
        + [pl.BlockSpec(memory_space=pltpu.VMEM)] * len(grads)
        + [pl.BlockSpec(memory_space=pl.ANY)] * len(waited),
        out_specs=pl.BlockSpec(memory_space=pltpu.VMEM),
        out_shape=jax.ShapeDtypeStruct((4, LEVELS), F32),
        compiler_params=PARAMS,
        cost_estimate=SMALL,
    )(seat, *grads, *waited)


def grand_total(value):
    rounds = []
    for axis in ("grp", "dev"):
        count = lax.axis_size(axis)
        rounds.append([(axis, 1 << bit, count) for bit in range(count.bit_length() - 1)])
    for axis, step, count in rounds[0][:1] + rounds[1] + rounds[0][1:]:
        pairs = [(member, member ^ step) for member in range(count)]
        value = value + lax.ppermute(value, axis, pairs)
    return value


def per_device(density, costate, phases, displacements, table_slot, checkpoint):
    parts = lax.axis_size("grp")
    share = WIDE // parts
    chunks = max(1, min(4, share // 8))
    size = share // chunks
    seat = lax.axis_index("grp").astype(jnp.int32)
    seats = seat.reshape(1)
    rows, cols = costate.shape[1:]

    opened_first, opened, turned_by, level, lane = make_weights(
        phases, displacements, table_slot, checkpoint, seats, parts, chunks
    )
    state_cut = open_first(costate, opened_first, parts, size)
    if chunks > 1:
        state_cut += open_state(
            costate, opened, parts, size, 1, chunks - 1, list(state_cut[0][:1])
        )
    rho = [
        cut_pieces(density, seats, parts, chunk, size, list(state_cut[-1][:1]))
        for chunk in range(chunks)
    ]
    state = [swap(pieces, parts) for pieces in state_cut[:3]]
    rho_there = [swap(pieces, parts) for pieces in rho]

    shape = (2, rows // WIDE, parts, chunks, size, cols)
    fields, closed, made, grads = [], [], [], []

    def close(chunk, waited):
        if chunk > 0:
            waited = waited + closed[chunk - 1][:1]
        out, grad = close_columns(
            fields[chunk], rho_there[chunk], lane, level, size, waited
        )
        closed.append(out)
        made.append(swap(out, parts))
        grads.append(grad)

    for chunk in range(chunks):
        waited = [rho[chunk][0]]
        if chunk > 0:
            waited.append(field)
        if chunk > 1:
            close(chunk - 2, [])
            waited += closed[chunk - 2][:1]
        field = turn_columns(state[chunk], turned_by, size, waited)
        if chunk + 1 == len(state) < chunks:
            pieces, field = lax.optimization_barrier((state_cut[chunk + 1], field))
            state.append(swap(pieces, parts))
        fields.append(lax.all_to_all(field, "dev", split_axis=0, concat_axis=0, tiled=True))
    whole = None
    for chunk in range(chunks):
        if chunk == len(made):
            waited = list(made[chunk - 2][1:]) if chunk > 1 else []
            close(chunk, [whole] if 0 < chunk == chunks - 1 else waited)
        whole = place_pieces(made[chunk], seats, whole, chunk, shape, size)
    grad = grand_total(device_grad(grads, seats, parts, made[-1][1:]))
    return whole.reshape(costate.shape), grad.reshape(2, 2, LEVELS)


def solution(mesh):
    return jax.shard_map(
        per_device,
        mesh=mesh,
        in_specs=(P(None, "dev", "grp"), P(None, "dev", "grp"), P(), P(), P(), P()),
        out_specs=(P(None, "dev", "grp"), P()),
        check_vma=False,
    )
```

```python
import functools

import jax
import jax.numpy as jnp
from jax import lax
from jax.experimental import pallas as pl
from jax.experimental.pallas import tpu as pltpu
from jax.sharding import PartitionSpec as P

LEVELS = 64
TRANSMON = 2
WIDE = LEVELS * TRANSMON
PAIR = 2 * WIDE
HIGH = lax.Precision.HIGHEST
F32 = jnp.float32
BF16 = jnp.bfloat16
SMALL = pl.CostEstimate(flops=1024, bytes_accessed=1024, transcendentals=0)
LARGE = pl.CostEstimate(flops=2 * 10**11, bytes_accessed=1024, transcendentals=0)
PARAMS = pltpu.CompilerParams(vmem_limit_bytes=60 * 1024 * 1024)


def split_value(value):
    high = value.astype(BF16)
    low = (value - high.astype(F32)).astype(BF16)
    return high, low


def mxu(left, right, dims=(((1,), (0,)), ((), ()))):
    return lax.dot_general(left, right, dims, preferred_element_type=F32)


def exact(left, right, dims=(((1,), (0,)), ((), ()))):
    return lax.dot_general(left, right, dims, precision=HIGH, preferred_element_type=F32)


def grid_of(shape, dim):
    return lax.broadcasted_iota(jnp.int32, shape, dim)


def pick_matrix(count, chosen):
    shape = (count, count)
    return (chosen(grid_of(shape, 0)) == grid_of(shape, 1)).astype(F32)


def spread(matrix):
    tall = (grid_of((WIDE, LEVELS), 0) // TRANSMON == grid_of((WIDE, LEVELS), 1)).astype(F32)
    long = (grid_of((LEVELS, WIDE), 1) // TRANSMON == grid_of((LEVELS, WIDE), 0)).astype(F32)
    same = grid_of((WIDE, WIDE), 0) % TRANSMON == grid_of((WIDE, WIDE), 1) % TRANSMON
    return jnp.where(same, exact(exact(tall, matrix), long), 0.0)


def blocks(upper_left, upper_right, lower_left, lower_right):
    return jnp.concatenate(
        [
            jnp.concatenate([upper_left, upper_right], axis=1),
            jnp.concatenate([lower_left, lower_right], axis=1),
        ],
        axis=0,
    )


def complex_product(left, right):
    return (
        exact(left[0], right[0]) - exact(left[1], right[1]),
        exact(left[0], right[1]) + exact(left[1], right[0]),
    )


def weights_kernel(parts, chunks, slot_ref, start_ref, seat_ref, *refs):
    angle_refs, matrix_refs = refs[0:2], refs[2:4]
    first_ref, open_ref, turn_ref, level_ref, lane_ref = refs[-5:]
    seat = seat_ref[0]
    width = LEVELS // parts
    share = WIDE // parts
    size = share // chunks
    first, second = [], []
    for layer in range(2):
        cosine = jnp.cos(angle_refs[layer][...])
        sine = jnp.sin(angle_refs[layer][...])
        for mode, kept in enumerate((first, second)):
            turn_real, turn_imag = cosine[mode:mode + 1], sine[mode:mode + 1]
            real_part = matrix_refs[layer][mode, 0]
            imag_part = matrix_refs[layer][mode, 1]
            kept.append(
                (
                    real_part * turn_real - imag_part * turn_imag,
                    real_part * turn_imag + imag_part * turn_real,
                )
            )
    both_first = complex_product(first[1], first[0])
    both_second = complex_product(second[1], second[0])

    order = pick_matrix(
        LEVELS, lambda row: lax.bitwise_xor(row // width, seat) * width + row % width
    )

    def put_level(ref, index, real_part, imag_part):
        full = blocks(real_part, -imag_part, imag_part, real_part)
        high, low = split_value(full)
        made = blocks(high, high, low, jnp.zeros_like(low))
        if index is None:
            ref[...] = made
        else:
            ref[index] = made

    put_level(turn_ref, None, exact(both_first[0].T, order), exact(-both_first[1].T, order))
    put_level(level_ref, 0, first[1][0].T, first[1][1].T)
    put_level(level_ref, 1, exact(first[0][0], order), exact(-first[0][1], order))
    put_level(level_ref, 2, exact(order, first[0][0].T), exact(order, first[0][1].T))

    def put_lane(index, real_part, imag_part):
        real_part, imag_part = spread(real_part), spread(imag_part)
        high, low = split_value(blocks(real_part, imag_part, -imag_part, real_part))
        lane_ref[index, 0] = high
        lane_ref[index, 1] = low

    put_lane(0, *second[1])
    put_lane(1, second[0][0].T, -second[0][1].T)
    put_lane(2, *second[0])

    real_part, imag_part = spread(both_second[0].T), spread(both_second[1].T)
    full = blocks(real_part, -imag_part, -imag_part, -real_part)

    def source(row):
        chunk, rest = row // (2 * size * parts), row % (2 * size * parts)
        step, rest = rest // (2 * size), rest % (2 * size)
        half, place = rest // size, rest % size
        return half * WIDE + lax.bitwise_xor(step, seat) * share + chunk * size + place

    chosen = exact(pick_matrix(PAIR, source), full)
    high, low = split_value(chosen)
    open_ref[0] = high
    open_ref[1] = low
    high, low = split_value(chosen[:PAIR // chunks].T)
    first_ref[...] = blocks(high, low, high, jnp.zeros_like(low))


def make_weights(phases, displacements, table_slot, checkpoint, seat, parts, chunks):
    def angles(layer):
        return pl.BlockSpec(
            (None, 2, LEVELS), lambda i, slot, start, own: (slot[start[0] + layer], 0, 0)
        )

    def matrices(layer):
        return pl.BlockSpec(
            (None, 2, 2, LEVELS, LEVELS),
            lambda i, slot, start, own: (start[0] + layer, 0, 0, 0, 0),
        )

    def whole(shape):
        return pl.BlockSpec(shape, lambda i, slot, start, own: (0,) * len(shape))

    shapes = [(2 * PAIR, 2 * PAIR // chunks), (2, PAIR, PAIR), (PAIR, PAIR), (3, PAIR, PAIR), (3, 2, PAIR, PAIR)]
    return pl.pallas_call(
        functools.partial(weights_kernel, parts, chunks),
        grid_spec=pltpu.PrefetchScalarGridSpec(
            num_scalar_prefetch=3,
            grid=(1,),
            in_specs=[angles(0), angles(1), matrices(0), matrices(1)],
            out_specs=[whole(shape) for shape in shapes],
        ),
        out_shape=[jax.ShapeDtypeStruct(shape, BF16) for shape in shapes],
        compiler_params=PARAMS,
        cost_estimate=SMALL,
    )(table_slot, checkpoint, seat, phases, phases, displacements, displacements)


def open_kernel(count, waited, weight_ref, field_ref, *refs):
    both = jnp.concatenate([field_ref[0], field_ref[1]], axis=1)
    high, low = split_value(both)
    across = (((1,), (1,)), ((), ()))
    made = mxu(weight_ref[0], high, across) + (
        mxu(weight_ref[0], low, across) + mxu(weight_ref[1], high, across)
    )
    tall = made.shape[0] // count
    for place, out in enumerate(refs[waited:]):
        piece = made[place * tall:(place + 1) * tall]
        for first in range(out.shape[0]):
            out[first] = piece[:, first * WIDE:(first + 1) * WIDE]


def open_first_kernel(size, weight_ref, field_ref, *out_refs):
    levels = field_ref.shape[2] // WIDE
    rows = []
    for level in range(levels):
        place = slice(level * WIDE, (level + 1) * WIDE)
        real_high, real_low = split_value(field_ref[0, :, place])
        imag_high, imag_low = split_value(field_ref[1, :, place])
        rows.append(jnp.concatenate([real_high, imag_high, real_low, imag_low], axis=1))
    made = mxu(jnp.concatenate(rows, axis=0), weight_ref[...])
    middle = made.shape[1] // 2
    tall = 2 * size
    for level in range(levels):
        turned = made[level * WIDE:(level + 1) * WIDE].T
        turned = turned[:middle] + turned[middle:]
        for step, out in enumerate(out_refs):
            out[level * tall:(level + 1) * tall, :] = turned[step * tall:(step + 1) * tall]


def open_first(field, weights, parts, size):
    rows, cols = field.shape[1:]
    firsts = rows // WIDE
    tall = cols // WIDE * 2 * size
    outs = pl.pallas_call(
        functools.partial(open_first_kernel, size),
        grid=(firsts,),
        in_specs=[
            pl.BlockSpec(weights.shape, lambda i: (0, 0)),
            pl.BlockSpec((2, WIDE, cols), lambda i: (0, i, 0)),
        ],
        out_specs=[pl.BlockSpec((None, tall, WIDE), lambda i: (i, 0, 0))] * parts,
        out_shape=[jax.ShapeDtypeStruct((firsts, tall, WIDE), F32)] * parts,
        compiler_params=PARAMS,
        cost_estimate=SMALL,
    )(weights, field)
    return [outs]


def open_state(field, weights, parts, size, chunk_start, chunk_count, waited):
    rows, cols = field.shape[1:]
    firsts = rows // WIDE
    column_levels = cols // WIDE
    count = parts * chunk_count
    tall = count * 2 * size
    shape = jax.ShapeDtypeStruct((firsts, column_levels * 2 * size, WIDE), F32)
    weights = lax.slice_in_dim(
        weights, chunk_start * parts * 2 * size, chunk_start * parts * 2 * size + tall, axis=1
    )
    outs = pl.pallas_call(
        functools.partial(open_kernel, count, len(waited)),
        grid=(column_levels,),
        in_specs=[
            pl.BlockSpec((2, tall, PAIR), lambda i: (0, 0, 0)),
            pl.BlockSpec((2, rows, WIDE), lambda i: (0, 0, i)),
        ]
        + [pl.BlockSpec(memory_space=pl.ANY)] * len(waited),
        out_specs=[pl.BlockSpec((firsts, 2 * size, WIDE), lambda i: (0, i, 0))] * count,
        out_shape=[shape] * count,
        compiler_params=PARAMS,
        cost_estimate=SMALL,
    )(weights, field, *waited)
    return [outs[c * parts:(c + 1) * parts] for c in range(chunk_count)]


def cut_kernel(size, waited, seat_ref, field_ref, *refs):
    seat = seat_ref[0]
    levels = field_ref.shape[-1] // WIDE
    for step, out in enumerate(refs[waited:]):
        part = lax.bitwise_xor(seat, step)
        for half in range(2):
            for level in range(levels):
                start = (2 * level + half) * size
                out[start:start + size, :] = field_ref[
                    half, part, :, level * WIDE:(level + 1) * WIDE
                ]


def cut_pieces(field, seat, parts, chunk, size, waited):
    rows, cols = field.shape[1:]
    firsts = rows // WIDE
    chunks = WIDE // parts // size
    tall = cols // WIDE * 2 * size
    return pl.pallas_call(
        functools.partial(cut_kernel, size, len(waited)),
        grid=(firsts,),
        in_specs=[
            pl.BlockSpec(memory_space=pltpu.SMEM),
            pl.BlockSpec((2, None, parts, None, size, cols), lambda i: (0, i, 0, chunk, 0, 0)),
        ]
        + [pl.BlockSpec(memory_space=pl.ANY)] * len(waited),
        out_specs=[pl.BlockSpec((None, tall, WIDE), lambda i: (i, 0, 0))] * parts,
        out_shape=[jax.ShapeDtypeStruct((firsts, tall, WIDE), F32)] * parts,
        compiler_params=PARAMS,
        cost_estimate=SMALL,
    )(seat, field.reshape(2, firsts, parts, chunks, size, cols), *waited)


def level_apply(weights, real_part, imag_part):
    real_high, real_low = split_value(real_part)
    imag_high, imag_low = split_value(imag_part)
    stacked = jnp.concatenate([real_high, imag_high, real_low, imag_low], axis=0)
    made = mxu(weights, stacked)
    return made[:WIDE] + made[WIDE:]


def lane_apply(weight_ref, index, real_part, imag_part):
    high, low = split_value(jnp.concatenate([real_part, imag_part], axis=1))
    made = mxu(high, weight_ref[index, 0]) + (
        mxu(low, weight_ref[index, 0]) + mxu(high, weight_ref[index, 1])
    )
    return made[:, :WIDE], made[:, WIDE:]


def gather_levels(refs, size, half):
    columns = []
    for place in range(size):
        parts = [
            ref[pl.ds(half * size + place, ref.shape[0] // (2 * size), stride=2 * size), :]
            for ref in refs
        ]
        columns.append(jnp.concatenate(parts, axis=0) if len(parts) > 1 else parts[0])
    return jnp.concatenate(columns, axis=1)


def scatter_levels(ref, size, half, value):
    for place in range(size):
        ref[pl.ds(half * size + place, LEVELS, stride=2 * size), :] = value[
            :, place * WIDE:(place + 1) * WIDE
        ]


def turn_kernel(parts, size, weight_ref, *refs):
    pieces = refs[:parts]
    out_ref = refs[-1].reshape(LEVELS * 2 * size, WIDE)
    made = level_apply(
        weight_ref[...], gather_levels(pieces, size, 0), gather_levels(pieces, size, 1)
    )
    scatter_levels(out_ref, size, 0, made[:LEVELS])
    scatter_levels(out_ref, size, 1, made[LEVELS:])


def turn_columns(pieces, weights, size, waited):
    firsts = pieces[0].shape[0]
    parts = len(pieces)
    block = pieces[0].shape[1:]
    return pl.pallas_call(
        functools.partial(turn_kernel, parts, size),
        grid=(firsts,),
        in_specs=[pl.BlockSpec((PAIR, PAIR), lambda i: (0, 0))]
        + [pl.BlockSpec((None,) + block, lambda i: (i, 0, 0))] * parts
        + [pl.BlockSpec(memory_space=pl.ANY)] * len(waited),
        out_specs=pl.BlockSpec((LEVELS, None, 2 * size, WIDE), lambda i: (0, i, 0, 0)),
        out_shape=jax.ShapeDtypeStruct((LEVELS, firsts, 2 * size, WIDE), F32),
        compiler_params=PARAMS,
        cost_estimate=SMALL,
    )(weights, *pieces, *waited)


def halves(value, size):
    value = value.reshape(LEVELS, 2, size, WIDE)
    rows = LEVELS * size
    return value[:, 0].reshape(rows, WIDE), value[:, 1].reshape(rows, WIDE)


def join(real_part, imag_part, size):
    shape = (LEVELS, 1, size, WIDE)
    both = jnp.concatenate([real_part.reshape(shape), imag_part.reshape(shape)], axis=1)
    return both.reshape(LEVELS * 2 * size, WIDE)


def close_kernel(parts, size, lane_ref, level_ref, field_ref, *refs):
    rho_refs = refs[:parts]
    out_refs = refs[-parts - 3:-3]
    grad_ref, work_a, work_b = refs[-3:]
    step = pl.program_id(0)

    @pl.when(step == 0)
    def _():
        grad_ref[...] = jnp.zeros_like(grad_ref)

    flat = field_ref.reshape(LEVELS * 2 * size, WIDE)
    real_part, imag_part = lane_apply(lane_ref, 0, *halves(flat[...], size))
    work_a[...] = join(real_part, imag_part, size)

    rho = jnp.concatenate([ref[...] for ref in rho_refs], axis=0)
    rho_real, rho_imag = halves(rho, size)
    real_part, imag_part = lane_apply(lane_ref, 1, rho_real, rho_imag)
    work_b[...] = join(real_part, imag_part, size)

    mid = level_apply(level_ref[0], gather_levels([work_a], size, 0), gather_levels([work_a], size, 1))
    seen = level_apply(level_ref[1], gather_levels([work_b], size, 0), gather_levels([work_b], size, 1))
    terms = seen[:LEVELS] * mid[LEVELS:] - seen[LEVELS:] * mid[:LEVELS]
    total = terms[:, :WIDE]
    for place in range(1, size):
        total = total + terms[:, place * WIDE:(place + 1) * WIDE]
    grad_ref[1] += total

    last = level_apply(level_ref[2], mid[:LEVELS], mid[LEVELS:])
    scatter_levels(work_a, size, 0, last[:LEVELS])
    scatter_levels(work_a, size, 1, last[LEVELS:])
    real_part, imag_part = lane_apply(lane_ref, 2, *halves(work_a[...], size))
    terms = rho_real * imag_part - rho_imag * real_part
    grad_ref[0] += jnp.sum(terms.reshape(LEVELS, size, WIDE), axis=1)
    made = join(real_part, imag_part, size)
    rows = made.shape[0] // parts
    for part in range(parts):
        out_refs[part][...] = made[part * rows:(part + 1) * rows]


def close_columns(field, rho_pieces, lane, level, size, waited):
    total_first, firsts = field.shape[:2]
    devs = total_first // firsts
    parts = len(rho_pieces)
    rows = LEVELS * 2 * size
    field = field.reshape(devs, firsts, firsts * 2 * size, WIDE)
    piece = rho_pieces[0]
    piece_spec = pl.BlockSpec((None,) + piece.shape[1:], lambda i: (i, 0, 0))
    outs = pl.pallas_call(
        functools.partial(close_kernel, parts, size),
        grid=(firsts,),
        in_specs=[
            pl.BlockSpec(lane.shape, lambda i: (0, 0, 0, 0)),
            pl.BlockSpec(level.shape, lambda i: (0, 0, 0)),
            pl.BlockSpec((devs, None, firsts * 2 * size, WIDE), lambda i: (0, i, 0, 0)),
        ]
        + [piece_spec] * parts
        + [pl.BlockSpec(memory_space=pl.ANY)] * len(waited),
        out_specs=[piece_spec] * parts + [pl.BlockSpec((2, LEVELS, WIDE), lambda i: (0, 0, 0))],
        out_shape=[jax.ShapeDtypeStruct(piece.shape, F32)] * parts
        + [jax.ShapeDtypeStruct((2, LEVELS, WIDE), F32)],
        scratch_shapes=[pltpu.VMEM((rows, WIDE), F32), pltpu.VMEM((rows, WIDE), F32)],
        compiler_params=PARAMS,
        cost_estimate=LARGE,
    )(lane, level, field, *rho_pieces, *waited)
    return list(outs[:parts]), outs[parts]


def place_kernel(parts, size, aliased, seat_ref, *refs):
    pieces = refs[:parts]
    out_ref = refs[parts + aliased]
    seat = seat_ref[0]
    levels = pieces[0].shape[0] // (2 * size)
    for step in range(parts):
        part = lax.bitwise_xor(seat, step)
        for half in range(2):
            for level in range(levels):
                start = level * 2 * size + half * size
                out_ref[half, part, :, level * WIDE:(level + 1) * WIDE] = pieces[step][
                    start:start + size, :
                ]


def place_pieces(pieces, seat, held, chunk, shape, size):
    parts = len(pieces)
    firsts, chunks = shape[1], shape[3]
    aliased = 0 if held is None else 1
    piece = pieces[0]
    cols = shape[-1]
    return pl.pallas_call(
        functools.partial(place_kernel, parts, size, aliased),
        grid=(firsts,),
        in_specs=[pl.BlockSpec(memory_space=pltpu.SMEM)]
        + [pl.BlockSpec((None,) + piece.shape[1:], lambda i: (i, 0, 0))] * parts
        + [pl.BlockSpec(memory_space=pl.ANY)] * aliased,
        out_specs=pl.BlockSpec(
            (2, None, parts, None, size, cols), lambda i: (0, i, 0, chunk, 0, 0)
        ),
        out_shape=jax.ShapeDtypeStruct(shape, F32),
        input_output_aliases={parts + 1: 0} if aliased else {},
        compiler_params=PARAMS,
        cost_estimate=SMALL,
    )(seat, *pieces, *([held] if aliased else []))


def swap(pieces, parts):
    moved = [pieces[0]]
    for step in range(1, parts):
        pairs = [(member, member ^ step) for member in range(parts)]
        moved.append(lax.ppermute(pieces[step], "grp", pairs))
    return moved


def grad_kernel(parts, count, seat_ref, *refs):
    out_ref = refs[-1]
    grad = refs[0][...]
    for ref in refs[1:count]:
        grad = grad + ref[...]
    grad = -2.0 * grad
    width = LEVELS // parts
    order = pick_matrix(
        LEVELS, lambda row: lax.bitwise_xor(row // width, seat_ref[0]) * width + row % width
    )
    fold = (grid_of((WIDE, LEVELS), 0) // TRANSMON == grid_of((WIDE, LEVELS), 1)).astype(F32)
    for layer in range(2):
        firsts = exact(jnp.ones((8, WIDE), F32), grad[layer], (((1,), (1,)), ((), ())))
        if layer == 0:
            firsts = exact(firsts, order)
        seconds = exact(exact(jnp.ones((8, LEVELS), F32), grad[layer]), fold)
        out_ref[2 * layer:2 * layer + 1, :] = firsts[:1]
        out_ref[2 * layer + 1:2 * layer + 2, :] = seconds[:1]


def device_grad(grads, seat, parts, waited):
    return pl.pallas_call(
        functools.partial(grad_kernel, parts, len(grads)),
        in_specs=[pl.BlockSpec(memory_space=pltpu.SMEM)]
        + [pl.BlockSpec(memory_space=pltpu.VMEM)] * len(grads)
        + [pl.BlockSpec(memory_space=pl.ANY)] * len(waited),
        out_specs=pl.BlockSpec(memory_space=pltpu.VMEM),
        out_shape=jax.ShapeDtypeStruct((4, LEVELS), F32),
        compiler_params=PARAMS,
        cost_estimate=SMALL,
    )(seat, *grads, *waited)


def grand_total(value):
    rounds = []
    for axis in ("grp", "dev"):
        count = lax.axis_size(axis)
        rounds.append([(axis, 1 << bit, count) for bit in range(count.bit_length() - 1)])
    for axis, step, count in rounds[0][:1] + rounds[1] + rounds[0][1:]:
        pairs = [(member, member ^ step) for member in range(count)]
        value = value + lax.ppermute(value, axis, pairs)
    return value


def per_device(density, costate, phases, displacements, table_slot, checkpoint):
    parts = lax.axis_size("grp")
    share = WIDE // parts
    chunks = max(1, min(4, share // 8))
    size = share // chunks
    seat = lax.axis_index("grp").astype(jnp.int32)
    seats = seat.reshape(1)
    rows, cols = costate.shape[1:]

    opened_first, opened, turned_by, level, lane = make_weights(
        phases, displacements, table_slot, checkpoint, seats, parts, chunks
    )
    state_cut = open_first(costate, opened_first, parts, size)
    if chunks > 1:
        state_cut += open_state(
            costate, opened, parts, size, 1, chunks - 1, list(state_cut[0][:1])
        )
    rho = [
        cut_pieces(density, seats, parts, chunk, size, list(state_cut[-1][:1]))
        for chunk in range(chunks)
    ]
    state = [swap(pieces, parts) for pieces in state_cut[:3]]
    rho_there = [swap(pieces, parts) for pieces in rho]

    shape = (2, rows // WIDE, parts, chunks, size, cols)
    fields, closed, made, grads = [], [], [], []

    def close(chunk, waited):
        if chunk > 0:
            waited = waited + closed[chunk - 1][:1]
        out, grad = close_columns(
            fields[chunk], rho_there[chunk], lane, level, size, waited
        )
        closed.append(out)
        if chunk == chunks - 2 and chunk > 0:
            out, rho_there[-1] = lax.optimization_barrier((out, rho_there[-1]))
        if chunk == chunks - 1 and chunk > 1:
            out, made[-1] = lax.optimization_barrier((out, made[-1]))
        made.append(swap(out, parts))
        grads.append(grad)

    for chunk in range(chunks):
        waited = [rho[chunk][0]]
        if chunk > 0:
            waited.append(field)
        if chunk > 1:
            close(chunk - 2, [])
            waited += closed[chunk - 2][:1]
        field = turn_columns(state[chunk], turned_by, size, waited)
        if chunk + 1 == len(state) < chunks:
            pieces, field = lax.optimization_barrier((state_cut[chunk + 1], field))
            state.append(swap(pieces, parts))
        fields.append(lax.all_to_all(field, "dev", split_axis=0, concat_axis=0, tiled=True))
    whole = None
    for chunk in range(chunks):
        while len(made) < min(chunk + 2, chunks):
            waited = list(made[-2][1:]) if len(made) > 1 else []
            close(len(made), [whole] if 0 < chunk == chunks - 2 else waited)
        whole = place_pieces(made[chunk], seats, whole, chunk, shape, size)
    grad = grand_total(device_grad(grads, seats, parts, []))
    return whole.reshape(costate.shape), grad.reshape(2, 2, LEVELS)


def solution(mesh):
    return jax.shard_map(
        per_device,
        mesh=mesh,
        in_specs=(P(None, "dev", "grp"), P(None, "dev", "grp"), P(), P(), P(), P()),
        out_specs=(P(None, "dev", "grp"), P()),
        check_vma=False,
    )
```

```python
import functools

import jax
import jax.numpy as jnp
from jax import lax
from jax.experimental import pallas as pl
from jax.experimental.pallas import tpu as pltpu
from jax.sharding import PartitionSpec as P

LEVELS = 64
TRANSMON = 2
WIDE = LEVELS * TRANSMON
PAIR = 2 * WIDE
HIGH = lax.Precision.HIGHEST
F32 = jnp.float32
BF16 = jnp.bfloat16
SMALL = pl.CostEstimate(flops=1024, bytes_accessed=1024, transcendentals=0)
LARGE = pl.CostEstimate(flops=2 * 10**11, bytes_accessed=1024, transcendentals=0)
PARAMS = pltpu.CompilerParams(vmem_limit_bytes=60 * 1024 * 1024)


def split_value(value):
    high = value.astype(BF16)
    low = (value - high.astype(F32)).astype(BF16)
    return high, low


def mxu(left, right, dims=(((1,), (0,)), ((), ()))):
    return lax.dot_general(left, right, dims, preferred_element_type=F32)


def exact(left, right, dims=(((1,), (0,)), ((), ()))):
    return lax.dot_general(left, right, dims, precision=HIGH, preferred_element_type=F32)


def grid_of(shape, dim):
    return lax.broadcasted_iota(jnp.int32, shape, dim)


def pick_matrix(count, chosen):
    shape = (count, count)
    return (chosen(grid_of(shape, 0)) == grid_of(shape, 1)).astype(F32)


def spread(matrix):
    tall = (grid_of((WIDE, LEVELS), 0) // TRANSMON == grid_of((WIDE, LEVELS), 1)).astype(F32)
    long = (grid_of((LEVELS, WIDE), 1) // TRANSMON == grid_of((LEVELS, WIDE), 0)).astype(F32)
    same = grid_of((WIDE, WIDE), 0) % TRANSMON == grid_of((WIDE, WIDE), 1) % TRANSMON
    return jnp.where(same, exact(exact(tall, matrix), long), 0.0)


def blocks(upper_left, upper_right, lower_left, lower_right):
    return jnp.concatenate(
        [
            jnp.concatenate([upper_left, upper_right], axis=1),
            jnp.concatenate([lower_left, lower_right], axis=1),
        ],
        axis=0,
    )


def complex_product(left, right):
    return (
        exact(left[0], right[0]) - exact(left[1], right[1]),
        exact(left[0], right[1]) + exact(left[1], right[0]),
    )


def weights_kernel(parts, chunks, slot_ref, start_ref, seat_ref, *refs):
    angle_refs, matrix_refs = refs[0:2], refs[2:4]
    first_ref, open_ref, turn_ref, level_ref, lane_ref = refs[-5:]
    seat = seat_ref[0]
    width = LEVELS // parts
    share = WIDE // parts
    size = share // chunks
    first, second = [], []
    for layer in range(2):
        cosine = jnp.cos(angle_refs[layer][...])
        sine = jnp.sin(angle_refs[layer][...])
        for mode, kept in enumerate((first, second)):
            turn_real, turn_imag = cosine[mode:mode + 1], sine[mode:mode + 1]
            real_part = matrix_refs[layer][mode, 0]
            imag_part = matrix_refs[layer][mode, 1]
            kept.append(
                (
                    real_part * turn_real - imag_part * turn_imag,
                    real_part * turn_imag + imag_part * turn_real,
                )
            )
    both_first = complex_product(first[1], first[0])
    both_second = complex_product(second[1], second[0])

    order = pick_matrix(
        LEVELS, lambda row: lax.bitwise_xor(row // width, seat) * width + row % width
    )

    def put_level(ref, index, real_part, imag_part):
        full = blocks(real_part, -imag_part, imag_part, real_part)
        high, low = split_value(full)
        made = blocks(high, high, low, jnp.zeros_like(low))
        if index is None:
            ref[...] = made
        else:
            ref[index] = made

    put_level(turn_ref, None, exact(both_first[0].T, order), exact(-both_first[1].T, order))
    put_level(level_ref, 0, first[1][0].T, first[1][1].T)
    put_level(level_ref, 1, exact(first[0][0], order), exact(-first[0][1], order))
    put_level(level_ref, 2, exact(order, first[0][0].T), exact(order, first[0][1].T))

    def put_lane(index, real_part, imag_part):
        real_part, imag_part = spread(real_part), spread(imag_part)
        high, low = split_value(blocks(real_part, imag_part, -imag_part, real_part))
        lane_ref[index, 0] = high
        lane_ref[index, 1] = low

    put_lane(0, *second[1])
    put_lane(1, second[0][0].T, -second[0][1].T)
    put_lane(2, *second[0])

    real_part, imag_part = spread(both_second[0].T), spread(both_second[1].T)
    full = blocks(real_part, -imag_part, -imag_part, -real_part)

    def source(row):
        chunk, rest = row // (2 * size * parts), row % (2 * size * parts)
        step, rest = rest // (2 * size), rest % (2 * size)
        half, place = rest // size, rest % size
        return half * WIDE + lax.bitwise_xor(step, seat) * share + chunk * size + place

    chosen = exact(pick_matrix(PAIR, source), full)
    high, low = split_value(chosen)
    open_ref[0] = high
    open_ref[1] = low
    high, low = split_value(chosen[:PAIR // chunks].T)
    first_ref[...] = blocks(high, low, high, jnp.zeros_like(low))


def make_weights(phases, displacements, table_slot, checkpoint, seat, parts, chunks):
    def angles(layer):
        return pl.BlockSpec(
            (None, 2, LEVELS), lambda i, slot, start, own: (slot[start[0] + layer], 0, 0)
        )

    def matrices(layer):
        return pl.BlockSpec(
            (None, 2, 2, LEVELS, LEVELS),
            lambda i, slot, start, own: (start[0] + layer, 0, 0, 0, 0),
        )

    def whole(shape):
        return pl.BlockSpec(shape, lambda i, slot, start, own: (0,) * len(shape))

    shapes = [(2 * PAIR, 2 * PAIR // chunks), (2, PAIR, PAIR), (PAIR, PAIR), (3, PAIR, PAIR), (3, 2, PAIR, PAIR)]
    return pl.pallas_call(
        functools.partial(weights_kernel, parts, chunks),
        grid_spec=pltpu.PrefetchScalarGridSpec(
            num_scalar_prefetch=3,
            grid=(1,),
            in_specs=[angles(0), angles(1), matrices(0), matrices(1)],
            out_specs=[whole(shape) for shape in shapes],
        ),
        out_shape=[jax.ShapeDtypeStruct(shape, BF16) for shape in shapes],
        compiler_params=PARAMS,
        cost_estimate=SMALL,
    )(table_slot, checkpoint, seat, phases, phases, displacements, displacements)


def open_kernel(count, waited, weight_ref, field_ref, *refs):
    both = jnp.concatenate([field_ref[0], field_ref[1]], axis=1)
    high, low = split_value(both)
    across = (((1,), (1,)), ((), ()))
    made = mxu(weight_ref[0], high, across) + (
        mxu(weight_ref[0], low, across) + mxu(weight_ref[1], high, across)
    )
    tall = made.shape[0] // count
    for place, out in enumerate(refs[waited:]):
        piece = made[place * tall:(place + 1) * tall]
        for first in range(out.shape[0]):
            out[first] = piece[:, first * WIDE:(first + 1) * WIDE]


def open_first_kernel(size, weight_ref, field_ref, *out_refs):
    levels = field_ref.shape[2] // WIDE
    rows = []
    for level in range(levels):
        place = slice(level * WIDE, (level + 1) * WIDE)
        real_high, real_low = split_value(field_ref[0, :, place])
        imag_high, imag_low = split_value(field_ref[1, :, place])
        rows.append(jnp.concatenate([real_high, imag_high, real_low, imag_low], axis=1))
    made = mxu(jnp.concatenate(rows, axis=0), weight_ref[...])
    middle = made.shape[1] // 2
    tall = 2 * size
    for level in range(levels):
        turned = made[level * WIDE:(level + 1) * WIDE].T
        turned = turned[:middle] + turned[middle:]
        for step, out in enumerate(out_refs):
            out[level * tall:(level + 1) * tall, :] = turned[step * tall:(step + 1) * tall]


def open_first(field, weights, parts, size):
    rows, cols = field.shape[1:]
    firsts = rows // WIDE
    tall = cols // WIDE * 2 * size
    outs = pl.pallas_call(
        functools.partial(open_first_kernel, size),
        grid=(firsts,),
        in_specs=[
            pl.BlockSpec(weights.shape, lambda i: (0, 0)),
            pl.BlockSpec((2, WIDE, cols), lambda i: (0, i, 0)),
        ],
        out_specs=[pl.BlockSpec((None, tall, WIDE), lambda i: (i, 0, 0))] * parts,
        out_shape=[jax.ShapeDtypeStruct((firsts, tall, WIDE), F32)] * parts,
        compiler_params=PARAMS,
        cost_estimate=SMALL,
    )(weights, field)
    return [outs]


def open_state(field, weights, parts, size, chunk_start, chunk_count, waited):
    rows, cols = field.shape[1:]
    firsts = rows // WIDE
    column_levels = cols // WIDE
    count = parts * chunk_count
    tall = count * 2 * size
    shape = jax.ShapeDtypeStruct((firsts, column_levels * 2 * size, WIDE), F32)
    weights = lax.slice_in_dim(
        weights, chunk_start * parts * 2 * size, chunk_start * parts * 2 * size + tall, axis=1
    )
    outs = pl.pallas_call(
        functools.partial(open_kernel, count, len(waited)),
        grid=(column_levels,),
        in_specs=[
            pl.BlockSpec((2, tall, PAIR), lambda i: (0, 0, 0)),
            pl.BlockSpec((2, rows, WIDE), lambda i: (0, 0, i)),
        ]
        + [pl.BlockSpec(memory_space=pl.ANY)] * len(waited),
        out_specs=[pl.BlockSpec((firsts, 2 * size, WIDE), lambda i: (0, i, 0))] * count,
        out_shape=[shape] * count,
        compiler_params=PARAMS,
        cost_estimate=SMALL,
    )(weights, field, *waited)
    return [outs[c * parts:(c + 1) * parts] for c in range(chunk_count)]


def cut_kernel(size, waited, seat_ref, field_ref, *refs):
    seat = seat_ref[0]
    levels = field_ref.shape[-1] // WIDE
    for step, out in enumerate(refs[waited:]):
        part = lax.bitwise_xor(seat, step)
        for half in range(2):
            for level in range(levels):
                start = (2 * level + half) * size
                out[start:start + size, :] = field_ref[
                    half, part, :, level * WIDE:(level + 1) * WIDE
                ]


def cut_pieces(field, seat, parts, chunk, size, waited):
    rows, cols = field.shape[1:]
    firsts = rows // WIDE
    chunks = WIDE // parts // size
    tall = cols // WIDE * 2 * size
    return pl.pallas_call(
        functools.partial(cut_kernel, size, len(waited)),
        grid=(firsts,),
        in_specs=[
            pl.BlockSpec(memory_space=pltpu.SMEM),
            pl.BlockSpec((2, None, parts, None, size, cols), lambda i: (0, i, 0, chunk, 0, 0)),
        ]
        + [pl.BlockSpec(memory_space=pl.ANY)] * len(waited),
        out_specs=[pl.BlockSpec((None, tall, WIDE), lambda i: (i, 0, 0))] * parts,
        out_shape=[jax.ShapeDtypeStruct((firsts, tall, WIDE), F32)] * parts,
        compiler_params=PARAMS,
        cost_estimate=SMALL,
    )(seat, field.reshape(2, firsts, parts, chunks, size, cols), *waited)


def level_apply(weights, real_part, imag_part):
    real_high, real_low = split_value(real_part)
    imag_high, imag_low = split_value(imag_part)
    stacked = jnp.concatenate([real_high, imag_high, real_low, imag_low], axis=0)
    made = mxu(weights, stacked)
    return made[:WIDE] + made[WIDE:]


def lane_apply(weight_ref, index, real_part, imag_part):
    high, low = split_value(jnp.concatenate([real_part, imag_part], axis=1))
    made = mxu(high, weight_ref[index, 0]) + (
        mxu(low, weight_ref[index, 0]) + mxu(high, weight_ref[index, 1])
    )
    return made[:, :WIDE], made[:, WIDE:]


def gather_levels(refs, size, half):
    columns = []
    for place in range(size):
        parts = [
            ref[pl.ds(half * size + place, ref.shape[0] // (2 * size), stride=2 * size), :]
            for ref in refs
        ]
        columns.append(jnp.concatenate(parts, axis=0) if len(parts) > 1 else parts[0])
    return jnp.concatenate(columns, axis=1)


def scatter_levels(ref, size, half, value):
    for place in range(size):
        ref[pl.ds(half * size + place, LEVELS, stride=2 * size), :] = value[
            :, place * WIDE:(place + 1) * WIDE
        ]


def turn_kernel(parts, size, weight_ref, *refs):
    pieces = refs[:parts]
    out_ref = refs[-1].reshape(LEVELS * 2 * size, WIDE)
    made = level_apply(
        weight_ref[...], gather_levels(pieces, size, 0), gather_levels(pieces, size, 1)
    )
    scatter_levels(out_ref, size, 0, made[:LEVELS])
    scatter_levels(out_ref, size, 1, made[LEVELS:])


def turn_columns(pieces, weights, size, waited):
    firsts = pieces[0].shape[0]
    parts = len(pieces)
    block = pieces[0].shape[1:]
    return pl.pallas_call(
        functools.partial(turn_kernel, parts, size),
        grid=(firsts,),
        in_specs=[pl.BlockSpec((PAIR, PAIR), lambda i: (0, 0))]
        + [pl.BlockSpec((None,) + block, lambda i: (i, 0, 0))] * parts
        + [pl.BlockSpec(memory_space=pl.ANY)] * len(waited),
        out_specs=pl.BlockSpec((LEVELS, None, 2 * size, WIDE), lambda i: (0, i, 0, 0)),
        out_shape=jax.ShapeDtypeStruct((LEVELS, firsts, 2 * size, WIDE), F32),
        compiler_params=PARAMS,
        cost_estimate=SMALL,
    )(weights, *pieces, *waited)


def halves(value, size):
    value = value.reshape(LEVELS, 2, size, WIDE)
    rows = LEVELS * size
    return value[:, 0].reshape(rows, WIDE), value[:, 1].reshape(rows, WIDE)


def join(real_part, imag_part, size):
    shape = (LEVELS, 1, size, WIDE)
    both = jnp.concatenate([real_part.reshape(shape), imag_part.reshape(shape)], axis=1)
    return both.reshape(LEVELS * 2 * size, WIDE)


def close_kernel(parts, size, lane_ref, level_ref, field_ref, *refs):
    rho_refs = refs[:parts]
    out_refs = refs[-parts - 3:-3]
    grad_ref, work_a, work_b = refs[-3:]
    step = pl.program_id(0)

    @pl.when(step == 0)
    def _():
        grad_ref[...] = jnp.zeros_like(grad_ref)

    flat = field_ref.reshape(LEVELS * 2 * size, WIDE)
    real_part, imag_part = lane_apply(lane_ref, 0, *halves(flat[...], size))
    work_a[...] = join(real_part, imag_part, size)

    rho = jnp.concatenate([ref[...] for ref in rho_refs], axis=0)
    rho_real, rho_imag = halves(rho, size)
    real_part, imag_part = lane_apply(lane_ref, 1, rho_real, rho_imag)
    work_b[...] = join(real_part, imag_part, size)

    mid = level_apply(level_ref[0], gather_levels([work_a], size, 0), gather_levels([work_a], size, 1))
    seen = level_apply(level_ref[1], gather_levels([work_b], size, 0), gather_levels([work_b], size, 1))
    terms = seen[:LEVELS] * mid[LEVELS:] - seen[LEVELS:] * mid[:LEVELS]
    total = terms[:, :WIDE]
    for place in range(1, size):
        total = total + terms[:, place * WIDE:(place + 1) * WIDE]
    grad_ref[1] += total

    last = level_apply(level_ref[2], mid[:LEVELS], mid[LEVELS:])
    scatter_levels(work_a, size, 0, last[:LEVELS])
    scatter_levels(work_a, size, 1, last[LEVELS:])
    real_part, imag_part = lane_apply(lane_ref, 2, *halves(work_a[...], size))
    terms = rho_real * imag_part - rho_imag * real_part
    grad_ref[0] += jnp.sum(terms.reshape(LEVELS, size, WIDE), axis=1)
    made = join(real_part, imag_part, size)
    rows = made.shape[0] // parts
    for part in range(parts):
        out_refs[part][...] = made[part * rows:(part + 1) * rows]


def close_columns(field, rho_pieces, lane, level, size, waited):
    total_first, firsts = field.shape[:2]
    devs = total_first // firsts
    parts = len(rho_pieces)
    rows = LEVELS * 2 * size
    field = field.reshape(devs, firsts, firsts * 2 * size, WIDE)
    piece = rho_pieces[0]
    piece_spec = pl.BlockSpec((None,) + piece.shape[1:], lambda i: (i, 0, 0))
    outs = pl.pallas_call(
        functools.partial(close_kernel, parts, size),
        grid=(firsts,),
        in_specs=[
            pl.BlockSpec(lane.shape, lambda i: (0, 0, 0, 0)),
            pl.BlockSpec(level.shape, lambda i: (0, 0, 0)),
            pl.BlockSpec((devs, None, firsts * 2 * size, WIDE), lambda i: (0, i, 0, 0)),
        ]
        + [piece_spec] * parts
        + [pl.BlockSpec(memory_space=pl.ANY)] * len(waited),
        out_specs=[piece_spec] * parts + [pl.BlockSpec((2, LEVELS, WIDE), lambda i: (0, 0, 0))],
        out_shape=[jax.ShapeDtypeStruct(piece.shape, F32)] * parts
        + [jax.ShapeDtypeStruct((2, LEVELS, WIDE), F32)],
        scratch_shapes=[pltpu.VMEM((rows, WIDE), F32), pltpu.VMEM((rows, WIDE), F32)],
        compiler_params=PARAMS,
        cost_estimate=LARGE,
    )(lane, level, field, *rho_pieces, *waited)
    return list(outs[:parts]), outs[parts]


def place_kernel(parts, size, aliased, seat_ref, *refs):
    pieces = refs[:parts]
    out_ref = refs[parts + aliased]
    seat = seat_ref[0]
    levels = pieces[0].shape[0] // (2 * size)
    for step in range(parts):
        part = lax.bitwise_xor(seat, step)
        for half in range(2):
            for level in range(levels):
                start = level * 2 * size + half * size
                out_ref[half, part, :, level * WIDE:(level + 1) * WIDE] = pieces[step][
                    start:start + size, :
                ]


def place_pieces(pieces, seat, held, chunk, shape, size):
    parts = len(pieces)
    firsts, chunks = shape[1], shape[3]
    aliased = 0 if held is None else 1
    piece = pieces[0]
    cols = shape[-1]
    return pl.pallas_call(
        functools.partial(place_kernel, parts, size, aliased),
        grid=(firsts,),
        in_specs=[pl.BlockSpec(memory_space=pltpu.SMEM)]
        + [pl.BlockSpec((None,) + piece.shape[1:], lambda i: (i, 0, 0))] * parts
        + [pl.BlockSpec(memory_space=pl.ANY)] * aliased,
        out_specs=pl.BlockSpec(
            (2, None, parts, None, size, cols), lambda i: (0, i, 0, chunk, 0, 0)
        ),
        out_shape=jax.ShapeDtypeStruct(shape, F32),
        input_output_aliases={parts + 1: 0} if aliased else {},
        compiler_params=PARAMS,
        cost_estimate=SMALL,
    )(seat, *pieces, *([held] if aliased else []))


def place_one_kernel(size, seat_ref, piece_ref, held_ref, out_ref):
    del seat_ref, held_ref
    for half in range(2):
        for level in range(out_ref.shape[-1] // WIDE):
            start = (2 * level + half) * size
            out_ref[half, :, level * WIDE:(level + 1) * WIDE] = piece_ref[start:start + size, :]


def place_one(piece, seat, held, chunk, step, shape, size):
    cols = shape[-1]
    return pl.pallas_call(
        functools.partial(place_one_kernel, size),
        grid_spec=pltpu.PrefetchScalarGridSpec(
            num_scalar_prefetch=1,
            grid=(shape[1],),
            in_specs=[
                pl.BlockSpec((None,) + piece.shape[1:], lambda i, own: (i, 0, 0)),
                pl.BlockSpec(memory_space=pl.ANY),
            ],
            out_specs=pl.BlockSpec(
                (2, None, None, None, size, cols),
                lambda i, own: (0, i, lax.bitwise_xor(own[0], step), chunk, 0, 0),
            ),
        ),
        out_shape=jax.ShapeDtypeStruct(shape, F32),
        input_output_aliases={2: 0},
        compiler_params=PARAMS,
        cost_estimate=SMALL,
    )(seat, piece, held)


def swap(pieces, parts):
    moved = [pieces[0]]
    for step in range(1, parts):
        pairs = [(member, member ^ step) for member in range(parts)]
        moved.append(lax.ppermute(pieces[step], "grp", pairs))
    return moved


def grad_kernel(parts, count, seat_ref, *refs):
    out_ref = refs[-1]
    grad = refs[0][...]
    for ref in refs[1:count]:
        grad = grad + ref[...]
    grad = -2.0 * grad
    width = LEVELS // parts
    order = pick_matrix(
        LEVELS, lambda row: lax.bitwise_xor(row // width, seat_ref[0]) * width + row % width
    )
    fold = (grid_of((WIDE, LEVELS), 0) // TRANSMON == grid_of((WIDE, LEVELS), 1)).astype(F32)
    for layer in range(2):
        firsts = exact(jnp.ones((8, WIDE), F32), grad[layer], (((1,), (1,)), ((), ())))
        if layer == 0:
            firsts = exact(firsts, order)
        seconds = exact(exact(jnp.ones((8, LEVELS), F32), grad[layer]), fold)
        out_ref[2 * layer:2 * layer + 1, :] = firsts[:1]
        out_ref[2 * layer + 1:2 * layer + 2, :] = seconds[:1]


def device_grad(grads, seat, parts, waited):
    return pl.pallas_call(
        functools.partial(grad_kernel, parts, len(grads)),
        in_specs=[pl.BlockSpec(memory_space=pltpu.SMEM)]
        + [pl.BlockSpec(memory_space=pltpu.VMEM)] * len(grads)
        + [pl.BlockSpec(memory_space=pl.ANY)] * len(waited),
        out_specs=pl.BlockSpec(memory_space=pltpu.VMEM),
        out_shape=jax.ShapeDtypeStruct((4, LEVELS), F32),
        compiler_params=PARAMS,
        cost_estimate=SMALL,
    )(seat, *grads, *waited)


def grand_total(value):
    rounds = []
    for axis in ("grp", "dev"):
        count = lax.axis_size(axis)
        rounds.append([(axis, 1 << bit, count) for bit in range(count.bit_length() - 1)])
    for axis, step, count in rounds[0][:1] + rounds[1] + rounds[0][1:]:
        pairs = [(member, member ^ step) for member in range(count)]
        value = value + lax.ppermute(value, axis, pairs)
    return value


def per_device(density, costate, phases, displacements, table_slot, checkpoint):
    parts = lax.axis_size("grp")
    share = WIDE // parts
    chunks = max(1, min(4, share // 8))
    size = share // chunks
    seat = lax.axis_index("grp").astype(jnp.int32)
    seats = seat.reshape(1)
    rows, cols = costate.shape[1:]

    opened_first, opened, turned_by, level, lane = make_weights(
        phases, displacements, table_slot, checkpoint, seats, parts, chunks
    )
    state_cut = open_first(costate, opened_first, parts, size)
    if chunks > 1:
        state_cut += open_state(
            costate, opened, parts, size, 1, chunks - 1, list(state_cut[0][:1])
        )
    rho = [
        cut_pieces(density, seats, parts, chunk, size, list(state_cut[-1][:1]) if chunk else [])
        for chunk in range(chunks)
    ]
    rho_there = [swap(pieces, parts) for pieces in rho]
    ahead = parts // 2
    state_cut[0], rho_there[0][ahead] = lax.optimization_barrier(
        (state_cut[0], rho_there[0][ahead])
    )
    state = [swap(pieces, parts) for pieces in state_cut[:3]]

    shape = (2, rows // WIDE, parts, chunks, size, cols)
    fields, closed, made, grads = [], [], [], []

    def close(chunk, waited):
        if chunk > 0:
            waited = waited + closed[chunk - 1][:1]
        out, grad = close_columns(
            fields[chunk], rho_there[chunk], lane, level, size, waited
        )
        closed.append(out)
        if chunk == chunks - 2 and chunk > 0:
            out, rho_there[-1] = lax.optimization_barrier((out, rho_there[-1]))
        if chunk == chunks - 1 and chunk > 1:
            out, made[-1] = lax.optimization_barrier((out, made[-1]))
        if chunk > 0 or chunks < 4:
            made.append(swap(out, parts))
        grads.append(grad)

    for chunk in range(chunks):
        waited = [rho[chunk][0]]
        if chunk > 0:
            waited.append(field)
        if chunk > 1:
            close(chunk - 2, [])
            waited += closed[chunk - 2][:1]
        field = turn_columns(state[chunk], turned_by, size, waited)
        if chunk + 1 == len(state) < chunks:
            pieces, field = lax.optimization_barrier((state_cut[chunk + 1], field))
            state.append(swap(pieces, parts))
            out, state[-1] = lax.optimization_barrier((closed[0], state[-1]))
            made.append(swap(out, parts))
        fields.append(lax.all_to_all(field, "dev", split_axis=0, concat_axis=0, tiled=True))
    whole = None
    for chunk in range(chunks):
        while len(made) < min(chunk + 2, chunks):
            waited = list(made[-2][1:]) if len(made) > 1 else []
            close(len(made), [whole] if 0 < chunk == chunks - 2 else waited)
        if chunk < chunks - 1 or whole is None:
            whole = place_pieces(made[chunk], seats, whole, chunk, shape, size)
        else:
            for step in range(parts):
                whole = place_one(made[chunk][step], seats, whole, chunk, step, shape, size)
    grad = grand_total(device_grad(grads, seats, parts, []))
    return whole.reshape(costate.shape), grad.reshape(2, 2, LEVELS)


def solution(mesh):
    return jax.shard_map(
        per_device,
        mesh=mesh,
        in_specs=(P(None, "dev", "grp"), P(None, "dev", "grp"), P(), P(), P(), P()),
        out_specs=(P(None, "dev", "grp"), P()),
        check_vma=False,
    )
```

```python
import functools

import jax
import jax.numpy as jnp
from jax import lax
from jax.experimental import pallas as pl
from jax.experimental.pallas import tpu as pltpu
from jax.sharding import PartitionSpec as P

LEVELS = 64
TRANSMON = 2
GROUP = 4
WIDE = LEVELS * TRANSMON
PAIR = 2 * WIDE
HIGH = lax.Precision.HIGHEST
F32 = jnp.float32
BF16 = jnp.bfloat16
SMALL = pl.CostEstimate(flops=1024, bytes_accessed=1024, transcendentals=0)
LARGE = pl.CostEstimate(flops=2 * 10**11, bytes_accessed=1024, transcendentals=0)
PARAMS = pltpu.CompilerParams(vmem_limit_bytes=60 * 1024 * 1024)


def split_value(value):
    high = value.astype(BF16)
    low = (value - high.astype(F32)).astype(BF16)
    return high, low


def mxu(left, right, dims=(((1,), (0,)), ((), ()))):
    return lax.dot_general(left, right, dims, preferred_element_type=F32)


def exact(left, right, dims=(((1,), (0,)), ((), ()))):
    return lax.dot_general(left, right, dims, precision=HIGH, preferred_element_type=F32)


def grid_of(shape, dim):
    return lax.broadcasted_iota(jnp.int32, shape, dim)


def pick_matrix(count, chosen):
    shape = (count, count)
    return (chosen(grid_of(shape, 0)) == grid_of(shape, 1)).astype(F32)


def spread(matrix):
    tall = (grid_of((WIDE, LEVELS), 0) // TRANSMON == grid_of((WIDE, LEVELS), 1)).astype(F32)
    long = (grid_of((LEVELS, WIDE), 1) // TRANSMON == grid_of((LEVELS, WIDE), 0)).astype(F32)
    same = grid_of((WIDE, WIDE), 0) % TRANSMON == grid_of((WIDE, WIDE), 1) % TRANSMON
    return jnp.where(same, exact(exact(tall, matrix), long), 0.0)


def blocks(upper_left, upper_right, lower_left, lower_right):
    return jnp.concatenate(
        [
            jnp.concatenate([upper_left, upper_right], axis=1),
            jnp.concatenate([lower_left, lower_right], axis=1),
        ],
        axis=0,
    )


def complex_product(left, right):
    return (
        exact(left[0], right[0]) - exact(left[1], right[1]),
        exact(left[0], right[1]) + exact(left[1], right[0]),
    )


def weights_kernel(parts, chunks, slot_ref, start_ref, seat_ref, *refs):
    angle_refs, matrix_refs = refs[0:2], refs[2:4]
    first_ref, open_ref, turn_ref, level_ref, lane_ref = refs[-5:]
    seat = seat_ref[0]
    width = LEVELS // parts
    share = WIDE // parts
    size = share // chunks
    first, second = [], []
    for layer in range(2):
        cosine = jnp.cos(angle_refs[layer][...])
        sine = jnp.sin(angle_refs[layer][...])
        for mode, kept in enumerate((first, second)):
            turn_real, turn_imag = cosine[mode:mode + 1], sine[mode:mode + 1]
            real_part = matrix_refs[layer][mode, 0]
            imag_part = matrix_refs[layer][mode, 1]
            kept.append(
                (
                    real_part * turn_real - imag_part * turn_imag,
                    real_part * turn_imag + imag_part * turn_real,
                )
            )
    both_first = complex_product(first[1], first[0])
    both_second = complex_product(second[1], second[0])

    order = pick_matrix(
        LEVELS, lambda row: lax.bitwise_xor(row // width, seat) * width + row % width
    )

    def put_level(ref, index, real_part, imag_part):
        full = blocks(real_part, -imag_part, imag_part, real_part)
        high, low = split_value(full)
        made = blocks(high, high, low, jnp.zeros_like(low))
        if index is None:
            ref[...] = made
        else:
            ref[index] = made

    put_level(turn_ref, None, exact(both_first[0].T, order), exact(-both_first[1].T, order))
    put_level(level_ref, 0, first[1][0].T, first[1][1].T)
    put_level(level_ref, 1, exact(first[0][0], order), exact(-first[0][1], order))
    put_level(level_ref, 2, exact(order, first[0][0].T), exact(order, first[0][1].T))

    def put_lane(index, real_part, imag_part):
        real_part, imag_part = spread(real_part), spread(imag_part)
        high, low = split_value(blocks(real_part, imag_part, -imag_part, real_part))
        lane_ref[index, 0] = high
        lane_ref[index, 1] = low

    put_lane(0, *second[1])
    put_lane(1, second[0][0].T, -second[0][1].T)
    put_lane(2, *second[0])

    real_part, imag_part = spread(both_second[0].T), spread(both_second[1].T)
    full = blocks(real_part, -imag_part, -imag_part, -real_part)

    def source(row):
        chunk, rest = row // (2 * size * parts), row % (2 * size * parts)
        step, rest = rest // (2 * size), rest % (2 * size)
        half, place = rest // size, rest % size
        return half * WIDE + lax.bitwise_xor(step, seat) * share + chunk * size + place

    chosen = exact(pick_matrix(PAIR, source), full)
    high, low = split_value(chosen)
    open_ref[0] = high
    open_ref[1] = low
    high, low = split_value(chosen[:PAIR // chunks].T)
    first_ref[...] = blocks(high, low, high, jnp.zeros_like(low))


def make_weights(phases, displacements, table_slot, checkpoint, seat, parts, chunks):
    def angles(layer):
        return pl.BlockSpec(
            (None, 2, LEVELS), lambda i, slot, start, own: (slot[start[0] + layer], 0, 0)
        )

    def matrices(layer):
        return pl.BlockSpec(
            (None, 2, 2, LEVELS, LEVELS),
            lambda i, slot, start, own: (start[0] + layer, 0, 0, 0, 0),
        )

    def whole(shape):
        return pl.BlockSpec(shape, lambda i, slot, start, own: (0,) * len(shape))

    shapes = [(2 * PAIR, 2 * PAIR // chunks), (2, PAIR, PAIR), (PAIR, PAIR), (3, PAIR, PAIR), (3, 2, PAIR, PAIR)]
    return pl.pallas_call(
        functools.partial(weights_kernel, parts, chunks),
        grid_spec=pltpu.PrefetchScalarGridSpec(
            num_scalar_prefetch=3,
            grid=(1,),
            in_specs=[angles(0), angles(1), matrices(0), matrices(1)],
            out_specs=[whole(shape) for shape in shapes],
        ),
        out_shape=[jax.ShapeDtypeStruct(shape, BF16) for shape in shapes],
        compiler_params=PARAMS,
        cost_estimate=SMALL,
    )(table_slot, checkpoint, seat, phases, phases, displacements, displacements)


def open_kernel(count, waited, weight_ref, field_ref, *refs):
    both = jnp.concatenate([field_ref[0], field_ref[1]], axis=1)
    high, low = split_value(both)
    across = (((1,), (1,)), ((), ()))
    made = mxu(weight_ref[0], high, across) + (
        mxu(weight_ref[0], low, across) + mxu(weight_ref[1], high, across)
    )
    tall = made.shape[0] // count
    for place, out in enumerate(refs[waited:]):
        piece = made[place * tall:(place + 1) * tall]
        for first in range(out.shape[0]):
            out[first] = piece[:, first * WIDE:(first + 1) * WIDE]


def open_first_kernel(size, weight_ref, field_ref, *out_refs):
    levels = field_ref.shape[2] // WIDE
    tall = 2 * size
    for first in range(field_ref.shape[1] // WIDE):
        rows = []
        down = slice(first * WIDE, (first + 1) * WIDE)
        for level in range(levels):
            place = slice(level * WIDE, (level + 1) * WIDE)
            real_high, real_low = split_value(field_ref[0, down, place])
            imag_high, imag_low = split_value(field_ref[1, down, place])
            rows.append(jnp.concatenate([real_high, imag_high, real_low, imag_low], axis=1))
        made = mxu(jnp.concatenate(rows, axis=0), weight_ref[...])
        middle = made.shape[1] // 2
        for level in range(levels):
            turned = made[level * WIDE:(level + 1) * WIDE].T
            turned = turned[:middle] + turned[middle:]
            for step, out in enumerate(out_refs):
                out[first, level * tall:(level + 1) * tall, :] = turned[
                    step * tall:(step + 1) * tall
                ]


def open_first(field, weights, parts, size):
    rows, cols = field.shape[1:]
    firsts = rows // WIDE
    tall = cols // WIDE * 2 * size
    group = min(2, firsts)
    outs = pl.pallas_call(
        functools.partial(open_first_kernel, size),
        grid=(firsts // group,),
        in_specs=[
            pl.BlockSpec(weights.shape, lambda i: (0, 0)),
            pl.BlockSpec((2, group * WIDE, cols), lambda i: (0, i, 0)),
        ],
        out_specs=[pl.BlockSpec((group, tall, WIDE), lambda i: (i, 0, 0))] * parts,
        out_shape=[jax.ShapeDtypeStruct((firsts, tall, WIDE), F32)] * parts,
        compiler_params=PARAMS,
        cost_estimate=SMALL,
    )(weights, field)
    return [outs]


def open_state(field, weights, parts, size, chunk_start, chunk_count, waited):
    rows, cols = field.shape[1:]
    firsts = rows // WIDE
    column_levels = cols // WIDE
    count = parts * chunk_count
    tall = count * 2 * size
    shape = jax.ShapeDtypeStruct((firsts, column_levels * 2 * size, WIDE), F32)
    weights = lax.slice_in_dim(
        weights, chunk_start * parts * 2 * size, chunk_start * parts * 2 * size + tall, axis=1
    )
    outs = pl.pallas_call(
        functools.partial(open_kernel, count, len(waited)),
        grid=(column_levels,),
        in_specs=[
            pl.BlockSpec((2, tall, PAIR), lambda i: (0, 0, 0)),
            pl.BlockSpec((2, rows, WIDE), lambda i: (0, 0, i)),
        ]
        + [pl.BlockSpec(memory_space=pl.ANY)] * len(waited),
        out_specs=[pl.BlockSpec((firsts, 2 * size, WIDE), lambda i: (0, i, 0))] * count,
        out_shape=[shape] * count,
        compiler_params=PARAMS,
        cost_estimate=SMALL,
    )(weights, field, *waited)
    return [outs[c * parts:(c + 1) * parts] for c in range(chunk_count)]


def cut_kernel(size, waited, seat_ref, field_ref, *refs):
    seat = seat_ref[0]
    levels = field_ref.shape[-1] // WIDE
    for first in range(field_ref.shape[1]):
        for step, out in enumerate(refs[waited:]):
            part = lax.bitwise_xor(seat, step)
            for half in range(2):
                for level in range(levels):
                    start = (2 * level + half) * size
                    out[first, start:start + size, :] = field_ref[
                        half, first, part, :, level * WIDE:(level + 1) * WIDE
                    ]


def cut_pieces(field, seat, parts, chunk, size, waited):
    rows, cols = field.shape[1:]
    firsts = rows // WIDE
    group = min(GROUP, firsts)
    chunks = WIDE // parts // size
    tall = cols // WIDE * 2 * size
    return pl.pallas_call(
        functools.partial(cut_kernel, size, len(waited)),
        grid=(firsts // group,),
        in_specs=[
            pl.BlockSpec(memory_space=pltpu.SMEM),
            pl.BlockSpec((2, group, parts, None, size, cols), lambda i: (0, i, 0, chunk, 0, 0)),
        ]
        + [pl.BlockSpec(memory_space=pl.ANY)] * len(waited),
        out_specs=[pl.BlockSpec((group, tall, WIDE), lambda i: (i, 0, 0))] * parts,
        out_shape=[jax.ShapeDtypeStruct((firsts, tall, WIDE), F32)] * parts,
        compiler_params=PARAMS,
        cost_estimate=SMALL,
    )(seat, field.reshape(2, firsts, parts, chunks, size, cols), *waited)


def level_apply(weights, real_part, imag_part):
    real_high, real_low = split_value(real_part)
    imag_high, imag_low = split_value(imag_part)
    stacked = jnp.concatenate([real_high, imag_high, real_low, imag_low], axis=0)
    made = mxu(weights, stacked)
    return made[:WIDE] + made[WIDE:]


def lane_apply(weight_ref, index, real_part, imag_part):
    high, low = split_value(jnp.concatenate([real_part, imag_part], axis=1))
    made = mxu(high, weight_ref[index, 0]) + (
        mxu(low, weight_ref[index, 0]) + mxu(high, weight_ref[index, 1])
    )
    return made[:, :WIDE], made[:, WIDE:]


def gather_levels(refs, size, half):
    columns = []
    for place in range(size):
        parts = [
            ref[pl.ds(half * size + place, ref.shape[0] // (2 * size), stride=2 * size), :]
            for ref in refs
        ]
        columns.append(jnp.concatenate(parts, axis=0) if len(parts) > 1 else parts[0])
    return jnp.concatenate(columns, axis=1)


def scatter_levels(ref, size, half, value, start=0, apart=None):
    for place in range(size):
        rows = pl.ds(start + half * size + place, LEVELS, stride=apart or 2 * size)
        ref[rows, :] = value[:, place * WIDE:(place + 1) * WIDE]


def turn_kernel(parts, size, group, weight_ref, *refs):
    apart = group * 2 * size
    out_ref = refs[-1].reshape(LEVELS * apart, WIDE)
    for first in range(group):
        pieces = [ref.at[first] for ref in refs[:parts]]
        made = level_apply(
            weight_ref[...], gather_levels(pieces, size, 0), gather_levels(pieces, size, 1)
        )
        scatter_levels(out_ref, size, 0, made[:LEVELS], first * 2 * size, apart)
        scatter_levels(out_ref, size, 1, made[LEVELS:], first * 2 * size, apart)


def turn_columns(pieces, weights, size, waited):
    firsts = pieces[0].shape[0]
    group = min(GROUP, firsts)
    parts = len(pieces)
    block = pieces[0].shape[1:]
    return pl.pallas_call(
        functools.partial(turn_kernel, parts, size, group),
        grid=(firsts // group,),
        in_specs=[pl.BlockSpec((PAIR, PAIR), lambda i: (0, 0))]
        + [pl.BlockSpec((group,) + block, lambda i: (i, 0, 0))] * parts
        + [pl.BlockSpec(memory_space=pl.ANY)] * len(waited),
        out_specs=pl.BlockSpec((LEVELS, group, 2 * size, WIDE), lambda i: (0, i, 0, 0)),
        out_shape=jax.ShapeDtypeStruct((LEVELS, firsts, 2 * size, WIDE), F32),
        compiler_params=PARAMS,
        cost_estimate=SMALL,
    )(weights, *pieces, *waited)


def halves(value, size):
    value = value.reshape(LEVELS, 2, size, WIDE)
    rows = LEVELS * size
    return value[:, 0].reshape(rows, WIDE), value[:, 1].reshape(rows, WIDE)


def join(real_part, imag_part, size):
    shape = (LEVELS, 1, size, WIDE)
    both = jnp.concatenate([real_part.reshape(shape), imag_part.reshape(shape)], axis=1)
    return both.reshape(LEVELS * 2 * size, WIDE)


def close_kernel(parts, size, lane_ref, level_ref, field_ref, *refs):
    rho_refs = refs[:parts]
    out_refs = refs[-parts - 3:-3]
    grad_ref, work_a, work_b = refs[-3:]
    step = pl.program_id(0)

    @pl.when(step == 0)
    def _():
        grad_ref[...] = jnp.zeros_like(grad_ref)

    flat = field_ref.reshape(LEVELS * 2 * size, WIDE)
    real_part, imag_part = lane_apply(lane_ref, 0, *halves(flat[...], size))
    work_a[...] = join(real_part, imag_part, size)

    rho = jnp.concatenate([ref[...] for ref in rho_refs], axis=0)
    rho_real, rho_imag = halves(rho, size)
    real_part, imag_part = lane_apply(lane_ref, 1, rho_real, rho_imag)
    work_b[...] = join(real_part, imag_part, size)

    mid = level_apply(level_ref[0], gather_levels([work_a], size, 0), gather_levels([work_a], size, 1))
    seen = level_apply(level_ref[1], gather_levels([work_b], size, 0), gather_levels([work_b], size, 1))
    terms = seen[:LEVELS] * mid[LEVELS:] - seen[LEVELS:] * mid[:LEVELS]
    total = terms[:, :WIDE]
    for place in range(1, size):
        total = total + terms[:, place * WIDE:(place + 1) * WIDE]
    grad_ref[1] += total

    last = level_apply(level_ref[2], mid[:LEVELS], mid[LEVELS:])
    scatter_levels(work_a, size, 0, last[:LEVELS])
    scatter_levels(work_a, size, 1, last[LEVELS:])
    real_part, imag_part = lane_apply(lane_ref, 2, *halves(work_a[...], size))
    terms = rho_real * imag_part - rho_imag * real_part
    grad_ref[0] += jnp.sum(terms.reshape(LEVELS, size, WIDE), axis=1)
    made = join(real_part, imag_part, size)
    rows = made.shape[0] // parts
    for part in range(parts):
        out_refs[part][...] = made[part * rows:(part + 1) * rows]


def close_columns(field, rho_pieces, lane, level, size, waited):
    total_first, firsts = field.shape[:2]
    devs = total_first // firsts
    parts = len(rho_pieces)
    rows = LEVELS * 2 * size
    field = field.reshape(devs, firsts, firsts * 2 * size, WIDE)
    piece = rho_pieces[0]
    piece_spec = pl.BlockSpec((None,) + piece.shape[1:], lambda i: (i, 0, 0))
    outs = pl.pallas_call(
        functools.partial(close_kernel, parts, size),
        grid=(firsts,),
        in_specs=[
            pl.BlockSpec(lane.shape, lambda i: (0, 0, 0, 0)),
            pl.BlockSpec(level.shape, lambda i: (0, 0, 0)),
            pl.BlockSpec((devs, None, firsts * 2 * size, WIDE), lambda i: (0, i, 0, 0)),
        ]
        + [piece_spec] * parts
        + [pl.BlockSpec(memory_space=pl.ANY)] * len(waited),
        out_specs=[piece_spec] * parts + [pl.BlockSpec((2, LEVELS, WIDE), lambda i: (0, 0, 0))],
        out_shape=[jax.ShapeDtypeStruct(piece.shape, F32)] * parts
        + [jax.ShapeDtypeStruct((2, LEVELS, WIDE), F32)],
        scratch_shapes=[pltpu.VMEM((rows, WIDE), F32), pltpu.VMEM((rows, WIDE), F32)],
        compiler_params=PARAMS,
        cost_estimate=LARGE,
    )(lane, level, field, *rho_pieces, *waited)
    return list(outs[:parts]), outs[parts]


def place_kernel(parts, size, seat_ref, *refs):
    pieces = refs[:parts]
    out_ref = refs[-1]
    seat = seat_ref[0]
    levels = out_ref.shape[-1] // WIDE
    for first in range(out_ref.shape[1]):
        for step in range(parts):
            part = lax.bitwise_xor(seat, step)
            for half in range(2):
                for level in range(levels):
                    start = (2 * level + half) * size
                    out_ref[half, first, part, :, level * WIDE:(level + 1) * WIDE] = pieces[step][
                        first, start:start + size, :
                    ]


def place_pieces(pieces, seat, held, chunk, shape, size, waited):
    parts = len(pieces)
    group = min(GROUP, shape[1])
    cols = shape[-1]
    return pl.pallas_call(
        functools.partial(place_kernel, parts, size),
        grid=(shape[1] // group,),
        in_specs=[pl.BlockSpec(memory_space=pltpu.SMEM)]
        + [pl.BlockSpec((group,) + pieces[0].shape[1:], lambda i: (i, 0, 0))] * parts
        + [pl.BlockSpec(memory_space=pl.ANY)],
        out_specs=pl.BlockSpec(
            (2, group, parts, None, size, cols), lambda i: (0, i, 0, chunk, 0, 0)
        ),
        out_shape=jax.ShapeDtypeStruct(shape, F32),
        input_output_aliases={} if held is None else {parts + 1: 0},
        compiler_params=PARAMS,
        cost_estimate=SMALL,
    )(seat, *pieces, waited if held is None else held)


def swap(pieces, parts):
    moved = [pieces[0]]
    for step in range(1, parts):
        pairs = [(member, member ^ step) for member in range(parts)]
        moved.append(lax.ppermute(pieces[step], "grp", pairs))
    return moved


def grad_kernel(parts, count, seat_ref, *refs):
    out_ref = refs[-1]
    grad = refs[0][...]
    for ref in refs[1:count]:
        grad = grad + ref[...]
    grad = -2.0 * grad
    width = LEVELS // parts
    order = pick_matrix(
        LEVELS, lambda row: lax.bitwise_xor(row // width, seat_ref[0]) * width + row % width
    )
    fold = (grid_of((WIDE, LEVELS), 0) // TRANSMON == grid_of((WIDE, LEVELS), 1)).astype(F32)
    for layer in range(2):
        firsts = exact(jnp.ones((8, WIDE), F32), grad[layer], (((1,), (1,)), ((), ())))
        if layer == 0:
            firsts = exact(firsts, order)
        seconds = exact(exact(jnp.ones((8, LEVELS), F32), grad[layer]), fold)
        out_ref[2 * layer:2 * layer + 1, :] = firsts[:1]
        out_ref[2 * layer + 1:2 * layer + 2, :] = seconds[:1]


def device_grad(grads, seat, parts, waited):
    return pl.pallas_call(
        functools.partial(grad_kernel, parts, len(grads)),
        in_specs=[pl.BlockSpec(memory_space=pltpu.SMEM)]
        + [pl.BlockSpec(memory_space=pltpu.VMEM)] * len(grads)
        + [pl.BlockSpec(memory_space=pl.ANY)] * len(waited),
        out_specs=pl.BlockSpec(memory_space=pltpu.VMEM),
        out_shape=jax.ShapeDtypeStruct((4, LEVELS), F32),
        compiler_params=PARAMS,
        cost_estimate=SMALL,
    )(seat, *grads, *waited)


def grand_total(value):
    rounds = []
    for axis in ("grp", "dev"):
        count = lax.axis_size(axis)
        rounds.append([(axis, 1 << bit, count) for bit in range(count.bit_length() - 1)])
    for axis, step, count in rounds[0][:1] + rounds[1] + rounds[0][1:]:
        pairs = [(member, member ^ step) for member in range(count)]
        value = value + lax.ppermute(value, axis, pairs)
    return value


def per_device(density, costate, phases, displacements, table_slot, checkpoint):
    parts = lax.axis_size("grp")
    share = WIDE // parts
    chunks = max(1, min(4, share // 8))
    size = share // chunks
    seat = lax.axis_index("grp").astype(jnp.int32)
    seats = seat.reshape(1)
    rows, cols = costate.shape[1:]

    opened_first, opened, turned_by, level, lane = make_weights(
        phases, displacements, table_slot, checkpoint, seats, parts, chunks
    )
    state_cut = open_first(costate, opened_first, parts, size)
    if chunks > 1:
        state_cut += open_state(
            costate, opened, parts, size, 1, chunks - 1, list(state_cut[0][:1])
        )
    rho = [
        cut_pieces(density, seats, parts, chunk, size, list(state_cut[-1][:1]) if chunk else [])
        for chunk in range(chunks)
    ]
    rho_there = [swap(pieces, parts) for pieces in rho]
    ahead = parts // 2
    state_cut[0], rho_there[0][ahead] = lax.optimization_barrier(
        (state_cut[0], rho_there[0][ahead])
    )
    state = [swap(pieces, parts) for pieces in state_cut[:3]]

    shape = (2, rows // WIDE, parts, chunks, size, cols)
    fields, closed, made, grads = [], [], [], []

    def close(chunk, waited):
        if chunk > 0:
            waited = waited + closed[chunk - 1][:1]
        out, grad = close_columns(
            fields[chunk], rho_there[chunk], lane, level, size, waited
        )
        closed.append(out)
        if chunk == chunks - 2 and chunk > 0:
            out, rho_there[-1] = lax.optimization_barrier((out, rho_there[-1]))
        if chunk == chunks - 1 and chunk > 1:
            out, made[-1] = lax.optimization_barrier((out, made[-1]))
        if chunk > 0 or chunks < 4:
            made.append(swap(out, parts))
        grads.append(grad)

    for chunk in range(chunks):
        waited = [rho[chunk][0]]
        if chunk == 0:
            waited += [pieces[0] for pieces in state_cut[1:2]]
        if chunk > 0:
            waited.append(field)
        if chunk > 1:
            close(chunk - 2, [])
            waited += closed[chunk - 2][:1]
        field = turn_columns(state[chunk], turned_by, size, waited)
        if chunk + 1 == len(state) < chunks:
            pieces, field = lax.optimization_barrier((state_cut[chunk + 1], field))
            state.append(swap(pieces, parts))
            out, rho_there[2] = lax.optimization_barrier((closed[0], rho_there[2]))
            made.append(swap(out, parts))
        fields.append(lax.all_to_all(field, "dev", split_axis=0, concat_axis=0, tiled=True))
    whole = None
    for chunk in range(chunks):
        while len(made) < min(chunk + 2, chunks):
            waited = list(made[-2][1:]) if len(made) > 1 else []
            close(len(made), [whole] if 0 < chunk == chunks - 2 else waited)
        whole = place_pieces(made[chunk], seats, whole, chunk, shape, size, field)
    grad = grand_total(device_grad(grads, seats, parts, []))
    return whole.reshape(costate.shape), grad.reshape(2, 2, LEVELS)


def solution(mesh):
    return jax.shard_map(
        per_device,
        mesh=mesh,
        in_specs=(P(None, "dev", "grp"), P(None, "dev", "grp"), P(), P(), P(), P()),
        out_specs=(P(None, "dev", "grp"), P()),
        check_vma=False,
    )
```

```python
import functools

import jax
import jax.numpy as jnp
from jax import lax
from jax.experimental import pallas as pl
from jax.experimental.pallas import tpu as pltpu
from jax.sharding import PartitionSpec as P

LEVELS = 64
TRANSMON = 2
GROUP = 4
WIDE = LEVELS * TRANSMON
PAIR = 2 * WIDE
HIGH = lax.Precision.HIGHEST
F32 = jnp.float32
BF16 = jnp.bfloat16
SMALL = pl.CostEstimate(flops=1024, bytes_accessed=1024, transcendentals=0)
LARGE = pl.CostEstimate(flops=2 * 10**11, bytes_accessed=1024, transcendentals=0)
PARAMS = pltpu.CompilerParams(vmem_limit_bytes=60 * 1024 * 1024)


def split_value(value):
    high = value.astype(BF16)
    low = (value - high.astype(F32)).astype(BF16)
    return high, low


def mxu(left, right, dims=(((1,), (0,)), ((), ()))):
    return lax.dot_general(left, right, dims, preferred_element_type=F32)


def exact(left, right, dims=(((1,), (0,)), ((), ()))):
    return lax.dot_general(left, right, dims, precision=HIGH, preferred_element_type=F32)


def grid_of(shape, dim):
    return lax.broadcasted_iota(jnp.int32, shape, dim)


def pick_matrix(count, chosen):
    shape = (count, count)
    return (chosen(grid_of(shape, 0)) == grid_of(shape, 1)).astype(F32)


def spread(matrix):
    tall = (grid_of((WIDE, LEVELS), 0) // TRANSMON == grid_of((WIDE, LEVELS), 1)).astype(F32)
    long = (grid_of((LEVELS, WIDE), 1) // TRANSMON == grid_of((LEVELS, WIDE), 0)).astype(F32)
    same = grid_of((WIDE, WIDE), 0) % TRANSMON == grid_of((WIDE, WIDE), 1) % TRANSMON
    return jnp.where(same, exact(exact(tall, matrix), long), 0.0)


def blocks(upper_left, upper_right, lower_left, lower_right):
    return jnp.concatenate(
        [
            jnp.concatenate([upper_left, upper_right], axis=1),
            jnp.concatenate([lower_left, lower_right], axis=1),
        ],
        axis=0,
    )


def complex_product(left, right):
    return (
        exact(left[0], right[0]) - exact(left[1], right[1]),
        exact(left[0], right[1]) + exact(left[1], right[0]),
    )


def weights_kernel(parts, chunks, slot_ref, start_ref, seat_ref, *refs):
    angle_refs, matrix_refs = refs[0:2], refs[2:4]
    first_ref, open_ref, turn_ref, level_ref, lane_ref = refs[-5:]
    seat = seat_ref[0]
    width = LEVELS // parts
    share = WIDE // parts
    size = share // chunks
    first, second = [], []
    for layer in range(2):
        cosine = jnp.cos(angle_refs[layer][...])
        sine = jnp.sin(angle_refs[layer][...])
        for mode, kept in enumerate((first, second)):
            turn_real, turn_imag = cosine[mode:mode + 1], sine[mode:mode + 1]
            real_part = matrix_refs[layer][mode, 0]
            imag_part = matrix_refs[layer][mode, 1]
            kept.append(
                (
                    real_part * turn_real - imag_part * turn_imag,
                    real_part * turn_imag + imag_part * turn_real,
                )
            )
    both_first = complex_product(first[1], first[0])
    both_second = complex_product(second[1], second[0])

    order = pick_matrix(
        LEVELS, lambda row: lax.bitwise_xor(row // width, seat) * width + row % width
    )

    def put_level(ref, index, real_part, imag_part):
        full = blocks(real_part, -imag_part, imag_part, real_part)
        high, low = split_value(full)
        made = blocks(high, high, low, jnp.zeros_like(low))
        if index is None:
            ref[...] = made
        else:
            ref[index] = made

    put_level(turn_ref, None, exact(both_first[0].T, order), exact(-both_first[1].T, order))
    put_level(level_ref, 0, first[1][0].T, first[1][1].T)
    put_level(level_ref, 1, exact(first[0][0], order), exact(-first[0][1], order))
    put_level(level_ref, 2, exact(order, first[0][0].T), exact(order, first[0][1].T))

    def put_lane(index, real_part, imag_part):
        real_part, imag_part = spread(real_part), spread(imag_part)
        high, low = split_value(blocks(real_part, imag_part, -imag_part, real_part))
        lane_ref[index, 0] = high
        lane_ref[index, 1] = low

    put_lane(0, *second[1])
    put_lane(1, second[0][0].T, -second[0][1].T)
    put_lane(2, *second[0])

    real_part, imag_part = spread(both_second[0].T), spread(both_second[1].T)
    full = blocks(real_part, -imag_part, -imag_part, -real_part)

    def source(row):
        chunk, rest = row // (2 * size * parts), row % (2 * size * parts)
        step, rest = rest // (2 * size), rest % (2 * size)
        half, place = rest // size, rest % size
        return half * WIDE + lax.bitwise_xor(step, seat) * share + chunk * size + place

    chosen = exact(pick_matrix(PAIR, source), full)
    high, low = split_value(chosen)
    open_ref[0] = high
    open_ref[1] = low
    high, low = split_value(chosen[:PAIR // chunks].T)
    first_ref[...] = blocks(high, low, high, jnp.zeros_like(low))


def make_weights(phases, displacements, table_slot, checkpoint, seat, parts, chunks):
    def angles(layer):
        return pl.BlockSpec(
            (None, 2, LEVELS), lambda i, slot, start, own: (slot[start[0] + layer], 0, 0)
        )

    def matrices(layer):
        return pl.BlockSpec(
            (None, 2, 2, LEVELS, LEVELS),
            lambda i, slot, start, own: (start[0] + layer, 0, 0, 0, 0),
        )

    def whole(shape):
        return pl.BlockSpec(shape, lambda i, slot, start, own: (0,) * len(shape))

    shapes = [(2 * PAIR, 2 * PAIR // chunks), (2, PAIR, PAIR), (PAIR, PAIR), (3, PAIR, PAIR), (3, 2, PAIR, PAIR)]
    return pl.pallas_call(
        functools.partial(weights_kernel, parts, chunks),
        grid_spec=pltpu.PrefetchScalarGridSpec(
            num_scalar_prefetch=3,
            grid=(1,),
            in_specs=[angles(0), angles(1), matrices(0), matrices(1)],
            out_specs=[whole(shape) for shape in shapes],
        ),
        out_shape=[jax.ShapeDtypeStruct(shape, BF16) for shape in shapes],
        compiler_params=PARAMS,
        cost_estimate=SMALL,
    )(table_slot, checkpoint, seat, phases, phases, displacements, displacements)


def open_kernel(count, waited, weight_ref, field_ref, *refs):
    both = jnp.concatenate([field_ref[0], field_ref[1]], axis=1)
    high, low = split_value(both)
    across = (((1,), (1,)), ((), ()))
    made = mxu(weight_ref[0], high, across) + (
        mxu(weight_ref[0], low, across) + mxu(weight_ref[1], high, across)
    )
    tall = made.shape[0] // count
    for place, out in enumerate(refs[waited:]):
        piece = made[place * tall:(place + 1) * tall]
        for first in range(out.shape[0]):
            out[first] = piece[:, first * WIDE:(first + 1) * WIDE]


def open_first_kernel(size, weight_ref, field_ref, *out_refs):
    levels = field_ref.shape[2] // WIDE
    tall = 2 * size
    for first in range(field_ref.shape[1] // WIDE):
        rows = []
        down = slice(first * WIDE, (first + 1) * WIDE)
        for level in range(levels):
            place = slice(level * WIDE, (level + 1) * WIDE)
            real_high, real_low = split_value(field_ref[0, down, place])
            imag_high, imag_low = split_value(field_ref[1, down, place])
            rows.append(jnp.concatenate([real_high, imag_high, real_low, imag_low], axis=1))
        made = mxu(jnp.concatenate(rows, axis=0), weight_ref[...])
        middle = made.shape[1] // 2
        for level in range(levels):
            turned = made[level * WIDE:(level + 1) * WIDE].T
            turned = turned[:middle] + turned[middle:]
            for step, out in enumerate(out_refs):
                out[first, level * tall:(level + 1) * tall, :] = turned[
                    step * tall:(step + 1) * tall
                ]


def open_first(field, weights, parts, size):
    rows, cols = field.shape[1:]
    firsts = rows // WIDE
    tall = cols // WIDE * 2 * size
    group = min(2, firsts)
    outs = pl.pallas_call(
        functools.partial(open_first_kernel, size),
        grid=(firsts // group,),
        in_specs=[
            pl.BlockSpec(weights.shape, lambda i: (0, 0)),
            pl.BlockSpec((2, group * WIDE, cols), lambda i: (0, i, 0)),
        ],
        out_specs=[pl.BlockSpec((group, tall, WIDE), lambda i: (i, 0, 0))] * parts,
        out_shape=[jax.ShapeDtypeStruct((firsts, tall, WIDE), F32)] * parts,
        compiler_params=PARAMS,
        cost_estimate=SMALL,
    )(weights, field)
    return [outs]


def open_state(field, weights, parts, size, chunk_start, chunk_count, waited):
    rows, cols = field.shape[1:]
    firsts = rows // WIDE
    column_levels = cols // WIDE
    count = parts * chunk_count
    tall = count * 2 * size
    shape = jax.ShapeDtypeStruct((firsts, column_levels * 2 * size, WIDE), F32)
    weights = lax.slice_in_dim(
        weights, chunk_start * parts * 2 * size, chunk_start * parts * 2 * size + tall, axis=1
    )
    outs = pl.pallas_call(
        functools.partial(open_kernel, count, len(waited)),
        grid=(column_levels,),
        in_specs=[
            pl.BlockSpec((2, tall, PAIR), lambda i: (0, 0, 0)),
            pl.BlockSpec((2, rows, WIDE), lambda i: (0, 0, i)),
        ]
        + [pl.BlockSpec(memory_space=pl.ANY)] * len(waited),
        out_specs=[pl.BlockSpec((firsts, 2 * size, WIDE), lambda i: (0, i, 0))] * count,
        out_shape=[shape] * count,
        compiler_params=PARAMS,
        cost_estimate=SMALL,
    )(weights, field, *waited)
    return [outs[c * parts:(c + 1) * parts] for c in range(chunk_count)]


def cut_kernel(size, waited, seat_ref, field_ref, *refs):
    seat = seat_ref[0]
    levels = field_ref.shape[-1] // WIDE
    for first in range(field_ref.shape[1]):
        for step, out in enumerate(refs[waited:]):
            part = lax.bitwise_xor(seat, step)
            for half in range(2):
                for level in range(levels):
                    start = (2 * level + half) * size
                    out[first, start:start + size, :] = field_ref[
                        half, first, part, :, level * WIDE:(level + 1) * WIDE
                    ]


def cut_pieces(field, seat, parts, chunk, size, waited):
    rows, cols = field.shape[1:]
    firsts = rows // WIDE
    group = min(GROUP, firsts)
    chunks = WIDE // parts // size
    tall = cols // WIDE * 2 * size
    return pl.pallas_call(
        functools.partial(cut_kernel, size, len(waited)),
        grid=(firsts // group,),
        in_specs=[
            pl.BlockSpec(memory_space=pltpu.SMEM),
            pl.BlockSpec((2, group, parts, None, size, cols), lambda i: (0, i, 0, chunk, 0, 0)),
        ]
        + [pl.BlockSpec(memory_space=pl.ANY)] * len(waited),
        out_specs=[pl.BlockSpec((group, tall, WIDE), lambda i: (i, 0, 0))] * parts,
        out_shape=[jax.ShapeDtypeStruct((firsts, tall, WIDE), F32)] * parts,
        compiler_params=PARAMS,
        cost_estimate=SMALL,
    )(seat, field.reshape(2, firsts, parts, chunks, size, cols), *waited)


def level_apply(weights, real_part, imag_part):
    real_high, real_low = split_value(real_part)
    imag_high, imag_low = split_value(imag_part)
    stacked = jnp.concatenate([real_high, imag_high, real_low, imag_low], axis=0)
    made = mxu(weights, stacked)
    return made[:WIDE] + made[WIDE:]


def lane_apply(weight_ref, index, real_part, imag_part):
    high, low = split_value(jnp.concatenate([real_part, imag_part], axis=1))
    made = mxu(high, weight_ref[index, 0]) + (
        mxu(low, weight_ref[index, 0]) + mxu(high, weight_ref[index, 1])
    )
    return made[:, :WIDE], made[:, WIDE:]


def gather_levels(refs, size, half):
    columns = []
    for place in range(size):
        parts = [
            ref[pl.ds(half * size + place, ref.shape[0] // (2 * size), stride=2 * size), :]
            for ref in refs
        ]
        columns.append(jnp.concatenate(parts, axis=0) if len(parts) > 1 else parts[0])
    return jnp.concatenate(columns, axis=1)


def scatter_levels(ref, size, half, value, start=0, apart=None):
    for place in range(size):
        rows = pl.ds(start + half * size + place, LEVELS, stride=apart or 2 * size)
        ref[rows, :] = value[:, place * WIDE:(place + 1) * WIDE]


def turn_kernel(parts, size, group, weight_ref, *refs):
    apart = group * 2 * size
    out_ref = refs[-1].reshape(LEVELS * apart, WIDE)
    for first in range(group):
        pieces = [ref.at[first] for ref in refs[:parts]]
        made = level_apply(
            weight_ref[...], gather_levels(pieces, size, 0), gather_levels(pieces, size, 1)
        )
        scatter_levels(out_ref, size, 0, made[:LEVELS], first * 2 * size, apart)
        scatter_levels(out_ref, size, 1, made[LEVELS:], first * 2 * size, apart)


def turn_columns(pieces, weights, size, waited):
    firsts = pieces[0].shape[0]
    group = min(GROUP, firsts)
    parts = len(pieces)
    block = pieces[0].shape[1:]
    return pl.pallas_call(
        functools.partial(turn_kernel, parts, size, group),
        grid=(firsts // group,),
        in_specs=[pl.BlockSpec((PAIR, PAIR), lambda i: (0, 0))]
        + [pl.BlockSpec((group,) + block, lambda i: (i, 0, 0))] * parts
        + [pl.BlockSpec(memory_space=pl.ANY)] * len(waited),
        out_specs=pl.BlockSpec((LEVELS, group, 2 * size, WIDE), lambda i: (0, i, 0, 0)),
        out_shape=jax.ShapeDtypeStruct((LEVELS, firsts, 2 * size, WIDE), F32),
        compiler_params=PARAMS,
        cost_estimate=SMALL,
    )(weights, *pieces, *waited)


def halves(value, size):
    value = value.reshape(LEVELS, 2, size, WIDE)
    rows = LEVELS * size
    return value[:, 0].reshape(rows, WIDE), value[:, 1].reshape(rows, WIDE)


def join(real_part, imag_part, size):
    shape = (LEVELS, 1, size, WIDE)
    both = jnp.concatenate([real_part.reshape(shape), imag_part.reshape(shape)], axis=1)
    return both.reshape(LEVELS * 2 * size, WIDE)


def close_kernel(parts, size, lane_ref, level_ref, field_ref, *refs):
    rho_refs = refs[:parts]
    out_refs = refs[-parts - 3:-3]
    grad_ref, work_a, work_b = refs[-3:]
    step = pl.program_id(0)

    @pl.when(step == 0)
    def _():
        grad_ref[...] = jnp.zeros_like(grad_ref)

    flat = field_ref.reshape(LEVELS * 2 * size, WIDE)
    real_part, imag_part = lane_apply(lane_ref, 0, *halves(flat[...], size))
    work_a[...] = join(real_part, imag_part, size)

    rho = jnp.concatenate([ref[...] for ref in rho_refs], axis=0)
    rho_real, rho_imag = halves(rho, size)
    real_part, imag_part = lane_apply(lane_ref, 1, rho_real, rho_imag)
    work_b[...] = join(real_part, imag_part, size)

    mid = level_apply(level_ref[0], gather_levels([work_a], size, 0), gather_levels([work_a], size, 1))
    seen = level_apply(level_ref[1], gather_levels([work_b], size, 0), gather_levels([work_b], size, 1))
    terms = seen[:LEVELS] * mid[LEVELS:] - seen[LEVELS:] * mid[:LEVELS]
    total = terms[:, :WIDE]
    for place in range(1, size):
        total = total + terms[:, place * WIDE:(place + 1) * WIDE]
    grad_ref[1] += total

    last = level_apply(level_ref[2], mid[:LEVELS], mid[LEVELS:])
    scatter_levels(work_a, size, 0, last[:LEVELS])
    scatter_levels(work_a, size, 1, last[LEVELS:])
    real_part, imag_part = lane_apply(lane_ref, 2, *halves(work_a[...], size))
    terms = rho_real * imag_part - rho_imag * real_part
    grad_ref[0] += jnp.sum(terms.reshape(LEVELS, size, WIDE), axis=1)
    made = join(real_part, imag_part, size)
    rows = made.shape[0] // parts
    for part in range(parts):
        out_refs[part][...] = made[part * rows:(part + 1) * rows]


def close_columns(field, rho_pieces, lane, level, size, waited):
    total_first, firsts = field.shape[:2]
    devs = total_first // firsts
    parts = len(rho_pieces)
    rows = LEVELS * 2 * size
    field = field.reshape(devs, firsts, firsts * 2 * size, WIDE)
    piece = rho_pieces[0]
    piece_spec = pl.BlockSpec((None,) + piece.shape[1:], lambda i: (i, 0, 0))
    outs = pl.pallas_call(
        functools.partial(close_kernel, parts, size),
        grid=(firsts,),
        in_specs=[
            pl.BlockSpec(lane.shape, lambda i: (0, 0, 0, 0)),
            pl.BlockSpec(level.shape, lambda i: (0, 0, 0)),
            pl.BlockSpec((devs, None, firsts * 2 * size, WIDE), lambda i: (0, i, 0, 0)),
        ]
        + [piece_spec] * parts
        + [pl.BlockSpec(memory_space=pl.ANY)] * len(waited),
        out_specs=[piece_spec] * parts + [pl.BlockSpec((2, LEVELS, WIDE), lambda i: (0, 0, 0))],
        out_shape=[jax.ShapeDtypeStruct(piece.shape, F32)] * parts
        + [jax.ShapeDtypeStruct((2, LEVELS, WIDE), F32)],
        scratch_shapes=[pltpu.VMEM((rows, WIDE), F32), pltpu.VMEM((rows, WIDE), F32)],
        compiler_params=PARAMS,
        cost_estimate=LARGE,
    )(lane, level, field, *rho_pieces, *waited)
    return list(outs[:parts]), outs[parts]


def place_kernel(parts, size, seat_ref, *refs):
    pieces = refs[:parts]
    out_ref = refs[-1]
    seat = seat_ref[0]
    levels = out_ref.shape[-1] // WIDE
    for first in range(out_ref.shape[1]):
        for step in range(parts):
            part = lax.bitwise_xor(seat, step)
            for half in range(2):
                for level in range(levels):
                    start = (2 * level + half) * size
                    out_ref[half, first, part, :, level * WIDE:(level + 1) * WIDE] = pieces[step][
                        first, start:start + size, :
                    ]


def place_pieces(pieces, seat, held, chunk, shape, size, waited):
    parts = len(pieces)
    group = min(GROUP, shape[1])
    cols = shape[-1]
    return pl.pallas_call(
        functools.partial(place_kernel, parts, size),
        grid=(shape[1] // group,),
        in_specs=[pl.BlockSpec(memory_space=pltpu.SMEM)]
        + [pl.BlockSpec((group,) + pieces[0].shape[1:], lambda i: (i, 0, 0))] * parts
        + [pl.BlockSpec(memory_space=pl.ANY)],
        out_specs=pl.BlockSpec(
            (2, group, parts, None, size, cols), lambda i: (0, i, 0, chunk, 0, 0)
        ),
        out_shape=jax.ShapeDtypeStruct(shape, F32),
        input_output_aliases={} if held is None else {parts + 1: 0},
        compiler_params=PARAMS,
        cost_estimate=SMALL,
    )(seat, *pieces, waited if held is None else held)


def swap(pieces, parts):
    moved = [pieces[0]]
    for step in range(1, parts):
        pairs = [(member, member ^ step) for member in range(parts)]
        moved.append(lax.ppermute(pieces[step], "grp", pairs))
    return moved


def grad_kernel(parts, count, seat_ref, *refs):
    out_ref = refs[-1]
    grad = refs[0][...]
    for ref in refs[1:count]:
        grad = grad + ref[...]
    grad = -2.0 * grad
    width = LEVELS // parts
    order = pick_matrix(
        LEVELS, lambda row: lax.bitwise_xor(row // width, seat_ref[0]) * width + row % width
    )
    fold = (grid_of((WIDE, LEVELS), 0) // TRANSMON == grid_of((WIDE, LEVELS), 1)).astype(F32)
    for layer in range(2):
        firsts = exact(jnp.ones((8, WIDE), F32), grad[layer], (((1,), (1,)), ((), ())))
        if layer == 0:
            firsts = exact(firsts, order)
        seconds = exact(exact(jnp.ones((8, LEVELS), F32), grad[layer]), fold)
        out_ref[2 * layer:2 * layer + 1, :] = firsts[:1]
        out_ref[2 * layer + 1:2 * layer + 2, :] = seconds[:1]


def device_grad(grads, seat, parts, waited):
    return pl.pallas_call(
        functools.partial(grad_kernel, parts, len(grads)),
        in_specs=[pl.BlockSpec(memory_space=pltpu.SMEM)]
        + [pl.BlockSpec(memory_space=pltpu.VMEM)] * len(grads)
        + [pl.BlockSpec(memory_space=pl.ANY)] * len(waited),
        out_specs=pl.BlockSpec(memory_space=pltpu.VMEM),
        out_shape=jax.ShapeDtypeStruct((4, LEVELS), F32),
        compiler_params=PARAMS,
        cost_estimate=SMALL,
    )(seat, *grads, *waited)


def grand_total(value):
    rounds = []
    for axis in ("grp", "dev"):
        count = lax.axis_size(axis)
        rounds.append([(axis, 1 << bit, count) for bit in range(count.bit_length() - 1)])
    for axis, step, count in rounds[0][:1] + rounds[1] + rounds[0][1:]:
        pairs = [(member, member ^ step) for member in range(count)]
        value = value + lax.ppermute(value, axis, pairs)
    return value


def per_device(density, costate, phases, displacements, table_slot, checkpoint):
    parts = lax.axis_size("grp")
    share = WIDE // parts
    chunks = max(1, min(4, share // 8))
    size = share // chunks
    seat = lax.axis_index("grp").astype(jnp.int32)
    seats = seat.reshape(1)
    rows, cols = costate.shape[1:]

    opened_first, opened, turned_by, level, lane = make_weights(
        phases, displacements, table_slot, checkpoint, seats, parts, chunks
    )
    state_cut = open_first(costate, opened_first, parts, size)
    if chunks > 1:
        state_cut += open_state(
            costate, opened, parts, size, 1, chunks - 1, list(state_cut[0][:1])
        )
    rho = [
        cut_pieces(density, seats, parts, chunk, size, list(state_cut[-1][:1]) if chunk else [])
        for chunk in range(chunks)
    ]
    rho_there = [swap(pieces, parts) for pieces in rho]
    ahead = parts // 2
    state_cut[0], rho_there[0][ahead] = lax.optimization_barrier(
        (state_cut[0], rho_there[0][ahead])
    )
    state = [swap(pieces, parts) for pieces in state_cut[:3]]

    shape = (2, rows // WIDE, parts, chunks, size, cols)
    fields, closed, made, grads = [], [], [], []

    def close(chunk, waited):
        if chunk > 0:
            waited = waited + closed[chunk - 1][:1]
        out, grad = close_columns(
            fields[chunk], rho_there[chunk], lane, level, size, waited
        )
        closed.append(out)
        if chunk == chunks - 2 and chunk > 0:
            out, rho_there[-1] = lax.optimization_barrier((out, rho_there[-1]))
        if chunk == chunks - 1 and chunk > 1:
            out, made[-1] = lax.optimization_barrier((out, made[-1]))
        if chunk > 0 or chunks < 4:
            made.append(swap(out, parts))
        grads.append(grad)

    for chunk in range(chunks):
        waited = [rho[chunk][0]]
        if chunk == 0:
            waited += [pieces[0] for pieces in state_cut[1:2]]
        if chunk > 0:
            waited.append(field)
        if chunk > 1:
            close(chunk - 2, [])
            waited += closed[chunk - 2][:1]
        field = turn_columns(state[chunk], turned_by, size, waited)
        if chunk + 1 == len(state) < chunks:
            pieces, field = lax.optimization_barrier((state_cut[chunk + 1], field))
            state.append(swap(pieces, parts))
            out, rho_there[2] = lax.optimization_barrier((closed[0], rho_there[2]))
            made.append(swap(out, parts))
        fields.append(lax.all_to_all(field, "dev", split_axis=0, concat_axis=0, tiled=True))
    whole = None
    for chunk in range(chunks):
        while len(made) < min(max(chunk + 2, chunks - 1), chunks):
            close(len(made), [whole] if 0 < chunk == chunks - 2 else [])
        whole = place_pieces(made[chunk], seats, whole, chunk, shape, size, closed[-1][0])
    grad = grand_total(device_grad(grads, seats, parts, []))
    return whole.reshape(costate.shape), grad.reshape(2, 2, LEVELS)


def solution(mesh):
    return jax.shard_map(
        per_device,
        mesh=mesh,
        in_specs=(P(None, "dev", "grp"), P(None, "dev", "grp"), P(), P(), P(), P()),
        out_specs=(P(None, "dev", "grp"), P()),
        check_vma=False,
    )
```

```python
import functools

import jax
import jax.numpy as jnp
from jax import lax
from jax.experimental import pallas as pl
from jax.experimental.pallas import tpu as pltpu
from jax.sharding import PartitionSpec as P

LEVELS = 64
TRANSMON = 2
GROUP = 4
WIDE = LEVELS * TRANSMON
PAIR = 2 * WIDE
HIGH = lax.Precision.HIGHEST
F32 = jnp.float32
BF16 = jnp.bfloat16
SMALL = pl.CostEstimate(flops=1024, bytes_accessed=1024, transcendentals=0)
LARGE = pl.CostEstimate(flops=2 * 10**11, bytes_accessed=1024, transcendentals=0)
PARAMS = pltpu.CompilerParams(vmem_limit_bytes=60 * 1024 * 1024)


def split_value(value):
    high = value.astype(BF16)
    low = (value - high.astype(F32)).astype(BF16)
    return high, low


def mxu(left, right, dims=(((1,), (0,)), ((), ()))):
    return lax.dot_general(left, right, dims, preferred_element_type=F32)


def exact(left, right, dims=(((1,), (0,)), ((), ()))):
    return lax.dot_general(left, right, dims, precision=HIGH, preferred_element_type=F32)


def grid_of(shape, dim):
    return lax.broadcasted_iota(jnp.int32, shape, dim)


def pick_matrix(count, chosen):
    shape = (count, count)
    return (chosen(grid_of(shape, 0)) == grid_of(shape, 1)).astype(F32)


def spread(matrix):
    tall = (grid_of((WIDE, LEVELS), 0) // TRANSMON == grid_of((WIDE, LEVELS), 1)).astype(F32)
    long = (grid_of((LEVELS, WIDE), 1) // TRANSMON == grid_of((LEVELS, WIDE), 0)).astype(F32)
    same = grid_of((WIDE, WIDE), 0) % TRANSMON == grid_of((WIDE, WIDE), 1) % TRANSMON
    return jnp.where(same, exact(exact(tall, matrix), long), 0.0)


def blocks(upper_left, upper_right, lower_left, lower_right):
    return jnp.concatenate(
        [
            jnp.concatenate([upper_left, upper_right], axis=1),
            jnp.concatenate([lower_left, lower_right], axis=1),
        ],
        axis=0,
    )


def complex_product(left, right):
    return (
        exact(left[0], right[0]) - exact(left[1], right[1]),
        exact(left[0], right[1]) + exact(left[1], right[0]),
    )


def weights_kernel(parts, chunks, slot_ref, start_ref, seat_ref, *refs):
    angle_refs, matrix_refs = refs[0:2], refs[2:4]
    first_ref, open_ref, turn_ref, level_ref, lane_ref = refs[-5:]
    seat = seat_ref[0]
    width = LEVELS // parts
    share = WIDE // parts
    size = share // chunks
    first, second = [], []
    for layer in range(2):
        cosine = jnp.cos(angle_refs[layer][...])
        sine = jnp.sin(angle_refs[layer][...])
        for mode, kept in enumerate((first, second)):
            turn_real, turn_imag = cosine[mode:mode + 1], sine[mode:mode + 1]
            real_part = matrix_refs[layer][mode, 0]
            imag_part = matrix_refs[layer][mode, 1]
            kept.append(
                (
                    real_part * turn_real - imag_part * turn_imag,
                    real_part * turn_imag + imag_part * turn_real,
                )
            )
    both_first = complex_product(first[1], first[0])
    both_second = complex_product(second[1], second[0])

    order = pick_matrix(
        LEVELS, lambda row: lax.bitwise_xor(row // width, seat) * width + row % width
    )

    def put_level(ref, index, real_part, imag_part):
        full = blocks(real_part, -imag_part, imag_part, real_part)
        high, low = split_value(full)
        made = blocks(high, high, low, jnp.zeros_like(low))
        if index is None:
            ref[...] = made
        else:
            ref[index] = made

    put_level(turn_ref, None, exact(both_first[0].T, order), exact(-both_first[1].T, order))
    put_level(level_ref, 0, first[1][0].T, first[1][1].T)
    put_level(level_ref, 1, exact(first[0][0], order), exact(-first[0][1], order))
    put_level(level_ref, 2, exact(order, first[0][0].T), exact(order, first[0][1].T))

    def put_lane(index, real_part, imag_part):
        real_part, imag_part = spread(real_part), spread(imag_part)
        high, low = split_value(blocks(real_part, imag_part, -imag_part, real_part))
        lane_ref[index, 0] = high
        lane_ref[index, 1] = low

    put_lane(0, *second[1])
    put_lane(1, second[0][0].T, -second[0][1].T)
    put_lane(2, *second[0])

    real_part, imag_part = spread(both_second[0].T), spread(both_second[1].T)
    full = blocks(real_part, -imag_part, -imag_part, -real_part)

    def source(row):
        chunk, rest = row // (2 * size * parts), row % (2 * size * parts)
        step, rest = rest // (2 * size), rest % (2 * size)
        half, place = rest // size, rest % size
        return half * WIDE + lax.bitwise_xor(step, seat) * share + chunk * size + place

    chosen = exact(pick_matrix(PAIR, source), full)
    high, low = split_value(chosen)
    open_ref[0] = high
    open_ref[1] = low
    high, low = split_value(chosen[:PAIR // chunks].T)
    first_ref[...] = blocks(high, low, high, jnp.zeros_like(low))


def make_weights(phases, displacements, table_slot, checkpoint, seat, parts, chunks):
    def angles(layer):
        return pl.BlockSpec(
            (None, 2, LEVELS), lambda i, slot, start, own: (slot[start[0] + layer], 0, 0)
        )

    def matrices(layer):
        return pl.BlockSpec(
            (None, 2, 2, LEVELS, LEVELS),
            lambda i, slot, start, own: (start[0] + layer, 0, 0, 0, 0),
        )

    def whole(shape):
        return pl.BlockSpec(shape, lambda i, slot, start, own: (0,) * len(shape))

    shapes = [(2 * PAIR, 2 * PAIR // chunks), (2, PAIR, PAIR), (PAIR, PAIR), (3, PAIR, PAIR), (3, 2, PAIR, PAIR)]
    return pl.pallas_call(
        functools.partial(weights_kernel, parts, chunks),
        grid_spec=pltpu.PrefetchScalarGridSpec(
            num_scalar_prefetch=3,
            grid=(1,),
            in_specs=[angles(0), angles(1), matrices(0), matrices(1)],
            out_specs=[whole(shape) for shape in shapes],
        ),
        out_shape=[jax.ShapeDtypeStruct(shape, BF16) for shape in shapes],
        compiler_params=PARAMS,
        cost_estimate=SMALL,
    )(table_slot, checkpoint, seat, phases, phases, displacements, displacements)


def open_kernel(count, waited, weight_ref, field_ref, *refs):
    both = jnp.concatenate([field_ref[0], field_ref[1]], axis=1)
    high, low = split_value(both)
    across = (((1,), (1,)), ((), ()))
    made = mxu(weight_ref[0], high, across) + (
        mxu(weight_ref[0], low, across) + mxu(weight_ref[1], high, across)
    )
    tall = made.shape[0] // count
    for place, out in enumerate(refs[waited:]):
        piece = made[place * tall:(place + 1) * tall]
        for first in range(out.shape[0]):
            out[first] = piece[:, first * WIDE:(first + 1) * WIDE]


def open_first_kernel(size, weight_ref, field_ref, *out_refs):
    levels = field_ref.shape[2] // WIDE
    tall = 2 * size
    for first in range(field_ref.shape[1] // WIDE):
        rows = []
        down = slice(first * WIDE, (first + 1) * WIDE)
        for level in range(levels):
            place = slice(level * WIDE, (level + 1) * WIDE)
            real_high, real_low = split_value(field_ref[0, down, place])
            imag_high, imag_low = split_value(field_ref[1, down, place])
            rows.append(jnp.concatenate([real_high, imag_high, real_low, imag_low], axis=1))
        made = mxu(jnp.concatenate(rows, axis=0), weight_ref[...])
        middle = made.shape[1] // 2
        for level in range(levels):
            turned = made[level * WIDE:(level + 1) * WIDE].T
            turned = turned[:middle] + turned[middle:]
            for step, out in enumerate(out_refs):
                out[first, level * tall:(level + 1) * tall, :] = turned[
                    step * tall:(step + 1) * tall
                ]


def open_first(field, weights, parts, size):
    rows, cols = field.shape[1:]
    firsts = rows // WIDE
    tall = cols // WIDE * 2 * size
    group = min(2, firsts)
    outs = pl.pallas_call(
        functools.partial(open_first_kernel, size),
        grid=(firsts // group,),
        in_specs=[
            pl.BlockSpec(weights.shape, lambda i: (0, 0)),
            pl.BlockSpec((2, group * WIDE, cols), lambda i: (0, i, 0)),
        ],
        out_specs=[pl.BlockSpec((group, tall, WIDE), lambda i: (i, 0, 0))] * parts,
        out_shape=[jax.ShapeDtypeStruct((firsts, tall, WIDE), F32)] * parts,
        compiler_params=PARAMS,
        cost_estimate=SMALL,
    )(weights, field)
    return [outs]


def open_state(field, weights, parts, size, chunk_start, chunk_count, waited):
    rows, cols = field.shape[1:]
    firsts = rows // WIDE
    column_levels = cols // WIDE
    count = parts * chunk_count
    tall = count * 2 * size
    shape = jax.ShapeDtypeStruct((firsts, column_levels * 2 * size, WIDE), F32)
    weights = lax.slice_in_dim(
        weights, chunk_start * parts * 2 * size, chunk_start * parts * 2 * size + tall, axis=1
    )
    outs = pl.pallas_call(
        functools.partial(open_kernel, count, len(waited)),
        grid=(column_levels,),
        in_specs=[
            pl.BlockSpec((2, tall, PAIR), lambda i: (0, 0, 0)),
            pl.BlockSpec((2, rows, WIDE), lambda i: (0, 0, i)),
        ]
        + [pl.BlockSpec(memory_space=pl.ANY)] * len(waited),
        out_specs=[pl.BlockSpec((firsts, 2 * size, WIDE), lambda i: (0, i, 0))] * count,
        out_shape=[shape] * count,
        compiler_params=PARAMS,
        cost_estimate=SMALL,
    )(weights, field, *waited)
    return [outs[c * parts:(c + 1) * parts] for c in range(chunk_count)]


def cut_kernel(size, waited, seat_ref, field_ref, *refs):
    seat = seat_ref[0]
    levels = field_ref.shape[-1] // WIDE
    for first in range(field_ref.shape[1]):
        for step, out in enumerate(refs[waited:]):
            part = lax.bitwise_xor(seat, step)
            for half in range(2):
                for level in range(levels):
                    start = (2 * level + half) * size
                    out[first, start:start + size, :] = field_ref[
                        half, first, part, :, level * WIDE:(level + 1) * WIDE
                    ]


def cut_pieces(field, seat, parts, chunk, size, waited):
    rows, cols = field.shape[1:]
    firsts = rows // WIDE
    group = min(GROUP, firsts)
    chunks = WIDE // parts // size
    tall = cols // WIDE * 2 * size
    return pl.pallas_call(
        functools.partial(cut_kernel, size, len(waited)),
        grid=(firsts // group,),
        in_specs=[
            pl.BlockSpec(memory_space=pltpu.SMEM),
            pl.BlockSpec((2, group, parts, None, size, cols), lambda i: (0, i, 0, chunk, 0, 0)),
        ]
        + [pl.BlockSpec(memory_space=pl.ANY)] * len(waited),
        out_specs=[pl.BlockSpec((group, tall, WIDE), lambda i: (i, 0, 0))] * parts,
        out_shape=[jax.ShapeDtypeStruct((firsts, tall, WIDE), F32)] * parts,
        compiler_params=PARAMS,
        cost_estimate=SMALL,
    )(seat, field.reshape(2, firsts, parts, chunks, size, cols), *waited)


def level_apply(weights, real_part, imag_part):
    real_high, real_low = split_value(real_part)
    imag_high, imag_low = split_value(imag_part)
    stacked = jnp.concatenate([real_high, imag_high, real_low, imag_low], axis=0)
    made = mxu(weights, stacked)
    return made[:WIDE] + made[WIDE:]


def lane_apply(weight_ref, index, real_part, imag_part):
    high, low = split_value(jnp.concatenate([real_part, imag_part], axis=1))
    made = mxu(high, weight_ref[index, 0]) + (
        mxu(low, weight_ref[index, 0]) + mxu(high, weight_ref[index, 1])
    )
    return made[:, :WIDE], made[:, WIDE:]


def gather_levels(refs, size, half):
    columns = []
    for place in range(size):
        parts = [
            ref[pl.ds(half * size + place, ref.shape[0] // (2 * size), stride=2 * size), :]
            for ref in refs
        ]
        columns.append(jnp.concatenate(parts, axis=0) if len(parts) > 1 else parts[0])
    return jnp.concatenate(columns, axis=1)


def scatter_levels(ref, size, half, value, start=0, apart=None):
    for place in range(size):
        rows = pl.ds(start + half * size + place, LEVELS, stride=apart or 2 * size)
        ref[rows, :] = value[:, place * WIDE:(place + 1) * WIDE]


def turn_kernel(parts, size, group, weight_ref, *refs):
    apart = group * 2 * size
    out_ref = refs[-1].reshape(LEVELS * apart, WIDE)
    for first in range(group):
        pieces = [ref.at[first] for ref in refs[:parts]]
        made = level_apply(
            weight_ref[...], gather_levels(pieces, size, 0), gather_levels(pieces, size, 1)
        )
        scatter_levels(out_ref, size, 0, made[:LEVELS], first * 2 * size, apart)
        scatter_levels(out_ref, size, 1, made[LEVELS:], first * 2 * size, apart)


def turn_columns(pieces, weights, size, waited):
    firsts = pieces[0].shape[0]
    group = min(GROUP, firsts)
    parts = len(pieces)
    block = pieces[0].shape[1:]
    return pl.pallas_call(
        functools.partial(turn_kernel, parts, size, group),
        grid=(firsts // group,),
        in_specs=[pl.BlockSpec((PAIR, PAIR), lambda i: (0, 0))]
        + [pl.BlockSpec((group,) + block, lambda i: (i, 0, 0))] * parts
        + [pl.BlockSpec(memory_space=pl.ANY)] * len(waited),
        out_specs=pl.BlockSpec((LEVELS, group, 2 * size, WIDE), lambda i: (0, i, 0, 0)),
        out_shape=jax.ShapeDtypeStruct((LEVELS, firsts, 2 * size, WIDE), F32),
        compiler_params=PARAMS,
        cost_estimate=SMALL,
    )(weights, *pieces, *waited)


def halves(value, size):
    value = value.reshape(LEVELS, 2, size, WIDE)
    rows = LEVELS * size
    return value[:, 0].reshape(rows, WIDE), value[:, 1].reshape(rows, WIDE)


def join(real_part, imag_part, size):
    shape = (LEVELS, 1, size, WIDE)
    both = jnp.concatenate([real_part.reshape(shape), imag_part.reshape(shape)], axis=1)
    return both.reshape(LEVELS * 2 * size, WIDE)


def close_kernel(parts, size, lane_ref, level_ref, field_ref, *refs):
    rho_refs = refs[:parts]
    out_refs = refs[-parts - 3:-3]
    grad_ref, work_a, work_b = refs[-3:]
    step = pl.program_id(0)

    @pl.when(step == 0)
    def _():
        grad_ref[...] = jnp.zeros_like(grad_ref)

    flat = field_ref.reshape(LEVELS * 2 * size, WIDE)
    real_part, imag_part = lane_apply(lane_ref, 0, *halves(flat[...], size))
    work_a[...] = join(real_part, imag_part, size)

    rho = jnp.concatenate([ref[...] for ref in rho_refs], axis=0)
    rho_real, rho_imag = halves(rho, size)
    real_part, imag_part = lane_apply(lane_ref, 1, rho_real, rho_imag)
    work_b[...] = join(real_part, imag_part, size)

    mid = level_apply(level_ref[0], gather_levels([work_a], size, 0), gather_levels([work_a], size, 1))
    seen = level_apply(level_ref[1], gather_levels([work_b], size, 0), gather_levels([work_b], size, 1))
    terms = seen[:LEVELS] * mid[LEVELS:] - seen[LEVELS:] * mid[:LEVELS]
    total = terms[:, :WIDE]
    for place in range(1, size):
        total = total + terms[:, place * WIDE:(place + 1) * WIDE]
    grad_ref[1] += total

    last = level_apply(level_ref[2], mid[:LEVELS], mid[LEVELS:])
    scatter_levels(work_a, size, 0, last[:LEVELS])
    scatter_levels(work_a, size, 1, last[LEVELS:])
    real_part, imag_part = lane_apply(lane_ref, 2, *halves(work_a[...], size))
    terms = rho_real * imag_part - rho_imag * real_part
    grad_ref[0] += jnp.sum(terms.reshape(LEVELS, size, WIDE), axis=1)
    made = join(real_part, imag_part, size)
    rows = made.shape[0] // parts
    for part in range(parts):
        out_refs[part][...] = made[part * rows:(part + 1) * rows]


def close_columns(field, rho_pieces, lane, level, size, waited):
    total_first, firsts = field.shape[:2]
    devs = total_first // firsts
    parts = len(rho_pieces)
    rows = LEVELS * 2 * size
    field = field.reshape(devs, firsts, firsts * 2 * size, WIDE)
    piece = rho_pieces[0]
    piece_spec = pl.BlockSpec((None,) + piece.shape[1:], lambda i: (i, 0, 0))
    outs = pl.pallas_call(
        functools.partial(close_kernel, parts, size),
        grid=(firsts,),
        in_specs=[
            pl.BlockSpec(lane.shape, lambda i: (0, 0, 0, 0)),
            pl.BlockSpec(level.shape, lambda i: (0, 0, 0)),
            pl.BlockSpec((devs, None, firsts * 2 * size, WIDE), lambda i: (0, i, 0, 0)),
        ]
        + [piece_spec] * parts
        + [pl.BlockSpec(memory_space=pl.ANY)] * len(waited),
        out_specs=[piece_spec] * parts + [pl.BlockSpec((2, LEVELS, WIDE), lambda i: (0, 0, 0))],
        out_shape=[jax.ShapeDtypeStruct(piece.shape, F32)] * parts
        + [jax.ShapeDtypeStruct((2, LEVELS, WIDE), F32)],
        scratch_shapes=[pltpu.VMEM((rows, WIDE), F32), pltpu.VMEM((rows, WIDE), F32)],
        compiler_params=PARAMS,
        cost_estimate=LARGE,
    )(lane, level, field, *rho_pieces, *waited)
    return list(outs[:parts]), outs[parts]


def place_kernel(parts, size, seat_ref, *refs):
    pieces = refs[:parts]
    out_ref = refs[-1]
    seat = seat_ref[0]
    levels = out_ref.shape[-1] // WIDE
    for first in range(out_ref.shape[1]):
        for step in range(parts):
            part = lax.bitwise_xor(seat, step)
            for half in range(2):
                for level in range(levels):
                    start = (2 * level + half) * size
                    out_ref[half, first, part, :, level * WIDE:(level + 1) * WIDE] = pieces[step][
                        first, start:start + size, :
                    ]


def place_pieces(pieces, seat, held, chunk, shape, size, waited):
    parts = len(pieces)
    group = min(GROUP, shape[1])
    cols = shape[-1]
    return pl.pallas_call(
        functools.partial(place_kernel, parts, size),
        grid=(shape[1] // group,),
        in_specs=[pl.BlockSpec(memory_space=pltpu.SMEM)]
        + [pl.BlockSpec((group,) + pieces[0].shape[1:], lambda i: (i, 0, 0))] * parts
        + [pl.BlockSpec(memory_space=pl.ANY)],
        out_specs=pl.BlockSpec(
            (2, group, parts, None, size, cols), lambda i: (0, i, 0, chunk, 0, 0)
        ),
        out_shape=jax.ShapeDtypeStruct(shape, F32),
        input_output_aliases={} if held is None else {parts + 1: 0},
        compiler_params=PARAMS,
        cost_estimate=SMALL,
    )(seat, *pieces, waited if held is None else held)


def swap(pieces, parts):
    moved = [pieces[0]]
    for step in range(1, parts):
        pairs = [(member, member ^ step) for member in range(parts)]
        moved.append(lax.ppermute(pieces[step], "grp", pairs))
    return moved


def grad_kernel(parts, count, seat_ref, *refs):
    out_ref = refs[-1]
    grad = refs[0][...]
    for ref in refs[1:count]:
        grad = grad + ref[...]
    grad = -2.0 * grad
    width = LEVELS // parts
    order = pick_matrix(
        LEVELS, lambda row: lax.bitwise_xor(row // width, seat_ref[0]) * width + row % width
    )
    fold = (grid_of((WIDE, LEVELS), 0) // TRANSMON == grid_of((WIDE, LEVELS), 1)).astype(F32)
    for layer in range(2):
        firsts = exact(jnp.ones((8, WIDE), F32), grad[layer], (((1,), (1,)), ((), ())))
        if layer == 0:
            firsts = exact(firsts, order)
        seconds = exact(exact(jnp.ones((8, LEVELS), F32), grad[layer]), fold)
        out_ref[2 * layer:2 * layer + 1, :] = firsts[:1]
        out_ref[2 * layer + 1:2 * layer + 2, :] = seconds[:1]


def device_grad(grads, seat, parts, waited):
    return pl.pallas_call(
        functools.partial(grad_kernel, parts, len(grads)),
        in_specs=[pl.BlockSpec(memory_space=pltpu.SMEM)]
        + [pl.BlockSpec(memory_space=pltpu.VMEM)] * len(grads)
        + [pl.BlockSpec(memory_space=pl.ANY)] * len(waited),
        out_specs=pl.BlockSpec(memory_space=pltpu.VMEM),
        out_shape=jax.ShapeDtypeStruct((4, LEVELS), F32),
        compiler_params=PARAMS,
        cost_estimate=SMALL,
    )(seat, *grads, *waited)


def total_rounds():
    rounds = []
    for axis in ("grp", "dev"):
        count = lax.axis_size(axis)
        rounds.append([(axis, 1 << bit, count) for bit in range(count.bit_length() - 1)])
    return rounds[0][:1] + rounds[1] + rounds[0][1:]


def add_rounds(value, rounds):
    for axis, step, count in rounds:
        pairs = [(member, member ^ step) for member in range(count)]
        value = value + lax.ppermute(value, axis, pairs)
    return value


def per_device(density, costate, phases, displacements, table_slot, checkpoint):
    parts = lax.axis_size("grp")
    share = WIDE // parts
    chunks = max(1, min(4, share // 8))
    size = share // chunks
    seat = lax.axis_index("grp").astype(jnp.int32)
    seats = seat.reshape(1)
    rows, cols = costate.shape[1:]

    opened_first, opened, turned_by, level, lane = make_weights(
        phases, displacements, table_slot, checkpoint, seats, parts, chunks
    )
    state_cut = open_first(costate, opened_first, parts, size)
    if chunks > 1:
        state_cut += open_state(
            costate, opened, parts, size, 1, chunks - 1, list(state_cut[0][:1])
        )
    rho = [
        cut_pieces(density, seats, parts, chunk, size, list(state_cut[-1][:1]) if chunk else [])
        for chunk in range(chunks)
    ]
    rho_there = [swap(pieces, parts) for pieces in (rho[:2] if chunks > 3 else rho)]
    ahead = parts // 2
    state_cut[0], rho_there[0][ahead] = lax.optimization_barrier(
        (state_cut[0], rho_there[0][ahead])
    )
    state = [swap(pieces, parts) for pieces in state_cut[:3]]

    shape = (2, rows // WIDE, parts, chunks, size, cols)
    fields, closed, made, grads, totals = [], [], [], [], []

    def close(chunk, waited):
        if chunk > 0:
            waited = waited + closed[chunk - 1][:1]
        out, grad = close_columns(
            fields[chunk], rho_there[chunk], lane, level, size, waited
        )
        closed.append(out)
        if chunk == chunks - 2 and chunk > 0:
            out, rho_there[-1] = lax.optimization_barrier((out, rho_there[-1]))
        grads.append(grad)
        if chunk == chunks - 1:
            total = add_rounds(device_grad(grads, seats, parts, []), total_rounds()[:-1])
            out, made[-1:], total = lax.optimization_barrier((out, made[-1:], total))
            totals.append(total)
        if chunk > 0 or chunks < 4:
            made.append(swap(out, parts))

    for chunk in range(chunks):
        waited = [rho[chunk][0]]
        if chunk == 0:
            waited += [pieces[0] for pieces in state_cut[1:2]]
        if chunk > 0:
            waited.append(field)
        if chunk > 1:
            close(chunk - 2, [])
            waited += closed[chunk - 2][:1]
        field = turn_columns(state[chunk], turned_by, size, waited)
        if chunk + 1 == len(state) < chunks:
            pieces, field = lax.optimization_barrier((state_cut[chunk + 1], field))
            state.append(swap(pieces, parts))
            pieces, state[-1] = lax.optimization_barrier((rho[2], state[-1]))
            rho_there += [swap(pieces, parts), swap(rho[3], parts)]
            out, rho_there[2] = lax.optimization_barrier((closed[0], rho_there[2]))
            made.append(swap(out, parts))
        fields.append(lax.all_to_all(field, "dev", split_axis=0, concat_axis=0, tiled=True))
    whole = None
    for chunk in range(chunks):
        while len(made) < min(max(chunk + 2, chunks - 1), chunks):
            close(len(made), [whole] if 0 < chunk == chunks - 2 else [])
        whole = place_pieces(made[chunk], seats, whole, chunk, shape, size, closed[-1][0])
    grad = add_rounds(totals[0], total_rounds()[-1:])
    return whole.reshape(costate.shape), grad.reshape(2, 2, LEVELS)


def solution(mesh):
    return jax.shard_map(
        per_device,
        mesh=mesh,
        in_specs=(P(None, "dev", "grp"), P(None, "dev", "grp"), P(), P(), P(), P()),
        out_specs=(P(None, "dev", "grp"), P()),
        check_vma=False,
    )
```

```python
import functools

import jax
import jax.numpy as jnp
from jax import lax
from jax.experimental import pallas as pl
from jax.experimental.pallas import tpu as pltpu
from jax.sharding import PartitionSpec as P

LEVELS = 64
TRANSMON = 2
GROUP = 4
WIDE = LEVELS * TRANSMON
PAIR = 2 * WIDE
HIGH = lax.Precision.HIGHEST
F32 = jnp.float32
BF16 = jnp.bfloat16
SMALL = pl.CostEstimate(flops=1024, bytes_accessed=1024, transcendentals=0)
LARGE = pl.CostEstimate(flops=2 * 10**11, bytes_accessed=1024, transcendentals=0)
PARAMS = pltpu.CompilerParams(vmem_limit_bytes=60 * 1024 * 1024)


def split_value(value):
    high = value.astype(BF16)
    low = (value - high.astype(F32)).astype(BF16)
    return high, low


def mxu(left, right, dims=(((1,), (0,)), ((), ()))):
    return lax.dot_general(left, right, dims, preferred_element_type=F32)


def exact(left, right, dims=(((1,), (0,)), ((), ()))):
    return lax.dot_general(left, right, dims, precision=HIGH, preferred_element_type=F32)


def grid_of(shape, dim):
    return lax.broadcasted_iota(jnp.int32, shape, dim)


def pick_matrix(count, chosen):
    shape = (count, count)
    return (chosen(grid_of(shape, 0)) == grid_of(shape, 1)).astype(F32)


def spread(matrix):
    tall = (grid_of((WIDE, LEVELS), 0) // TRANSMON == grid_of((WIDE, LEVELS), 1)).astype(F32)
    long = (grid_of((LEVELS, WIDE), 1) // TRANSMON == grid_of((LEVELS, WIDE), 0)).astype(F32)
    same = grid_of((WIDE, WIDE), 0) % TRANSMON == grid_of((WIDE, WIDE), 1) % TRANSMON
    return jnp.where(same, exact(exact(tall, matrix), long), 0.0)


def blocks(upper_left, upper_right, lower_left, lower_right):
    return jnp.concatenate(
        [
            jnp.concatenate([upper_left, upper_right], axis=1),
            jnp.concatenate([lower_left, lower_right], axis=1),
        ],
        axis=0,
    )


def complex_product(left, right):
    return (
        exact(left[0], right[0]) - exact(left[1], right[1]),
        exact(left[0], right[1]) + exact(left[1], right[0]),
    )


def weights_kernel(parts, chunks, slot_ref, start_ref, seat_ref, *refs):
    angle_refs, matrix_refs = refs[0:2], refs[2:4]
    first_ref, open_ref, turn_ref, level_ref, lane_ref = refs[-5:]
    seat = seat_ref[0]
    width = LEVELS // parts
    share = WIDE // parts
    size = share // chunks
    first, second = [], []
    for layer in range(2):
        cosine = jnp.cos(angle_refs[layer][...])
        sine = jnp.sin(angle_refs[layer][...])
        for mode, kept in enumerate((first, second)):
            turn_real, turn_imag = cosine[mode:mode + 1], sine[mode:mode + 1]
            real_part = matrix_refs[layer][mode, 0]
            imag_part = matrix_refs[layer][mode, 1]
            kept.append(
                (
                    real_part * turn_real - imag_part * turn_imag,
                    real_part * turn_imag + imag_part * turn_real,
                )
            )
    both_first = complex_product(first[1], first[0])
    both_second = complex_product(second[1], second[0])

    order = pick_matrix(
        LEVELS, lambda row: lax.bitwise_xor(row // width, seat) * width + row % width
    )

    def put_level(ref, index, real_part, imag_part):
        full = blocks(real_part, -imag_part, imag_part, real_part)
        high, low = split_value(full)
        made = blocks(high, high, low, jnp.zeros_like(low))
        if index is None:
            ref[...] = made
        else:
            ref[index] = made

    put_level(turn_ref, None, exact(both_first[0].T, order), exact(-both_first[1].T, order))
    put_level(level_ref, 0, first[1][0].T, first[1][1].T)
    put_level(level_ref, 1, exact(first[0][0], order), exact(-first[0][1], order))
    put_level(level_ref, 2, exact(order, first[0][0].T), exact(order, first[0][1].T))

    def put_lane(index, real_part, imag_part):
        real_part, imag_part = spread(real_part), spread(imag_part)
        high, low = split_value(blocks(real_part, imag_part, -imag_part, real_part))
        lane_ref[index, 0] = high
        lane_ref[index, 1] = low

    put_lane(0, *second[1])
    put_lane(1, second[0][0].T, -second[0][1].T)
    put_lane(2, *second[0])

    real_part, imag_part = spread(both_second[0].T), spread(both_second[1].T)
    full = blocks(real_part, -imag_part, -imag_part, -real_part)

    def source(row):
        chunk, rest = row // (2 * size * parts), row % (2 * size * parts)
        step, rest = rest // (2 * size), rest % (2 * size)
        half, place = rest // size, rest % size
        return half * WIDE + lax.bitwise_xor(step, seat) * share + chunk * size + place

    chosen = exact(pick_matrix(PAIR, source), full)
    high, low = split_value(chosen)
    open_ref[0] = high
    open_ref[1] = low
    high, low = split_value(chosen[:PAIR // chunks].T)
    first_ref[...] = blocks(high, low, high, jnp.zeros_like(low))


def make_weights(phases, displacements, table_slot, checkpoint, seat, parts, chunks):
    def angles(layer):
        return pl.BlockSpec(
            (None, 2, LEVELS), lambda i, slot, start, own: (slot[start[0] + layer], 0, 0)
        )

    def matrices(layer):
        return pl.BlockSpec(
            (None, 2, 2, LEVELS, LEVELS),
            lambda i, slot, start, own: (start[0] + layer, 0, 0, 0, 0),
        )

    def whole(shape):
        return pl.BlockSpec(shape, lambda i, slot, start, own: (0,) * len(shape))

    shapes = [(2 * PAIR, 2 * PAIR // chunks), (2, PAIR, PAIR), (PAIR, PAIR), (3, PAIR, PAIR), (3, 2, PAIR, PAIR)]
    return pl.pallas_call(
        functools.partial(weights_kernel, parts, chunks),
        grid_spec=pltpu.PrefetchScalarGridSpec(
            num_scalar_prefetch=3,
            grid=(1,),
            in_specs=[angles(0), angles(1), matrices(0), matrices(1)],
            out_specs=[whole(shape) for shape in shapes],
        ),
        out_shape=[jax.ShapeDtypeStruct(shape, BF16) for shape in shapes],
        compiler_params=PARAMS,
        cost_estimate=SMALL,
    )(table_slot, checkpoint, seat, phases, phases, displacements, displacements)


def open_kernel(count, waited, weight_ref, field_ref, *refs):
    both = jnp.concatenate([field_ref[0], field_ref[1]], axis=1)
    high, low = split_value(both)
    across = (((1,), (1,)), ((), ()))
    made = mxu(weight_ref[0], high, across) + (
        mxu(weight_ref[0], low, across) + mxu(weight_ref[1], high, across)
    )
    tall = made.shape[0] // count
    for place, out in enumerate(refs[waited:]):
        piece = made[place * tall:(place + 1) * tall]
        for first in range(out.shape[0]):
            out[first] = piece[:, first * WIDE:(first + 1) * WIDE]


def open_first_kernel(size, weight_ref, field_ref, *out_refs):
    levels = field_ref.shape[2] // WIDE
    tall = 2 * size
    for first in range(field_ref.shape[1] // WIDE):
        rows = []
        down = slice(first * WIDE, (first + 1) * WIDE)
        for level in range(levels):
            place = slice(level * WIDE, (level + 1) * WIDE)
            real_high, real_low = split_value(field_ref[0, down, place])
            imag_high, imag_low = split_value(field_ref[1, down, place])
            rows.append(jnp.concatenate([real_high, imag_high, real_low, imag_low], axis=1))
        made = mxu(jnp.concatenate(rows, axis=0), weight_ref[...])
        middle = made.shape[1] // 2
        for level in range(levels):
            turned = made[level * WIDE:(level + 1) * WIDE].T
            turned = turned[:middle] + turned[middle:]
            for step, out in enumerate(out_refs):
                out[first, level * tall:(level + 1) * tall, :] = turned[
                    step * tall:(step + 1) * tall
                ]


def open_first(field, weights, parts, size):
    rows, cols = field.shape[1:]
    firsts = rows // WIDE
    tall = cols // WIDE * 2 * size
    group = min(2, firsts)
    outs = pl.pallas_call(
        functools.partial(open_first_kernel, size),
        grid=(firsts // group,),
        in_specs=[
            pl.BlockSpec(weights.shape, lambda i: (0, 0)),
            pl.BlockSpec((2, group * WIDE, cols), lambda i: (0, i, 0)),
        ],
        out_specs=[pl.BlockSpec((group, tall, WIDE), lambda i: (i, 0, 0))] * parts,
        out_shape=[jax.ShapeDtypeStruct((firsts, tall, WIDE), F32)] * parts,
        compiler_params=PARAMS,
        cost_estimate=SMALL,
    )(weights, field)
    return [outs]


def open_state(field, weights, parts, size, chunk_start, chunk_count, waited):
    rows, cols = field.shape[1:]
    firsts = rows // WIDE
    column_levels = cols // WIDE
    count = parts * chunk_count
    tall = count * 2 * size
    shape = jax.ShapeDtypeStruct((firsts, column_levels * 2 * size, WIDE), F32)
    weights = lax.slice_in_dim(
        weights, chunk_start * parts * 2 * size, chunk_start * parts * 2 * size + tall, axis=1
    )
    outs = pl.pallas_call(
        functools.partial(open_kernel, count, len(waited)),
        grid=(column_levels,),
        in_specs=[
            pl.BlockSpec((2, tall, PAIR), lambda i: (0, 0, 0)),
            pl.BlockSpec((2, rows, WIDE), lambda i: (0, 0, i)),
        ]
        + [pl.BlockSpec(memory_space=pl.ANY)] * len(waited),
        out_specs=[pl.BlockSpec((firsts, 2 * size, WIDE), lambda i: (0, i, 0))] * count,
        out_shape=[shape] * count,
        compiler_params=PARAMS,
        cost_estimate=SMALL,
    )(weights, field, *waited)
    return [outs[c * parts:(c + 1) * parts] for c in range(chunk_count)]


def cut_kernel(size, waited, seat_ref, field_ref, *refs):
    seat = seat_ref[0]
    levels = field_ref.shape[-1] // WIDE
    for first in range(field_ref.shape[1]):
        for step, out in enumerate(refs[waited:]):
            part = lax.bitwise_xor(seat, step)
            for half in range(2):
                for level in range(levels):
                    start = (2 * level + half) * size
                    out[first, start:start + size, :] = field_ref[
                        half, first, part, :, level * WIDE:(level + 1) * WIDE
                    ]


def cut_pieces(field, seat, parts, chunk, size, waited):
    rows, cols = field.shape[1:]
    firsts = rows // WIDE
    group = min(GROUP, firsts)
    chunks = WIDE // parts // size
    tall = cols // WIDE * 2 * size
    return pl.pallas_call(
        functools.partial(cut_kernel, size, len(waited)),
        grid=(firsts // group,),
        in_specs=[
            pl.BlockSpec(memory_space=pltpu.SMEM),
            pl.BlockSpec((2, group, parts, None, size, cols), lambda i: (0, i, 0, chunk, 0, 0)),
        ]
        + [pl.BlockSpec(memory_space=pl.ANY)] * len(waited),
        out_specs=[pl.BlockSpec((group, tall, WIDE), lambda i: (i, 0, 0))] * parts,
        out_shape=[jax.ShapeDtypeStruct((firsts, tall, WIDE), F32)] * parts,
        compiler_params=PARAMS,
        cost_estimate=SMALL,
    )(seat, field.reshape(2, firsts, parts, chunks, size, cols), *waited)


def level_apply(weights, real_part, imag_part):
    real_high, real_low = split_value(real_part)
    imag_high, imag_low = split_value(imag_part)
    stacked = jnp.concatenate([real_high, imag_high, real_low, imag_low], axis=0)
    made = mxu(weights, stacked)
    return made[:WIDE] + made[WIDE:]


def lane_apply(weight_ref, index, real_part, imag_part):
    high, low = split_value(jnp.concatenate([real_part, imag_part], axis=1))
    made = mxu(high, weight_ref[index, 0]) + (
        mxu(low, weight_ref[index, 0]) + mxu(high, weight_ref[index, 1])
    )
    return made[:, :WIDE], made[:, WIDE:]


def gather_levels(refs, size, half):
    columns = []
    for place in range(size):
        parts = [
            ref[pl.ds(half * size + place, ref.shape[0] // (2 * size), stride=2 * size), :]
            for ref in refs
        ]
        columns.append(jnp.concatenate(parts, axis=0) if len(parts) > 1 else parts[0])
    return jnp.concatenate(columns, axis=1)


def scatter_levels(ref, size, half, value, start=0, apart=None):
    for place in range(size):
        rows = pl.ds(start + half * size + place, LEVELS, stride=apart or 2 * size)
        ref[rows, :] = value[:, place * WIDE:(place + 1) * WIDE]


def turn_kernel(parts, size, group, weight_ref, *refs):
    apart = group * 2 * size
    out_ref = refs[-1].reshape(LEVELS * apart, WIDE)
    for first in range(group):
        pieces = [ref.at[first] for ref in refs[:parts]]
        made = level_apply(
            weight_ref[...], gather_levels(pieces, size, 0), gather_levels(pieces, size, 1)
        )
        scatter_levels(out_ref, size, 0, made[:LEVELS], first * 2 * size, apart)
        scatter_levels(out_ref, size, 1, made[LEVELS:], first * 2 * size, apart)


def turn_columns(pieces, weights, size, waited):
    firsts = pieces[0].shape[0]
    group = min(GROUP, firsts)
    parts = len(pieces)
    block = pieces[0].shape[1:]
    return pl.pallas_call(
        functools.partial(turn_kernel, parts, size, group),
        grid=(firsts // group,),
        in_specs=[pl.BlockSpec((PAIR, PAIR), lambda i: (0, 0))]
        + [pl.BlockSpec((group,) + block, lambda i: (i, 0, 0))] * parts
        + [pl.BlockSpec(memory_space=pl.ANY)] * len(waited),
        out_specs=pl.BlockSpec((LEVELS, group, 2 * size, WIDE), lambda i: (0, i, 0, 0)),
        out_shape=jax.ShapeDtypeStruct((LEVELS, firsts, 2 * size, WIDE), F32),
        compiler_params=PARAMS,
        cost_estimate=SMALL,
    )(weights, *pieces, *waited)


def halves(value, size):
    value = value.reshape(LEVELS, 2, size, WIDE)
    rows = LEVELS * size
    return value[:, 0].reshape(rows, WIDE), value[:, 1].reshape(rows, WIDE)


def join(real_part, imag_part, size):
    shape = (LEVELS, 1, size, WIDE)
    both = jnp.concatenate([real_part.reshape(shape), imag_part.reshape(shape)], axis=1)
    return both.reshape(LEVELS * 2 * size, WIDE)


def close_kernel(parts, size, lane_ref, level_ref, field_ref, *refs):
    rho_refs = refs[:parts]
    out_refs = refs[-parts - 3:-3]
    grad_ref, work_a, work_b = refs[-3:]
    step = pl.program_id(0)

    @pl.when(step == 0)
    def _():
        grad_ref[...] = jnp.zeros_like(grad_ref)

    flat = field_ref.reshape(LEVELS * 2 * size, WIDE)
    real_part, imag_part = lane_apply(lane_ref, 0, *halves(flat[...], size))
    work_a[...] = join(real_part, imag_part, size)

    rho = jnp.concatenate([ref[...] for ref in rho_refs], axis=0)
    rho_real, rho_imag = halves(rho, size)
    real_part, imag_part = lane_apply(lane_ref, 1, rho_real, rho_imag)
    work_b[...] = join(real_part, imag_part, size)

    mid = level_apply(level_ref[0], gather_levels([work_a], size, 0), gather_levels([work_a], size, 1))
    seen = level_apply(level_ref[1], gather_levels([work_b], size, 0), gather_levels([work_b], size, 1))
    terms = seen[:LEVELS] * mid[LEVELS:] - seen[LEVELS:] * mid[:LEVELS]
    total = terms[:, :WIDE]
    for place in range(1, size):
        total = total + terms[:, place * WIDE:(place + 1) * WIDE]
    grad_ref[1] += total

    last = level_apply(level_ref[2], mid[:LEVELS], mid[LEVELS:])
    scatter_levels(work_a, size, 0, last[:LEVELS])
    scatter_levels(work_a, size, 1, last[LEVELS:])
    real_part, imag_part = lane_apply(lane_ref, 2, *halves(work_a[...], size))
    terms = rho_real * imag_part - rho_imag * real_part
    grad_ref[0] += jnp.sum(terms.reshape(LEVELS, size, WIDE), axis=1)
    made = join(real_part, imag_part, size)
    rows = made.shape[0] // parts
    for part in range(parts):
        out_refs[part][...] = made[part * rows:(part + 1) * rows]


def close_columns(field, rho_pieces, lane, level, size, waited):
    total_first, firsts = field.shape[:2]
    devs = total_first // firsts
    parts = len(rho_pieces)
    rows = LEVELS * 2 * size
    field = field.reshape(devs, firsts, firsts * 2 * size, WIDE)
    piece = rho_pieces[0]
    piece_spec = pl.BlockSpec((None,) + piece.shape[1:], lambda i: (i, 0, 0))
    outs = pl.pallas_call(
        functools.partial(close_kernel, parts, size),
        grid=(firsts,),
        in_specs=[
            pl.BlockSpec(lane.shape, lambda i: (0, 0, 0, 0)),
            pl.BlockSpec(level.shape, lambda i: (0, 0, 0)),
            pl.BlockSpec((devs, None, firsts * 2 * size, WIDE), lambda i: (0, i, 0, 0)),
        ]
        + [piece_spec] * parts
        + [pl.BlockSpec(memory_space=pl.ANY)] * len(waited),
        out_specs=[piece_spec] * parts + [pl.BlockSpec((2, LEVELS, WIDE), lambda i: (0, 0, 0))],
        out_shape=[jax.ShapeDtypeStruct(piece.shape, F32)] * parts
        + [jax.ShapeDtypeStruct((2, LEVELS, WIDE), F32)],
        scratch_shapes=[pltpu.VMEM((rows, WIDE), F32), pltpu.VMEM((rows, WIDE), F32)],
        compiler_params=PARAMS,
        cost_estimate=LARGE,
    )(lane, level, field, *rho_pieces, *waited)
    return list(outs[:parts]), outs[parts]


def place_kernel(parts, size, seat_ref, *refs):
    pieces = refs[:parts]
    out_ref = refs[-1]
    seat = seat_ref[0]
    levels = out_ref.shape[-1] // WIDE
    for first in range(out_ref.shape[1]):
        for step in range(parts):
            part = lax.bitwise_xor(seat, step)
            for half in range(2):
                for level in range(levels):
                    start = (2 * level + half) * size
                    out_ref[half, first, part, :, level * WIDE:(level + 1) * WIDE] = pieces[step][
                        first, start:start + size, :
                    ]


def place_pieces(pieces, seat, held, chunk, shape, size, waited):
    parts = len(pieces)
    group = min(GROUP, shape[1])
    cols = shape[-1]
    return pl.pallas_call(
        functools.partial(place_kernel, parts, size),
        grid=(shape[1] // group,),
        in_specs=[pl.BlockSpec(memory_space=pltpu.SMEM)]
        + [pl.BlockSpec((group,) + pieces[0].shape[1:], lambda i: (i, 0, 0))] * parts
        + [pl.BlockSpec(memory_space=pl.ANY)],
        out_specs=pl.BlockSpec(
            (2, group, parts, None, size, cols), lambda i: (0, i, 0, chunk, 0, 0)
        ),
        out_shape=jax.ShapeDtypeStruct(shape, F32),
        input_output_aliases={} if held is None else {parts + 1: 0},
        compiler_params=PARAMS,
        cost_estimate=SMALL,
    )(seat, *pieces, waited if held is None else held)


def swap(pieces, parts):
    moved = [pieces[0]]
    for step in range(1, parts):
        pairs = [(member, member ^ step) for member in range(parts)]
        moved.append(lax.ppermute(pieces[step], "grp", pairs))
    return moved


def grad_kernel(parts, count, seat_ref, *refs):
    out_ref = refs[-1]
    grad = refs[0][...]
    for ref in refs[1:count]:
        grad = grad + ref[...]
    grad = -2.0 * grad
    width = LEVELS // parts
    order = pick_matrix(
        LEVELS, lambda row: lax.bitwise_xor(row // width, seat_ref[0]) * width + row % width
    )
    fold = (grid_of((WIDE, LEVELS), 0) // TRANSMON == grid_of((WIDE, LEVELS), 1)).astype(F32)
    for layer in range(2):
        firsts = exact(jnp.ones((8, WIDE), F32), grad[layer], (((1,), (1,)), ((), ())))
        if layer == 0:
            firsts = exact(firsts, order)
        seconds = exact(exact(jnp.ones((8, LEVELS), F32), grad[layer]), fold)
        out_ref[2 * layer:2 * layer + 1, :] = firsts[:1]
        out_ref[2 * layer + 1:2 * layer + 2, :] = seconds[:1]


def device_grad(grads, seat, parts, waited):
    return pl.pallas_call(
        functools.partial(grad_kernel, parts, len(grads)),
        in_specs=[pl.BlockSpec(memory_space=pltpu.SMEM)]
        + [pl.BlockSpec(memory_space=pltpu.VMEM)] * len(grads)
        + [pl.BlockSpec(memory_space=pl.ANY)] * len(waited),
        out_specs=pl.BlockSpec(memory_space=pltpu.VMEM),
        out_shape=jax.ShapeDtypeStruct((4, LEVELS), F32),
        compiler_params=PARAMS,
        cost_estimate=SMALL,
    )(seat, *grads, *waited)


def total_rounds():
    rounds = []
    for axis in ("grp", "dev"):
        count = lax.axis_size(axis)
        rounds.append([(axis, 1 << bit, count) for bit in range(count.bit_length() - 1)])
    return rounds[0][:1] + rounds[1] + rounds[0][1:]


def add_rounds(value, rounds):
    for axis, step, count in rounds:
        pairs = [(member, member ^ step) for member in range(count)]
        value = value + lax.ppermute(value, axis, pairs)
    return value


def per_device(density, costate, phases, displacements, table_slot, checkpoint):
    parts = lax.axis_size("grp")
    share = WIDE // parts
    chunks = max(1, min(4, share // 8))
    size = share // chunks
    seat = lax.axis_index("grp").astype(jnp.int32)
    seats = seat.reshape(1)
    rows, cols = costate.shape[1:]

    opened_first, opened, turned_by, level, lane = make_weights(
        phases, displacements, table_slot, checkpoint, seats, parts, chunks
    )
    state_cut = open_first(costate, opened_first, parts, size)
    if chunks > 1:
        state_cut += open_state(
            costate, opened, parts, size, 1, chunks - 1, list(state_cut[0][:1])
        )
    rho = [
        cut_pieces(density, seats, parts, chunk, size, list(state_cut[-1][:1]) if chunk else [])
        for chunk in range(chunks)
    ]
    rho_there = [swap(pieces, parts) for pieces in rho]
    ahead = parts // 2
    state_cut[0], rho_there[0][ahead] = lax.optimization_barrier(
        (state_cut[0], rho_there[0][ahead])
    )
    state = [swap(pieces, parts) for pieces in state_cut[:3]]

    shape = (2, rows // WIDE, parts, chunks, size, cols)
    fields, closed, made, grads, totals = [], [], [], [], []

    def close(chunk, waited):
        if chunk > 0:
            waited = waited + closed[chunk - 1][:1]
        out, grad = close_columns(
            fields[chunk], rho_there[chunk], lane, level, size, waited
        )
        closed.append(out)
        if chunk == chunks - 2 and chunk > 0:
            out, rho_there[-1] = lax.optimization_barrier((out, rho_there[-1]))
        grads.append(grad)
        if chunk == chunks - 1:
            total = add_rounds(device_grad(grads, seats, parts, []), total_rounds())
            out, made[-1:], total = lax.optimization_barrier((out, made[-1:], total))
            totals.append(total)
        if chunk > 0 or chunks < 4:
            made.append(swap(out, parts))

    for chunk in range(chunks):
        waited = [rho[chunk][0]]
        if chunk == 0:
            waited += [pieces[0] for pieces in state_cut[1:2]]
        if chunk > 0:
            waited.append(field)
        if chunk > 1:
            close(chunk - 2, [])
            waited += closed[chunk - 2][:1]
        field = turn_columns(state[chunk], turned_by, size, waited)
        if chunk + 1 == len(state) < chunks:
            pieces, field = lax.optimization_barrier((state_cut[chunk + 1], field))
            state.append(swap(pieces, parts))
            out, rho_there[2] = lax.optimization_barrier((closed[0], rho_there[2]))
            made.append(swap(out, parts))
        fields.append(lax.all_to_all(field, "dev", split_axis=0, concat_axis=0, tiled=True))
    whole = None
    for chunk in range(chunks):
        while len(made) < min(max(chunk + 2, chunks - 1), chunks):
            close(len(made), [whole] if 0 < chunk == chunks - 2 else [])
        whole = place_pieces(made[chunk], seats, whole, chunk, shape, size, closed[-1][0])
    return whole.reshape(costate.shape), totals[0].reshape(2, 2, LEVELS)


def solution(mesh):
    return jax.shard_map(
        per_device,
        mesh=mesh,
        in_specs=(P(None, "dev", "grp"), P(None, "dev", "grp"), P(), P(), P(), P()),
        out_specs=(P(None, "dev", "grp"), P()),
        check_vma=False,
    )
```
